128 devices in a mesh: slab: 4 (over x_hi, core), sx: 4 (over z), syz: 8 (over x_lo, y).
Axes of the slice: x: 4 (x_hi: 2, x_lo: 2; x = x_hi * 2 + x_lo), y: 4, z: 4, core: 2. Of those that a mesh axis runs over, the one named last changes fastest.
Arguments:
- gauge_links: float32 [4, 2, 3, 3, 8, 12, 1024], P(None, None, None, None, 'slab', 'sx', 'syz'), may hold values from -1 to 1, as said below
- langevin_noise: bfloat16 [2, 4, 8, 8, 12, 1024], P(None, None, None, 'slab', 'sx', 'syz'), may hold values from -4 to 4
- separations: int32 [4], replicated, may hold values from 1 to 3, as said below
Outputs:
- correlator: float32 [4, 12, 1024], P('slab', 'sx', 'syz')
The draws below stay inside these ranges and needn't reach their ends.
Inputs may be any that keep to these rules, and one draw needn't show every extreme that they name: Each 3x3 complex matrix of real part gauge_links[mu, 0] and imaginary part gauge_links[mu, 1] is unitary. `separations`: separations from 1 to 3 sites; at least one equals 3.
All inputs are finite; a program needn't handle non-finite values.
Results may differ from the reference program's by a relative error of at most 0.0003.
Values sent between devices are 32-bit elements; how exact they have to be, the bound alone decides.
A program may use at most 64 MiB of HBM per device.

```python
from functools import partial
import jax
import jax.numpy as jnp
from jax import lax

SLAB_TIMES = 2
CX = 3
SITES_ALONG_Z = 32
SWEEPS = 2
NT = 8
SITES_ALONG_X = 12
SITES_ALONG_Y = 32
NYZ = 1024
NR = 4
N_SLAB = 4


root_third = 0.5773502691896258


def complex_times_drawn(first, second):
    return (first[0] * second[0] - first[1] * second[1], first[0] * second[1] + first[1] * second[0])


def draw_gauge_links(key, part):
    key = jax.random.fold_in(key, 5)
    coeff_shape = (8, 4, NT, SITES_ALONG_X, SITES_ALONG_Y * SITES_ALONG_Z)
    coeffs = 2.0 * jax.random.normal(key, coeff_shape, jnp.float32)
    zero_part = jnp.zeros_like(coeffs[0])
    diag_first = coeffs[2] + root_third * coeffs[7]
    diag_second = -coeffs[2] + root_third * coeffs[7]
    diag_third = -2.0 * root_third * coeffs[7]
    herm_real = [[diag_first, coeffs[0], coeffs[3]], [coeffs[0], diag_second, coeffs[5]], [coeffs[3], coeffs[5], diag_third]]
    herm_imag = [[zero_part, -coeffs[1], -coeffs[4]], [coeffs[1], zero_part, -coeffs[6]], [coeffs[4], coeffs[6], zero_part]]

    def element(row_index, col_index):
        row_index = row_index % 3
        col_index = col_index % 3
        delta_value = 1.0 if row_index == col_index else 0.0
        return (delta_value + 0.25 * herm_imag[row_index][col_index], -0.25 * herm_real[row_index][col_index])
    cofactor = []
    for row_index in range(3):
        cof_row = []
        for col_index in range(3):
            forward = complex_times_drawn(element(row_index + 1, col_index + 1), element(row_index + 2, col_index + 2))
            backward = complex_times_drawn(element(row_index + 1, col_index + 2), element(row_index + 2, col_index + 1))
            cof_row.append((forward[0] - backward[0], forward[1] - backward[1]))
        cofactor.append(cof_row)
    det_real = 0.0
    det_imag = 0.0
    for col_index in range(3):
        det_term = complex_times_drawn(element(0, col_index), cofactor[0][col_index])
        det_real = det_real + det_term[0]
        det_imag = det_imag + det_term[1]
    weight = 1.0 / (det_real * det_real + det_imag * det_imag)
    inverse_det = (det_real * weight, -det_imag * weight)
    rows_real = []
    rows_imag = []
    for row_index in range(3):
        real_row = []
        imag_row = []
        for col_index in range(3):
            inverse_entry = complex_times_drawn(cofactor[col_index][row_index], inverse_det)
            delta_value = 1.0 if row_index == col_index else 0.0
            real_row.append(2.0 * inverse_entry[0] - delta_value)
            imag_row.append(2.0 * inverse_entry[1])
        rows_real.append(jnp.stack(real_row))
        rows_imag.append(jnp.stack(imag_row))
    unitary = jnp.stack([jnp.stack(rows_real), jnp.stack(rows_imag)])
    return jnp.moveaxis(unitary, 3, 0).astype(jnp.float32)


def draw_separations(key, part):
    key = jax.random.fold_in(key, 9)
    first_key, second_key = jax.random.split(key)
    values_drawn = jax.random.randint(first_key, (NR,), 1, CX + 1)
    marked = jax.random.randint(second_key, (), 0, NR)
    return jnp.where(jnp.arange(NR) == marked, CX, values_drawn).astype(jnp.int32)


def level_of(stream_key, extent, cuts, least, largest):
    gain = 1.0
    for dim, blocks in cuts:
        heights = jax.random.uniform(jax.random.fold_in(jax.random.fold_in(stream_key, 6), dim), (blocks,), jnp.float32, least / len(cuts), largest / len(cuts))
        gain = gain * jnp.repeat(jnp.exp(heights), extent[dim] // blocks).reshape((-1,) + (1,) * (len(extent) - 1 - dim))
    return gain


def noise(own_key, dims, deviation, reach, shards=(), kind=jnp.bfloat16):
    drawn = deviation * jax.random.normal(own_key, dims, jnp.float32)
    if shards:
        drawn = drawn * level_of(own_key, dims, shards, -0.22, 0.18)
    return jnp.clip(drawn, -reach, reach).astype(kind)


def setup_inputs(seed: int = 0) -> dict:
    arg_keys = jax.random.split(jax.random.key(seed), 4)
    return {
        "gauge_links": draw_gauge_links(jax.random.fold_in(arg_keys[3], 71), 0),
        "langevin_noise": noise(arg_keys[1], (SWEEPS, 4, 8, NT, SITES_ALONG_X, NYZ), 1.0, 4.0, ((3, 4), (4, 4), (5, 8))),
        "separations": draw_separations(jax.random.fold_in(arg_keys[3], 71), 0),
    }


step_drift = 0.2
step_noise = 0.4
root_third = 0.5773502691896258


def swapped(matrix_part):
    return jnp.swapaxes(matrix_part, 0, 1)


def dagger(matrix):
    return jnp.stack([swapped(matrix[0]), -swapped(matrix[1])])


def matrix_product(first, second):
    summed = None
    for middle in range(first.shape[1]):
        first_real = first[0][:, middle][:, None]
        first_imag = first[1][:, middle][:, None]
        second_real = second[0][middle][None]
        second_imag = second[1][middle][None]
        term_value = jnp.stack([first_real * second_real - first_imag * second_imag,
                                first_real * second_imag + first_imag * second_real])
        summed = term_value if summed is None else summed + term_value
    return summed


def identity_like(matrix_part):
    return jnp.eye(3, dtype=matrix_part.dtype).reshape((3, 3) + (1,) * (matrix_part.ndim - 2))


def traceless_anti(matrix):
    anti_real = 0.5 * (matrix[0] - swapped(matrix[0]))
    anti_imag = 0.5 * (matrix[1] + swapped(matrix[1]))
    trace_third = (anti_imag[0, 0] + anti_imag[1, 1] + anti_imag[2, 2]) / 3.0
    anti_imag = anti_imag - identity_like(anti_imag) * trace_third[None, None]
    return jnp.stack([anti_real, anti_imag])


def algebra(coeffs):
    zero_part = jnp.zeros_like(coeffs[0])
    diag_first = coeffs[2] + root_third * coeffs[7]
    diag_second = -coeffs[2] + root_third * coeffs[7]
    diag_third = -2.0 * root_third * coeffs[7]
    herm_real = jnp.stack([jnp.stack([diag_first, coeffs[0], coeffs[3]]),
                           jnp.stack([coeffs[0], diag_second, coeffs[5]]),
                           jnp.stack([coeffs[3], coeffs[5], diag_third])])
    herm_imag = jnp.stack([jnp.stack([zero_part, -coeffs[1], -coeffs[4]]),
                           jnp.stack([coeffs[1], zero_part, -coeffs[6]]),
                           jnp.stack([coeffs[4], coeffs[6], zero_part])])
    return 0.5 * jnp.stack([-herm_imag, herm_real])


def complex_times(first, second):
    return (first[0] * second[0] - first[1] * second[1], first[0] * second[1] + first[1] * second[0])


def cayley(generator, matrix):
    shift_real = identity_like(generator[0]) - 0.5 * generator[0]
    shift_imag = -0.5 * generator[1]

    def element(row_index, col_index):
        return (shift_real[row_index % 3, col_index % 3], shift_imag[row_index % 3, col_index % 3])

    cofactor = []
    for row_index in range(3):
        cof_row = []
        for col_index in range(3):
            forward = complex_times(element(row_index + 1, col_index + 1), element(row_index + 2, col_index + 2))
            backward = complex_times(element(row_index + 1, col_index + 2), element(row_index + 2, col_index + 1))
            cof_row.append((forward[0] - backward[0], forward[1] - backward[1]))
        cofactor.append(cof_row)
    det_real = 0.0
    det_imag = 0.0
    for col_index in range(3):
        det_term = complex_times(element(0, col_index), cofactor[0][col_index])
        det_real = det_real + det_term[0]
        det_imag = det_imag + det_term[1]
    weight = 1.0 / (det_real * det_real + det_imag * det_imag)
    inverse_det = (det_real * weight, -det_imag * weight)
    rotation_real = []
    rotation_imag = []
    for row_index in range(3):
        real_row = []
        imag_row = []
        for col_index in range(3):
            inverse_entry = complex_times(cofactor[col_index][row_index], inverse_det)
            delta_value = 1.0 if row_index == col_index else 0.0
            real_row.append(2.0 * inverse_entry[0] - delta_value)
            imag_row.append(2.0 * inverse_entry[1])
        rotation_real.append(jnp.stack(real_row))
        rotation_imag.append(jnp.stack(imag_row))
    rotation = jnp.stack([jnp.stack(rotation_real), jnp.stack(rotation_imag)])
    return matrix_product(rotation, matrix)


def unit_step(direction):
    return tuple(1 if axis_number == direction else 0 for axis_number in range(4))


def add_steps(first, second):
    return tuple(first_part + second_part for first_part, second_part in zip(first, second))


def negate(offsets):
    return tuple(-part_value for part_value in offsets)


def staple_sum(fetcher, direction):
    summed = None
    resting = (0, 0, 0, 0)
    onward = unit_step(direction)
    for transverse in range(4):
        if transverse == direction:
            continue
        across = unit_step(transverse)
        upper_loop = matrix_product(matrix_product(fetcher(transverse, onward), dagger(fetcher(direction, across))),
                             dagger(fetcher(transverse, resting)))
        lower_loop = matrix_product(matrix_product(dagger(fetcher(transverse, add_steps(onward, negate(across)))),
                                     dagger(fetcher(direction, negate(across)))),
                             fetcher(transverse, negate(across)))
        summed = upper_loop + lower_loop if summed is None else summed + upper_loop + lower_loop
    return summed


def updated_link(fetcher, direction, coeffs):
    current = fetcher(direction, (0, 0, 0, 0))
    force = traceless_anti(matrix_product(current, staple_sum(fetcher, direction)))
    generator = -step_drift * force + step_noise * algebra(coeffs)
    return cayley(generator, current)


def kron_conj(first, second):
    first_real = first[0][:, None, :, None]
    first_imag = first[1][:, None, :, None]
    second_real = second[0][None, :, None, :]
    second_imag = second[1][None, :, None, :]
    real_part = first_real * second_real + first_imag * second_imag
    imag_part = first_imag * second_real - first_real * second_imag
    new_shape = (9, 9) + real_part.shape[4:]
    return jnp.stack([real_part.reshape(new_shape), imag_part.reshape(new_shape)])


def mean_tensor(own_lines, far_lines):
    summed = None
    for measure in range(own_lines.shape[0]):
        term_value = kron_conj(own_lines[measure], far_lines[measure])
        summed = term_value if summed is None else summed + term_value
    return summed / own_lines.shape[0]


def diagonal_sum(matrix_part):
    summed = matrix_part[0, 0]
    for index_value in range(1, matrix_part.shape[0]):
        summed = summed + matrix_part[index_value, index_value]
    return summed


def shifted_field(lattice, link_dir, offsets):
    rolled = lattice[link_dir]
    for axis_number, offset in zip((-4, -3, -2, -1), offsets):
        if offset != 0:
            rolled = jnp.roll(rolled, -offset, axis=axis_number)
    return rolled


def slab_lines(temporal_links):
    slab_grouped = temporal_links.reshape(2, 3, 3, N_SLAB, SLAB_TIMES, SITES_ALONG_X, SITES_ALONG_Y, SITES_ALONG_Z)
    linked_product = slab_grouped[:, :, :, :, 0]
    for time_slice_index in range(1, SLAB_TIMES):
        linked_product = matrix_product(linked_product, slab_grouped[:, :, :, :, time_slice_index])
    return linked_product


def reference(gauge_links, langevin_noise, separations):
    lattice = gauge_links.reshape(4, 2, 3, 3, NT, SITES_ALONG_X, SITES_ALONG_Y, SITES_ALONG_Z)
    kick_field = langevin_noise.astype(jnp.float32).reshape(SWEEPS, 4, 8, NT, SITES_ALONG_X, SITES_ALONG_Y, SITES_ALONG_Z)
    time_axis = jnp.arange(NT).reshape(NT, 1, 1, 1)
    x_axis = jnp.arange(SITES_ALONG_X).reshape(1, SITES_ALONG_X, 1, 1)
    y_axis = jnp.arange(SITES_ALONG_Y).reshape(1, 1, SITES_ALONG_Y, 1)
    z_axis = jnp.arange(SITES_ALONG_Z).reshape(1, 1, 1, SITES_ALONG_Z)
    parity = (time_axis + x_axis + y_axis + z_axis) % 2
    interior = jnp.broadcast_to(time_axis % SLAB_TIMES != 0, (NT, SITES_ALONG_X, SITES_ALONG_Y, SITES_ALONG_Z))
    measured = []
    for sweep_index in range(SWEEPS):
        for direction in range(4):
            for colour in range(2):
                fetcher = partial(shifted_field, lattice)
                candidate = updated_link(fetcher, direction, kick_field[sweep_index, direction])
                chosen = parity == colour
                if direction > 0:
                    chosen = jnp.logical_and(chosen, interior)
                lattice = lattice.at[direction].set(jnp.where(chosen, candidate, lattice[direction]))
        measured.append(slab_lines(lattice[0]))
    line_stack = jnp.stack(measured)

    def correlate(separation):
        linked_product = None
        for slab_index in range(N_SLAB):
            own_lines = line_stack[:, :, :, :, slab_index]
            far_lines = jnp.roll(own_lines, -separation, axis=-3)
            tensor = mean_tensor(own_lines, far_lines)
            linked_product = tensor if linked_product is None else matrix_product(linked_product, tensor)
        return diagonal_sum(linked_product[0]).reshape(SITES_ALONG_X, SITES_ALONG_Y * SITES_ALONG_Z)

    return lax.map(correlate, separations)
```

```python
import jax
import jax.numpy as jnp
from jax import lax
from jax.experimental import pallas as pl
from jax.experimental.pallas import tpu as pltpu
from jax.sharding import PartitionSpec as P

SITES_ALONG_Z = 32
SWEEPS = 2

step_drift = 0.2
step_noise = 0.4
root_third = 0.5773502691896258

MESH = pl.DeviceIdType.MESH

OWN = slice(2, 5)
FIELDS = ((0, 0), (0, 1), (1, 1), (2, 1), (3, 1), (1, 0), (2, 0), (3, 0), (1, 2), (2, 2), (3, 2))
FIELD_OF = {field: index for index, field in enumerate(FIELDS)}
OWN_FIELDS = 8
FROZEN = 5
KICKS = ((0, 0, 0), (0, 0, 1), (0, 1, 1), (0, 2, 1), (0, 3, 1), (1, 0, 0), (1, 0, 1))
KICK_OF = {kick: index for index, kick in enumerate(KICKS)}
EARLY_KICKS = 3
FACES = tuple((dx, dy) for dx in (-1, 0, 1) for dy in (-1, 0, 1))
RING = tuple(face for face in FACES if face != (0, 0))


def rows_sent(dx):
    if dx == 1:
        return pl.ds(3, 2), pl.ds(0, 2)
    if dx == -1:
        return pl.ds(2, 3), pl.ds(5, 3)
    return pl.ds(2, 3), pl.ds(2, 3)


def mm(a, b):
    real = imag = None
    for k in range(3):
        ar, ai = a[0][:, k][:, None], a[1][:, k][:, None]
        br, bi = b[0][k][None], b[1][k][None]
        re, im = ar * br - ai * bi, ar * bi + ai * br
        real, imag = (re, im) if real is None else (real + re, imag + im)
    return real, imag


def mm_nh(a, b):
    real = imag = None
    for k in range(3):
        ar, ai = a[0][:, k][:, None], a[1][:, k][:, None]
        br, bi = b[0][:, k][None], b[1][:, k][None]
        re, im = ar * br + ai * bi, ai * br - ar * bi
        real, imag = (re, im) if real is None else (real + re, imag + im)
    return real, imag


def mm_hn(a, b):
    real = imag = None
    for k in range(3):
        ar, ai = a[0][k][:, None], a[1][k][:, None]
        br, bi = b[0][k][None], b[1][k][None]
        re, im = ar * br + ai * bi, ar * bi - ai * br
        real, imag = (re, im) if real is None else (real + re, imag + im)
    return real, imag


def times(a, b):
    return a[0] * b[0] - a[1] * b[1], a[0] * b[1] + a[1] * b[0]


def conj_times(a, b):
    return a[0] * b[0] + a[1] * b[1], a[0] * b[1] - a[1] * b[0]


def add(a, b):
    return a[0] + b[0], a[1] + b[1]


def cayley(product, noise, link):
    mr, mi = product
    n = noise
    drift = 0.25 * step_drift
    kick = 0.25 * step_noise

    def off(i, j, nr, ni):
        return (
            kick * nr - drift * (mr[i, j] - mr[j, i]),
            kick * ni - drift * (mi[i, j] + mi[j, i]),
        )

    p = off(0, 1, n[1], n[0])
    q = off(0, 2, n[4], n[3])
    r = off(1, 2, n[6], n[5])
    third = (mi[0, 0] + mi[1, 1] + mi[2, 2]) / 3.0
    eighth = root_third * n[7]
    a = kick * (eighth + n[2]) - 2.0 * drift * (mi[0, 0] - third)
    b = kick * (eighth - n[2]) - 2.0 * drift * (mi[1, 1] - third)
    c = -(a + b)
    pp = p[0] * p[0] + p[1] * p[1]
    qq = q[0] * q[0] + q[1] * q[1]
    rr = r[0] * r[0] + r[1] * r[1]
    bc, ac, ab = b * c, a * c, a * b
    pr = times(p, r)
    real = 1.0 + (pp + qq + rr) - (ab + ac + bc)
    odd = a * rr + b * qq + c * pp - a * bc - 2.0 * (pr[1] * q[0] - pr[0] * q[1])
    weight = 2.0 / (real * real + odd * odd)
    inv = (real * weight, odd * weight)
    rs = conj_times(r, q)
    ps = conj_times(p, q)
    s01 = (c * p[1] - rs[0], -c * p[0] - rs[1])
    s02 = (b * q[1] + pr[0], pr[1] - b * q[0])
    s12 = (a * r[1] - ps[0], -a * r[0] - ps[1])
    adj = [
        [(1.0 + rr - bc, a), add(s01, p), add(s02, q)],
        [(s01[0] - p[0], p[1] - s01[1]), (1.0 + qq - ac, b), add(s12, r)],
        [(s02[0] - q[0], q[1] - s02[1]), (s12[0] - r[0], r[1] - s12[1]), (1.0 + pp - ab, c)],
    ]
    rotation = [[times(entry, inv) for entry in row] for row in adj]
    for i in range(3):
        rotation[i][i] = (rotation[i][i][0] - 1.0, rotation[i][i][1])
    stacked = tuple(
        jnp.stack([jnp.stack([entry[part] for entry in row]) for row in rotation])
        for part in range(2)
    )
    return mm(stacked, link)


def kernel(
    links, kicks, separations, out,
    xb, yp, ym, ylo, yhi, xn, ynp, ynm, ynlo, ynhi,
    x1, y1p, y1m, y1lo, y1hi, x2, y2p, y2m, y2lo, y2hi,
    win, kwin, lines, send_sem, recv_sem,
):
    slabs, sxs, syzs = (lax.axis_size(axis) for axis in ("slab", "sx", "syz"))
    slab, sx, syz = (lax.axis_index(axis) for axis in ("slab", "sx", "syz"))

    def peer(ds, dx, dy):
        return (
            lax.rem(slab + ds + slabs, slabs),
            lax.rem(sx + dx + sxs, sxs),
            lax.rem(syz + dy + syzs, syzs),
        )

    peers = [(0, *face) for face in RING] + [(ds, *face) for ds in (-1, 1) for face in FACES]
    peers += [(2, dx, 0) for dx in (-1, 0, 1)]
    barrier = pltpu.get_barrier_semaphore()
    for one in peers:
        pl.semaphore_signal(barrier, inc=1, device_id=peer(*one), device_id_type=MESH)

    started = []

    def send(src, dst, target):
        index = len(started)
        copy = pltpu.make_async_remote_copy(
            src_ref=src,
            dst_ref=dst,
            send_sem=send_sem.at[index],
            recv_sem=recv_sem.at[index],
            device_id=peer(*target),
            device_id_type=MESH,
        )
        copy.start()
        started.append(copy)
        return copy

    shape = (8, 128)
    lane = lax.broadcasted_iota(jnp.int32, shape, 1)
    row = lax.broadcasted_iota(jnp.int32, shape, 0)
    half = lane % 16
    quarter = lane // 32
    low_half = lane < 64
    middle = jnp.logical_and(lane >= 32, lane < 96)
    first_of_half = (lane % 64) < 32
    odd_site = (sx * 3 + row + lane // 16) % 2
    is_odd = [odd_site == 1, odd_site == 0]
    last_half, first_half = half == 15, half == 0

    def own_index(time):
        lane3 = lax.broadcasted_iota(jnp.int32, (3, 128), 1)
        row3 = lax.broadcasted_iota(jnp.int32, (3, 128), 0)
        y = (lane3 % 64) // 16
        bit = (time + sx * 3 + row3 + y + lane3 // 64) % 2
        return y * 32 + (lane3 % 16) * 2 + bit

    own_gather = [own_index(0), own_index(1)]

    def put(x_buf, p_buf, m_buf, comp, pair, first, second, first3):
        count = first.shape[0]
        rolled = pltpu.roll(first, 96, 2)
        x_buf[comp : comp + count, OWN] = first
        x_buf[comp + count : comp + 2 * count, OWN] = second
        p_buf[pair : pair + count, OWN] = jnp.where(first3, rolled, second)
        m_buf[pair : pair + count, OWN] = jnp.where(first3, second, rolled)

    first3 = first_of_half[0:3]

    def spread(x_buf, p_buf, m_buf, lo_buf, hi_buf, comps, pairs, src=(0, 0), dst=(0, 0), ds=0):
        faces = RING if ds == 0 else FACES
        copies = []
        for dx, dy in faces:
            out_rows, in_rows = rows_sent(dx)
            if dy == 0:
                copies.append(
                    send(
                        x_buf.at[pl.ds(src[0], comps), out_rows],
                        x_buf.at[pl.ds(dst[0], comps), in_rows],
                        (ds, dx, dy),
                    )
                )
            else:
                out_buf, in_buf = (p_buf, lo_buf) if dy == 1 else (m_buf, hi_buf)
                copies.append(
                    send(
                        out_buf.at[pl.ds(src[1], pairs), out_rows],
                        in_buf.at[pl.ds(dst[1], pairs), in_rows],
                        (ds, dx, dy),
                    )
                )
        return copies

    def assemble(x_buf, lo_buf, hi_buf, comp, pair, count, target):
        lo, hi = lo_buf[pair : pair + count], hi_buf[pair : pair + count]
        for member in range(2):
            own = x_buf[comp + member * count : comp + (member + 1) * count]
            for parity in range(2):
                q = 2 * parity + member
                edge = jnp.where(quarter == q, lo, hi)
                if q:
                    edge = pltpu.roll(edge, 128 - 32 * q, 2)
                centre = pltpu.roll(own, 32 if parity == 0 else 96, 2)
                target(parity, member, jnp.where(middle, centre, edge))

    def link_target(field):
        def store(parity, member, value):
            win[field, parity, member] = value

        return store

    def kick_target(index):
        def store(parity, member, value):
            kwin[index, parity, member * 4 : member * 4 + 4] = value

        return store

    def packed(parts, time):
        return jnp.stack([jnp.take_along_axis(part, own_gather[time], axis=1) for part in parts])

    def pack_kick(index, x_buf, p_buf, m_buf, comp, pair):
        sweep, direction, time = KICKS[index]
        parts = [kicks[sweep, direction, a, time].astype(jnp.float32) for a in range(8)]
        put(x_buf, p_buf, m_buf, comp, pair, packed(parts[:4], time), packed(parts[4:], time), first3)

    link_comp = 8 * EARLY_KICKS
    link_pair = 4 * EARLY_KICKS
    for index in range(EARLY_KICKS):
        pack_kick(index, xb, yp, ym, 8 * index, 4 * index)
    for field in range(OWN_FIELDS):
        direction, time = FIELDS[field]
        first, second = (
            packed([links[direction, part, i, j, time] for i in range(3) for j in range(3)], time)
            for part in range(2)
        )
        put(xb, yp, ym, link_comp + 18 * field, link_pair + 9 * field, first, second, first3)

    pl.semaphore_wait(barrier, len(peers))

    own_comps = link_comp + 18 * OWN_FIELDS
    own_pairs = link_pair + 9 * OWN_FIELDS
    frozen = spread(
        xb, yp, ym, ylo, yhi, 54, 27,
        (link_comp + 18 * FROZEN, link_pair + 9 * FROZEN), (own_comps, own_pairs), -1,
    )
    first_halo = spread(xb, yp, ym, ylo, yhi, own_comps, own_pairs)
    late = len(KICKS) - EARLY_KICKS
    for index in range(late):
        pack_kick(EARLY_KICKS + index, xn, ynp, ynm, 8 * index, 4 * index)
    late_halo = spread(xn, ynp, ynm, ynlo, ynhi, 8 * late, 4 * late)

    for copy in first_halo + frozen:
        copy.wait_recv()
    for index in range(EARLY_KICKS):
        assemble(xb, ylo, yhi, 8 * index, 4 * index, 4, kick_target(index))
    for field in range(len(FIELDS)):
        assemble(xb, ylo, yhi, link_comp + 18 * field, link_pair + 9 * field, 9, link_target(field))

    def shifted(pair, axis, sign, time, parity):
        def one(value):
            if axis == 0:
                return value
            flat = value.reshape(9, 8, 128)
            if axis == 1:
                flat = pltpu.roll(flat, 7 if sign == 1 else 1, 1)
            elif axis == 2:
                flat = pltpu.roll(flat, 112 if sign == 1 else 16, 2)
            else:
                odd = is_odd[(time + parity) % 2]
                if sign == 1:
                    inner = jnp.where(last_half, pltpu.roll(flat, 15, 2), pltpu.roll(flat, 127, 2))
                    flat = jnp.where(odd, inner, flat)
                else:
                    inner = jnp.where(first_half, pltpu.roll(flat, 113, 2), pltpu.roll(flat, 1, 2))
                    flat = jnp.where(odd, flat, inner)
            return flat.reshape(3, 3, 8, 128)

        return one(pair[0]), one(pair[1])

    def link(direction, time, parity):
        field = FIELD_OF[direction, time]
        return tuple(win[field, parity, part].reshape(3, 3, 8, 128) for part in range(2))

    def staples(mu, time, parity):
        total = None
        other = 1 - parity
        for nu in range(4):
            if nu == mu:
                continue
            if mu == 0:
                ahead = link(nu, time + 1, other)
                ahead_low = link(nu, time + 1, parity)
            else:
                ahead = shifted(link(nu, time, other), mu, 1, time, parity)
            if nu == 0:
                above, below = link(mu, time + 1, other), link(mu, time - 1, other)
                low_time = time - 1
            else:
                above = shifted(link(mu, time, other), nu, 1, time, parity)
                below = link(mu, time, other)
                low_time = time
            if mu != 0:
                ahead_low = shifted(
                    link(nu, low_time, parity), mu, 1, low_time, other
                )
            upper = mm_nh(mm_nh(ahead, above), link(nu, time, parity))
            lower = mm_hn(mm(below, ahead_low), link(nu, low_time, other))
            lower = shifted(lower, nu, -1, time, parity)
            both = add(upper, lower)
            total = both if total is None else add(total, both)
        return total

    def substep(sweep, mu, parity):
        for time in (0, 1) if mu == 0 else (1,):
            current = link(mu, time, parity)
            noise = kwin[KICK_OF[sweep, mu, time], parity]
            new = cayley(mm(current, staples(mu, time, parity)), noise, current)
            field = FIELD_OF[mu, time]
            for part in range(2):
                win[field, parity, part] = new[part].reshape(9, 8, 128)

    def own_part(two):
        return jnp.where(low_half, pltpu.roll(two[0], 96, 2), pltpu.roll(two[1], 32, 2))

    def exchange(fields, x_buf, p_buf, m_buf, lo_buf, hi_buf):
        for index, field in enumerate(fields):
            first, second = (
                own_part([win[field, parity, part] for parity in range(2)])[:, OWN]
                for part in range(2)
            )
            put(x_buf, p_buf, m_buf, 18 * index, 9 * index, first, second, first3)
        return spread(x_buf, p_buf, m_buf, lo_buf, hi_buf, 18 * len(fields), 9 * len(fields))

    def collect(copies, fields, x_buf, lo_buf, hi_buf):
        for copy in copies:
            copy.wait_recv()
        for index, field in enumerate(fields):
            assemble(x_buf, lo_buf, hi_buf, 18 * index, 9 * index, 9, link_target(field))

    def measure(sweep):
        products = [mm(link(0, 0, parity), link(0, 1, 1 - parity)) for parity in range(2)]
        for part in range(2):
            two = [product[part].reshape(9, 8, 128) for product in products]
            lines[sweep, 0, 9 * part : 9 * part + 9, 0:3] = own_part(two)[:, OWN]
        copies = []
        src = lines.at[sweep, 0, :, pl.ds(0, 3)]
        for ds in range(4):
            if ds:
                copies.append(send(src, lines.at[sweep, ds, :, pl.ds(0, 3)], (-ds, 0, 0)))
            copies.append(send(src, lines.at[sweep, ds, :, pl.ds(3, 3)], (-ds, -1, 0)))
        return copies

    substep(0, 0, 0)
    substep(0, 0, 1)
    substep(0, 1, 0)
    after = (FIELD_OF[0, 0], FIELD_OF[0, 1], FIELD_OF[1, 1])
    copies = exchange(after, x1, y1p, y1m, y1lo, y1hi)
    line_copies = measure(0)
    for copy in late_halo:
        copy.wait_recv()
    for index in range(late):
        assemble(xn, ynlo, ynhi, 8 * index, 4 * index, 4, kick_target(EARLY_KICKS + index))
    collect(copies, after, x1, y1lo, y1hi)
    substep(0, 1, 1)
    substep(0, 2, 0)
    substep(0, 2, 1)
    substep(0, 3, 0)
    after = (FIELD_OF[1, 1], FIELD_OF[2, 1], FIELD_OF[3, 1])
    copies = exchange(after, x2, y2p, y2m, y2lo, y2hi)
    collect(copies, after, x2, y2lo, y2hi)
    substep(0, 3, 1)
    substep(1, 0, 0)
    substep(1, 0, 1)
    line_copies += measure(1)
    for copy in line_copies:
        copy.wait_recv()

    def line(sweep, ds):
        return tuple(
            lines[sweep, ds, 9 * part : 9 * part + 9].reshape(3, 3, 8, 128) for part in range(2)
        )

    low = [mm(line(m, 0), line(n, 1)) for m in range(SWEEPS) for n in range(SWEEPS)]
    high = [mm(line(m, 2), line(n, 3)) for m in range(SWEEPS) for n in range(SWEEPS)]
    loops = []
    for left in low:
        for right in high:
            rr, ri = (jnp.swapaxes(part, 0, 1) for part in right)
            loops.append(jnp.sum((left[0] * rr - left[1] * ri).reshape(9, 8, 128), axis=0))
            loops.append(jnp.sum((left[0] * ri + left[1] * rr).reshape(9, 8, 128), axis=0))
    loops = jnp.stack(loops)
    distance = separations[slab]
    result = None
    for r in (3, 2, 1):
        far = pltpu.roll(loops, 8 - r, 1)
        if r % 2:
            far = pltpu.roll(far, 64, 2)
        value = jnp.sum(loops * far, axis=0)
        result = value if result is None else jnp.where(distance == r, value, result)
    result = result * (1.0 / SWEEPS**4)
    lane3 = lax.broadcasted_iota(jnp.int32, (3, 128), 1)
    row3 = lax.broadcasted_iota(jnp.int32, (3, 128), 0)
    y, z = lane3 // 32, lane3 % 32
    index = ((z + y + row3 + sx * 3) % 2) * 64 + y * 16 + z // 2
    out[0] = jnp.take_along_axis(result[0:3], index, axis=1)

    for copy in started:
        copy.wait_send()


def local(gauge_links, langevin_noise, separations):
    early = 8 * EARLY_KICKS + 18 * len(FIELDS)
    late = 8 * (len(KICKS) - EARLY_KICKS)

    def buffers(comps):
        halves = [pltpu.VMEM((comps // 2, 8, 128), jnp.float32)] * 4
        return [pltpu.VMEM((comps, 8, 128), jnp.float32)] + halves

    copies = 9 + 5 * 8 - 8 + 14
    vmem = pl.BlockSpec(memory_space=pltpu.VMEM)
    return pl.pallas_call(
        kernel,
        out_shape=jax.ShapeDtypeStruct((1, 3, 128), jnp.float32),
        in_specs=[vmem, vmem, pl.BlockSpec(memory_space=pltpu.SMEM)],
        out_specs=vmem,
        scratch_shapes=buffers(early) + buffers(late) + buffers(54) + buffers(54) + [
            pltpu.VMEM((len(FIELDS), 2, 2, 9, 8, 128), jnp.float32),
            pltpu.VMEM((len(KICKS), 2, 8, 8, 128), jnp.float32),
            pltpu.VMEM((SWEEPS, 4, 18, 8, 128), jnp.float32),
            pltpu.SemaphoreType.DMA((copies,)),
            pltpu.SemaphoreType.DMA((copies,)),
        ],
        compiler_params=pltpu.CompilerParams(
            collective_id=0, has_side_effects=True, vmem_limit_bytes=40 * 1024 * 1024
        ),
    )(gauge_links, langevin_noise, separations)


def solution(mesh):
    return jax.shard_map(
        local,
        mesh=mesh,
        in_specs=(
            P(None, None, None, None, "slab", "sx", "syz"),
            P(None, None, None, "slab", "sx", "syz"),
            P(),
        ),
        out_specs=P("slab", "sx", "syz"),
        check_vma=False,
    )
```

```python
import jax
import jax.numpy as jnp
from jax import lax
from jax.experimental import pallas as pl
from jax.experimental.pallas import tpu as pltpu
from jax.sharding import PartitionSpec as P

SITES_ALONG_Z = 32
SWEEPS = 2

step_drift = 0.2
step_noise = 0.4
root_third = 0.5773502691896258

MESH = pl.DeviceIdType.MESH

OWN = slice(2, 5)
FIELDS = ((0, 0), (0, 1), (1, 1), (2, 1), (3, 1), (1, 0), (2, 0), (3, 0), (1, 2), (2, 2), (3, 2))
FIELD_OF = {field: index for index, field in enumerate(FIELDS)}
KICKS = ((0, 0, 0), (0, 0, 1), (0, 1, 1), (0, 2, 1), (0, 3, 1), (1, 0, 0), (1, 0, 1))
KICK_OF = {kick: index for index, kick in enumerate(KICKS)}
LINK, KICK = 7, 4


def placed(*entries):
    offsets, total = {}, 0
    for entry in entries:
        offsets[entry] = total
        total += LINK if len(entry) == 2 else KICK
    return offsets, total


FIRST, FIRST_PAIRS = placed(
    (0, 0), (0, 0, 0), (1, 1), (2, 0), (3, 0), (1, 0), (2, 1), (3, 1)
)
SECOND, SECOND_PAIRS = placed((2, 2), (3, 2), (1, 2), (0, 1), (0, 0, 1), (0, 1, 1))
LATE, LATE_PAIRS = placed((0, 2, 1), (0, 3, 1), (1, 0, 0), (1, 0, 1))
TURN, TURN_PAIRS = placed((0, 0), (0, 1), (1, 1))
TURN2, TURN2_PAIRS = placed((1, 1), (2, 1), (3, 1))
FACES = tuple((dx, dy) for dx in (-1, 0, 1) for dy in (-1, 0, 1))
RING = tuple(face for face in FACES if face != (0, 0))
COPIES = 11 + 11 + 11 + 8 + 3 * 8 + 3 * 8 + 14


def rows_sent(dx, count):
    if dx == 1:
        return pl.ds(5 - count, count), pl.ds(2 - count, count)
    if dx == -1:
        return pl.ds(2, count), pl.ds(5, count)
    return pl.ds(2, 3), pl.ds(2, 3)


def mm(a, b):
    real = imag = None
    for k in range(3):
        ar, ai = a[0][:, k][:, None], a[1][:, k][:, None]
        br, bi = b[0][k][None], b[1][k][None]
        re, im = ar * br - ai * bi, ar * bi + ai * br
        real, imag = (re, im) if real is None else (real + re, imag + im)
    return real, imag


def mm_nh(a, b):
    real = imag = None
    for k in range(3):
        ar, ai = a[0][:, k][:, None], a[1][:, k][:, None]
        br, bi = b[0][:, k][None], b[1][:, k][None]
        re, im = ar * br + ai * bi, ai * br - ar * bi
        real, imag = (re, im) if real is None else (real + re, imag + im)
    return real, imag


def mm_hn(a, b):
    real = imag = None
    for k in range(3):
        ar, ai = a[0][k][:, None], a[1][k][:, None]
        br, bi = b[0][k][None], b[1][k][None]
        re, im = ar * br + ai * bi, ar * bi - ai * br
        real, imag = (re, im) if real is None else (real + re, imag + im)
    return real, imag


def times(a, b):
    return a[0] * b[0] - a[1] * b[1], a[0] * b[1] + a[1] * b[0]


def conj_times(a, b):
    return a[0] * b[0] + a[1] * b[1], a[0] * b[1] - a[1] * b[0]


def add(a, b):
    return a[0] + b[0], a[1] + b[1]


def cross(re, im):
    entry = [(re[k], im[k]) for k in range(6)]
    found = []
    for j in range(3):
        k, m = (j + 1) % 3, (j + 2) % 3
        one, two = times(entry[k], entry[3 + m]), times(entry[m], entry[3 + k])
        found.append((one[0] - two[0], one[1] - two[1]))
    return found


def compress(re, im):
    terms = [times((re[6 + j], im[6 + j]), value) for j, value in enumerate(cross(re, im))]
    phase = add(add(terms[0], terms[1]), terms[2])
    return (
        jnp.concatenate([re[0:6], phase[0][None]], axis=0),
        jnp.concatenate([im[0:6], phase[1][None]], axis=0),
    )


def restore(re, im):
    third = [conj_times(value, (re[6], im[6])) for value in cross(re, im)]
    return (
        jnp.concatenate([re[0:6], jnp.stack([value[0] for value in third])], axis=0),
        jnp.concatenate([im[0:6], jnp.stack([value[1] for value in third])], axis=0),
    )


def cayley(product, noise, link):
    mr, mi = product
    n = noise
    drift = 0.25 * step_drift
    kick = 0.25 * step_noise

    def off(i, j, nr, ni):
        return (
            kick * nr - drift * (mr[i, j] - mr[j, i]),
            kick * ni - drift * (mi[i, j] + mi[j, i]),
        )

    p = off(0, 1, n[1], n[0])
    q = off(0, 2, n[4], n[3])
    r = off(1, 2, n[6], n[5])
    third = (mi[0, 0] + mi[1, 1] + mi[2, 2]) / 3.0
    eighth = root_third * n[7]
    a = kick * (eighth + n[2]) - 2.0 * drift * (mi[0, 0] - third)
    b = kick * (eighth - n[2]) - 2.0 * drift * (mi[1, 1] - third)
    c = -(a + b)
    pp = p[0] * p[0] + p[1] * p[1]
    qq = q[0] * q[0] + q[1] * q[1]
    rr = r[0] * r[0] + r[1] * r[1]
    bc, ac, ab = b * c, a * c, a * b
    pr = times(p, r)
    real = 1.0 + (pp + qq + rr) - (ab + ac + bc)
    odd = a * rr + b * qq + c * pp - a * bc - 2.0 * (pr[1] * q[0] - pr[0] * q[1])
    weight = 2.0 / (real * real + odd * odd)
    inv = (real * weight, odd * weight)
    rs = conj_times(r, q)
    ps = conj_times(p, q)
    s01 = (c * p[1] - rs[0], -c * p[0] - rs[1])
    s02 = (b * q[1] + pr[0], pr[1] - b * q[0])
    s12 = (a * r[1] - ps[0], -a * r[0] - ps[1])
    adj = [
        [(1.0 + rr - bc, a), add(s01, p), add(s02, q)],
        [(s01[0] - p[0], p[1] - s01[1]), (1.0 + qq - ac, b), add(s12, r)],
        [(s02[0] - q[0], q[1] - s02[1]), (s12[0] - r[0], r[1] - s12[1]), (1.0 + pp - ab, c)],
    ]
    rotation = [[times(entry, inv) for entry in row] for row in adj]
    for i in range(3):
        rotation[i][i] = (rotation[i][i][0] - 1.0, rotation[i][i][1])
    stacked = tuple(
        jnp.stack([jnp.stack([entry[part] for entry in row]) for row in rotation])
        for part in range(2)
    )
    return mm(stacked, link)


def kernel(
    links, kicks, separations, out,
    first_set, second_set, late_set, turn_set, turn2_set,
    win, kwin, lines, send_sem, recv_sem,
):
    slabs, sxs, syzs = (lax.axis_size(axis) for axis in ("slab", "sx", "syz"))
    slab, sx, syz = (lax.axis_index(axis) for axis in ("slab", "sx", "syz"))

    def peer(ds, dx, dy):
        return (
            lax.rem(slab + ds + slabs, slabs),
            lax.rem(sx + dx + sxs, sxs),
            lax.rem(syz + dy + syzs, syzs),
        )

    peers = [(0, *face) for face in RING] + [(ds, *face) for ds in (-1, 1) for face in FACES]
    peers += [(2, dx, 0) for dx in (-1, 0, 1)]
    barrier = pltpu.get_barrier_semaphore()
    for one in peers:
        pl.semaphore_signal(barrier, inc=1, device_id=peer(*one), device_id_type=MESH)

    started = []

    def send(src, dst, target):
        index = len(started)
        copy = pltpu.make_async_remote_copy(
            src_ref=src,
            dst_ref=dst,
            send_sem=send_sem.at[index],
            recv_sem=recv_sem.at[index],
            device_id=peer(*target),
            device_id_type=MESH,
        )
        copy.start()
        started.append(copy)
        return copy

    shape = (8, 128)
    lane = lax.broadcasted_iota(jnp.int32, shape, 1)
    row = lax.broadcasted_iota(jnp.int32, shape, 0)
    half = lane % 16
    quarter = lane // 32
    low_half = lane < 64
    middle = jnp.logical_and(lane >= 32, lane < 96)
    first_of_half = (lane % 64) < 32
    odd_site = (sx * 3 + row + lane // 16) % 2
    is_odd = [odd_site == 1, odd_site == 0]
    last_half, first_half = half == 15, half == 0

    def own_index(time):
        lane3 = lax.broadcasted_iota(jnp.int32, (3, 128), 1)
        row3 = lax.broadcasted_iota(jnp.int32, (3, 128), 0)
        y = (lane3 % 64) // 16
        bit = (time + sx * 3 + row3 + y + lane3 // 64) % 2
        return y * 32 + (lane3 % 16) * 2 + bit

    own_gather = [own_index(0), own_index(1)]

    first3 = first_of_half[0:3]

    def put(bufs, pair, first, second):
        x_buf, p_buf, m_buf = bufs[:3]
        count = first.shape[0]
        rolled = pltpu.roll(first, 96, 2)
        x_buf[2 * pair : 2 * pair + count, OWN] = first
        x_buf[2 * pair + count : 2 * pair + 2 * count, OWN] = second
        p_buf[pair : pair + count, OWN] = jnp.where(first3, rolled, second)
        m_buf[pair : pair + count, OWN] = jnp.where(first3, second, rolled)

    def hand(bufs, face, low, high, count=2, ds=0, to=None):
        dx, dy = face
        goal, goal_low = (bufs, low) if to is None else to
        out_rows, in_rows = rows_sent(dx, count)
        if dy == 0:
            low, high, goal_low = 2 * low, 2 * high, 2 * goal_low
            src, dst = bufs[0], goal[0]
        else:
            src, dst = (bufs[1], goal[3]) if dy == 1 else (bufs[2], goal[4])
        return send(
            src.at[pl.ds(low, high - low), out_rows],
            dst.at[pl.ds(goal_low, high - low), in_rows],
            (ds, dx, dy),
        )

    def assemble(bufs, pair, count):
        x_buf, _, _, lo_buf, hi_buf = bufs
        lo, hi = lo_buf[pair : pair + count], hi_buf[pair : pair + count]
        found = [[None, None], [None, None]]
        for member in range(2):
            start = 2 * pair + member * count
            own = x_buf[start : start + count]
            for parity in range(2):
                q = 2 * parity + member
                edge = jnp.where(quarter == q, lo, hi)
                if q:
                    edge = pltpu.roll(edge, 128 - 32 * q, 2)
                centre = pltpu.roll(own, 32 if parity == 0 else 96, 2)
                found[parity][member] = jnp.where(middle, centre, edge)
        return found

    def take_in(bufs, places, entries):
        for entry in entries:
            if len(entry) == 2:
                found = assemble(bufs, places[entry], LINK)
                for parity in range(2):
                    for part, value in enumerate(restore(*found[parity])):
                        win[FIELD_OF[entry], parity, part] = value
            else:
                found = assemble(bufs, places[entry], KICK)
                for parity in range(2):
                    for member in range(2):
                        kwin[KICK_OF[entry], parity, 4 * member : 4 * member + 4] = found[parity][member]

    def packed(parts, time):
        return jnp.stack([jnp.take_along_axis(part, own_gather[time], axis=1) for part in parts])

    def pack(bufs, places, entries):
        for entry in entries:
            if len(entry) == 2:
                direction, time = entry
                whole = [
                    packed(
                        [links[direction, part, i, j, time] for i in range(3) for j in range(3)], time
                    )
                    for part in range(2)
                ]
                put(bufs, places[entry], *compress(*whole))
            else:
                sweep, direction, time = entry
                parts = [kicks[sweep, direction, a, time].astype(jnp.float32) for a in range(8)]
                put(bufs, places[entry], packed(parts[:4], time), packed(parts[4:], time))

    def wait(copies):
        for copy in copies:
            copy.wait_recv()

    pack(first_set, FIRST, FIRST)
    pl.semaphore_wait(barrier, len(peers))

    pair, wide = FIRST_PAIRS, FIRST[1, 0]
    first_copies = [
        hand(first_set, (1, 0), 0, pair),
        hand(first_set, (-1, 0), 0, LINK, 3),
        hand(first_set, (-1, 0), LINK, pair),
    ]
    for dy in (1, -1):
        first_copies.append(hand(first_set, (0, dy), 0, pair))
        first_copies.append(hand(first_set, (1, dy), 0, wide, 1))
        first_copies.append(hand(first_set, (1, dy), wide, pair))
        first_copies.append(hand(first_set, (-1, dy), 0, pair))
    low, high = FIRST[2, 0], FIRST[1, 0] + LINK
    goal = (second_set, SECOND[2, 2])
    second_copies = []
    for face in ((0, 0), (1, 0), (-1, 0), (0, 1), (0, -1), (-1, 1), (-1, -1)):
        second_copies.append(hand(first_set, face, low, high, 2, -1, goal))
    for dy in (1, -1):
        second_copies.append(hand(first_set, (1, dy), low, FIRST[1, 0], 1, -1, goal))
        second_copies.append(
            hand(first_set, (1, dy), FIRST[1, 0], high, 2, -1, (second_set, SECOND[1, 2]))
        )
    pack(second_set, SECOND, ((0, 1), (0, 0, 1), (0, 1, 1)))
    low, high, wide = SECOND[0, 1], SECOND_PAIRS, SECOND[0, 1, 1]
    second_copies += [
        hand(second_set, (1, 0), low, high),
        hand(second_set, (-1, 0), low, low + LINK, 3),
        hand(second_set, (-1, 0), low + LINK, high),
    ]
    for dy in (1, -1):
        second_copies.append(hand(second_set, (0, dy), low, high))
        second_copies.append(hand(second_set, (1, dy), low, wide, 1))
        second_copies.append(hand(second_set, (1, dy), wide, high))
        second_copies.append(hand(second_set, (-1, dy), low, high))
    pack(late_set, LATE, LATE)
    late_copies = [hand(late_set, face, 0, LATE_PAIRS, 1) for face in RING]

    def shifted(pair, axis, sign, time, parity):
        def one(value):
            if axis == 0:
                return value
            flat = value.reshape(9, 8, 128)
            if axis == 1:
                flat = pltpu.roll(flat, 7 if sign == 1 else 1, 1)
            elif axis == 2:
                flat = pltpu.roll(flat, 112 if sign == 1 else 16, 2)
            else:
                odd = is_odd[(time + parity) % 2]
                if sign == 1:
                    inner = jnp.where(last_half, pltpu.roll(flat, 15, 2), pltpu.roll(flat, 127, 2))
                    flat = jnp.where(odd, inner, flat)
                else:
                    inner = jnp.where(first_half, pltpu.roll(flat, 113, 2), pltpu.roll(flat, 1, 2))
                    flat = jnp.where(odd, flat, inner)
            return flat.reshape(3, 3, 8, 128)

        return one(pair[0]), one(pair[1])

    def link(direction, time, parity):
        field = FIELD_OF[direction, time]
        return tuple(win[field, parity, part].reshape(3, 3, 8, 128) for part in range(2))

    def staples(mu, time, parity):
        total = None
        other = 1 - parity
        for nu in range(4):
            if nu == mu:
                continue
            if mu == 0:
                ahead = link(nu, time + 1, other)
                ahead_low = link(nu, time + 1, parity)
            else:
                ahead = shifted(link(nu, time, other), mu, 1, time, parity)
            if nu == 0:
                above, below = link(mu, time + 1, other), link(mu, time - 1, other)
                low_time = time - 1
            else:
                above = shifted(link(mu, time, other), nu, 1, time, parity)
                below = link(mu, time, other)
                low_time = time
            if mu != 0:
                ahead_low = shifted(
                    link(nu, low_time, parity), mu, 1, low_time, other
                )
            upper = mm_nh(mm_nh(ahead, above), link(nu, time, parity))
            lower = mm_hn(mm(below, ahead_low), link(nu, low_time, other))
            lower = shifted(lower, nu, -1, time, parity)
            both = add(upper, lower)
            total = both if total is None else add(total, both)
        return total

    def substep(sweep, mu, parity, time=1):
        current = link(mu, time, parity)
        noise = kwin[KICK_OF[sweep, mu, time], parity]
        new = cayley(mm(current, staples(mu, time, parity)), noise, current)
        field = FIELD_OF[mu, time]
        for part in range(2):
            win[field, parity, part] = new[part].reshape(9, 8, 128)

    def own_part(two):
        return jnp.where(low_half, pltpu.roll(two[0], 96, 2), pltpu.roll(two[1], 32, 2))

    def pass_on(bufs, places, entry, corner):
        whole = [
            own_part([win[FIELD_OF[entry], parity, part] for parity in range(2)])[:, OWN]
            for part in range(2)
        ]
        low = places[entry]
        put(bufs, low, *compress(*whole))
        return [
            hand(bufs, face, low, low + LINK, corner if face[0] and face[1] else 2) for face in RING
        ]

    def measure(sweep):
        products = [mm(link(0, 0, parity), link(0, 1, 1 - parity)) for parity in range(2)]
        whole = [
            own_part([product[part].reshape(9, 8, 128) for product in products])[:, OWN]
            for part in range(2)
        ]
        for part, value in enumerate(compress(*whole)):
            lines[sweep, 0, LINK * part : LINK * part + LINK, 0:3] = value
        copies = []
        src = lines.at[sweep, 0, :, pl.ds(0, 3)]
        for ds in range(4):
            if ds:
                copies.append(send(src, lines.at[sweep, ds, :, pl.ds(0, 3)], (-ds, 0, 0)))
            copies.append(send(src, lines.at[sweep, ds, :, pl.ds(3, 3)], (-ds, -1, 0)))
        return copies

    wait(first_copies)
    take_in(first_set, FIRST, FIRST)
    substep(0, 0, 0, 0)
    substep(0, 0, 1, 0)
    turn_copies = pass_on(turn_set, TURN, (0, 0), 2)
    wait(second_copies)
    take_in(second_set, SECOND, SECOND)
    substep(0, 0, 0, 1)
    substep(0, 0, 1, 1)
    turn_copies += pass_on(turn_set, TURN, (0, 1), 2)
    substep(0, 1, 0)
    turn_copies += pass_on(turn_set, TURN, (1, 1), 2)
    line_copies = measure(0)
    wait(late_copies)
    take_in(late_set, LATE, LATE)
    wait(turn_copies)
    take_in(turn_set, TURN, TURN)
    substep(0, 1, 1)
    turn_copies = pass_on(turn2_set, TURN2, (1, 1), 1)
    substep(0, 2, 0)
    substep(0, 2, 1)
    turn_copies += pass_on(turn2_set, TURN2, (2, 1), 1)
    substep(0, 3, 0)
    turn_copies += pass_on(turn2_set, TURN2, (3, 1), 1)
    wait(turn_copies)
    take_in(turn2_set, TURN2, TURN2)
    substep(0, 3, 1)
    for time in range(2):
        substep(1, 0, 0, time)
        substep(1, 0, 1, time)
    line_copies += measure(1)
    wait(line_copies)

    def line(sweep, ds):
        whole = restore(lines[sweep, ds, 0:LINK], lines[sweep, ds, LINK : 2 * LINK])
        return tuple(part.reshape(3, 3, 8, 128) for part in whole)

    line_of = [[line(m, ds) for ds in range(4)] for m in range(SWEEPS)]
    low = [mm(line_of[m][0], line_of[n][1]) for m in range(SWEEPS) for n in range(SWEEPS)]
    high = [mm(line_of[m][2], line_of[n][3]) for m in range(SWEEPS) for n in range(SWEEPS)]
    loops = []
    for left in low:
        for right in high:
            rr, ri = (jnp.swapaxes(part, 0, 1) for part in right)
            loops.append(jnp.sum((left[0] * rr - left[1] * ri).reshape(9, 8, 128), axis=0))
            loops.append(jnp.sum((left[0] * ri + left[1] * rr).reshape(9, 8, 128), axis=0))
    loops = jnp.stack(loops)
    distance = separations[slab]
    result = None
    for r in (3, 2, 1):
        far = pltpu.roll(loops, 8 - r, 1)
        if r % 2:
            far = pltpu.roll(far, 64, 2)
        value = jnp.sum(loops * far, axis=0)
        result = value if result is None else jnp.where(distance == r, value, result)
    result = result * (1.0 / SWEEPS**4)
    lane3 = lax.broadcasted_iota(jnp.int32, (3, 128), 1)
    row3 = lax.broadcasted_iota(jnp.int32, (3, 128), 0)
    y, z = lane3 // 32, lane3 % 32
    index = ((z + y + row3 + sx * 3) % 2) * 64 + y * 16 + z // 2
    out[0] = jnp.take_along_axis(result[0:3], index, axis=1)

    for copy in started:
        copy.wait_send()


def local(gauge_links, langevin_noise, separations):
    def buffers(pairs):
        halves = tuple(pltpu.VMEM((pairs, 8, 128), jnp.float32) for _ in range(4))
        return (pltpu.VMEM((2 * pairs, 8, 128), jnp.float32), *halves)

    sets = (FIRST_PAIRS, SECOND_PAIRS, LATE_PAIRS, TURN_PAIRS, TURN2_PAIRS)
    vmem = pl.BlockSpec(memory_space=pltpu.VMEM)
    return pl.pallas_call(
        kernel,
        out_shape=jax.ShapeDtypeStruct((1, 3, 128), jnp.float32),
        in_specs=[vmem, vmem, pl.BlockSpec(memory_space=pltpu.SMEM)],
        out_specs=vmem,
        scratch_shapes=[buffers(pairs) for pairs in sets] + [
            pltpu.VMEM((len(FIELDS), 2, 2, 9, 8, 128), jnp.float32),
            pltpu.VMEM((len(KICKS), 2, 8, 8, 128), jnp.float32),
            pltpu.VMEM((SWEEPS, 4, 2 * LINK, 8, 128), jnp.float32),
            pltpu.SemaphoreType.DMA((COPIES,)),
            pltpu.SemaphoreType.DMA((COPIES,)),
        ],
        compiler_params=pltpu.CompilerParams(
            collective_id=0, has_side_effects=True, vmem_limit_bytes=40 * 1024 * 1024
        ),
    )(gauge_links, langevin_noise, separations)


def solution(mesh):
    return jax.shard_map(
        local,
        mesh=mesh,
        in_specs=(
            P(None, None, None, None, "slab", "sx", "syz"),
            P(None, None, None, "slab", "sx", "syz"),
            P(),
        ),
        out_specs=P("slab", "sx", "syz"),
        check_vma=False,
    )
```

```python
import jax
import jax.numpy as jnp
from jax import lax
from jax.experimental import pallas as pl
from jax.experimental.pallas import tpu as pltpu
from jax.sharding import PartitionSpec as P

SITES_ALONG_Z = 32
SWEEPS = 2

step_drift = 0.2
step_noise = 0.4
root_third = 0.5773502691896258

MESH = pl.DeviceIdType.MESH
VMEM_LIMIT = 60 * 1024 * 1024

OWN = slice(2, 5)
FIELDS = ((0, 0), (0, 1), (1, 1), (2, 1), (3, 1), (1, 0), (2, 0), (3, 0), (1, 2), (2, 2), (3, 2))
FIELD_OF = {field: index for index, field in enumerate(FIELDS)}
KICKS = ((0, 0, 0), (0, 0, 1), (0, 1, 1), (0, 2, 1), (0, 3, 1), (1, 0, 0), (1, 0, 1))
KICK_OF = {kick: index for index, kick in enumerate(KICKS)}
LINK, KICK = 7, 4


def placed(*entries):
    offsets, total = {}, 0
    for entry in entries:
        offsets[entry] = total
        total += LINK if len(entry) == 2 else KICK
    return offsets, total


FIRST, FIRST_PAIRS = placed(
    (0, 0), (0, 0, 0), (3, 0), (2, 0), (1, 0), (1, 1), (2, 1), (3, 1)
)
FROZEN = {(3, 0): (3, 2), (2, 0): (2, 2), (1, 0): (1, 2)}
SECOND, SECOND_PAIRS = placed((3, 2), (2, 2), (1, 2), (0, 1), (0, 0, 1), (0, 1, 1))
LATE, LATE_PAIRS = placed((0, 2, 1), (0, 3, 1), (1, 0, 0), (1, 0, 1))
TURN, TURN_PAIRS = placed((0, 0), (0, 1), (1, 1))
TURN2, TURN2_PAIRS = placed((1, 1), (2, 1), (3, 1))
FIRST_ROWS = {
    (0, 0): (2, 3, 1, 1, 2, 2),
    (0, 0, 0): (1, 2, 0, 0, 1, 1),
    (3, 0): (1, 2, 0, 0, 1, 1),
    (2, 0): (1, 2, 1, 0, 2, 1),
    (1, 0): (2, 2, 2, 2, 1, 1),
    (1, 1): (2, 2, 2, 2, 1, 1),
    (2, 1): (2, 2, 2, 2, 2, 2),
    (3, 1): (2, 2, 2, 2, 2, 2),
}
SECOND_ROWS = {
    (0, 1): (2, 3, 1, 1, 2, 2),
    (0, 0, 1): (1, 2, 0, 0, 1, 1),
    (0, 1, 1): (2, 1, 2, 2, 1, 1),
}
LATE_ROWS = {
    (0, 2, 1): (1, 1, 1, 0, 1, 0),
    (0, 3, 1): (1, 1, 0, 0, 0, 0),
    (1, 0, 0): (1, 1, 0, 0, 0, 0),
    (1, 0, 1): (1, 1, 0, 0, 0, 0),
}
TURN_ROWS = {
    (0, 0): (2, 2, 2, 2, 2, 2),
    (0, 1): (2, 2, 2, 2, 2, 2),
    (1, 1): (2, 1, 2, 2, 1, 1),
}
TURN2_ROWS = {
    (1, 1): (2, 1, 1, 1, 0, 0),
    (2, 1): (1, 1, 1, 0, 1, 0),
    (3, 1): (2, 2, 1, 1, 1, 1),
}
FACES = tuple((dx, dy) for dx in (-1, 0, 1) for dy in (-1, 0, 1))
FACES = tuple(sorted(FACES, key=lambda face: -abs(face[0]) - abs(face[1])))
RING = tuple(face for face in FACES if face != (0, 0))


def runs(places, rows, face):
    dx, dy = face
    found = []
    for entry, needed in rows.items():
        if dx == 0:
            count = 3
        elif dy == 0:
            count = needed[0 if dx == 1 else 1]
        else:
            count = needed[(2 if dx == 1 else 4) + (0 if dy == 1 else 1)]
        if not count:
            continue
        low = places[entry]
        high = low + (LINK if len(entry) == 2 else KICK)
        if found and found[-1][1:] == (low, count):
            found[-1] = (found[-1][0], high, count)
        else:
            found.append((low, high, count))
    return found


def count_of(places, rows, faces):
    return sum(len(runs(places, rows, face)) for face in faces)


FROZEN_ROWS = {entry: FIRST_ROWS[entry] for entry in FROZEN}
COPIES = (
    count_of(FIRST, FIRST_ROWS, RING)
    + count_of(FIRST, FROZEN_ROWS, FACES)
    + count_of(SECOND, SECOND_ROWS, RING)
    + count_of(LATE, LATE_ROWS, RING)
    + sum(count_of(TURN, {entry: TURN_ROWS[entry]}, RING) for entry in TURN)
    + sum(count_of(TURN2, {entry: TURN2_ROWS[entry]}, RING) for entry in TURN2)
    + 7 * SWEEPS
)


def rows_sent(dx, count):
    if dx == 1:
        return pl.ds(5 - count, count), pl.ds(2 - count, count)
    if dx == -1:
        return pl.ds(2, count), pl.ds(5, count)
    return pl.ds(2, 3), pl.ds(2, 3)


def mm(a, b):
    real = imag = None
    for k in range(3):
        ar, ai = a[0][:, k][:, None], a[1][:, k][:, None]
        br, bi = b[0][k][None], b[1][k][None]
        re, im = ar * br - ai * bi, ar * bi + ai * br
        real, imag = (re, im) if real is None else (real + re, imag + im)
    return real, imag


def mm_nh(a, b):
    real = imag = None
    for k in range(3):
        ar, ai = a[0][:, k][:, None], a[1][:, k][:, None]
        br, bi = b[0][:, k][None], b[1][:, k][None]
        re, im = ar * br + ai * bi, ai * br - ar * bi
        real, imag = (re, im) if real is None else (real + re, imag + im)
    return real, imag


def mm_hn(a, b):
    real = imag = None
    for k in range(3):
        ar, ai = a[0][k][:, None], a[1][k][:, None]
        br, bi = b[0][k][None], b[1][k][None]
        re, im = ar * br + ai * bi, ar * bi - ai * br
        real, imag = (re, im) if real is None else (real + re, imag + im)
    return real, imag


def times(a, b):
    return a[0] * b[0] - a[1] * b[1], a[0] * b[1] + a[1] * b[0]


def conj_times(a, b):
    return a[0] * b[0] + a[1] * b[1], a[0] * b[1] - a[1] * b[0]


def add(a, b):
    return a[0] + b[0], a[1] + b[1]


def cross(re, im):
    entry = [(re[k], im[k]) for k in range(6)]
    found = []
    for j in range(3):
        k, m = (j + 1) % 3, (j + 2) % 3
        one, two = times(entry[k], entry[3 + m]), times(entry[m], entry[3 + k])
        found.append((one[0] - two[0], one[1] - two[1]))
    return found


def compress(re, im):
    terms = [times((re[6 + j], im[6 + j]), value) for j, value in enumerate(cross(re, im))]
    phase = add(add(terms[0], terms[1]), terms[2])
    return (
        jnp.concatenate([re[0:6], phase[0][None]], axis=0),
        jnp.concatenate([im[0:6], phase[1][None]], axis=0),
    )


def restore(re, im):
    third = [conj_times(value, (re[6], im[6])) for value in cross(re, im)]
    return (
        jnp.concatenate([re[0:6], jnp.stack([value[0] for value in third])], axis=0),
        jnp.concatenate([im[0:6], jnp.stack([value[1] for value in third])], axis=0),
    )


def cayley(product, noise, link):
    mr, mi = product
    n = noise
    drift = 0.25 * step_drift
    kick = 0.25 * step_noise

    def off(i, j, nr, ni):
        return (
            kick * nr - drift * (mr[i, j] - mr[j, i]),
            kick * ni - drift * (mi[i, j] + mi[j, i]),
        )

    p = off(0, 1, n[1], n[0])
    q = off(0, 2, n[4], n[3])
    r = off(1, 2, n[6], n[5])
    third = (mi[0, 0] + mi[1, 1] + mi[2, 2]) / 3.0
    eighth = root_third * n[7]
    a = kick * (eighth + n[2]) - 2.0 * drift * (mi[0, 0] - third)
    b = kick * (eighth - n[2]) - 2.0 * drift * (mi[1, 1] - third)
    c = -(a + b)
    pp = p[0] * p[0] + p[1] * p[1]
    qq = q[0] * q[0] + q[1] * q[1]
    rr = r[0] * r[0] + r[1] * r[1]
    bc, ac, ab = b * c, a * c, a * b
    pr = times(p, r)
    real = 1.0 + (pp + qq + rr) - (ab + ac + bc)
    odd = a * rr + b * qq + c * pp - a * bc - 2.0 * (pr[1] * q[0] - pr[0] * q[1])
    weight = 2.0 / (real * real + odd * odd)
    inv = (real * weight, odd * weight)
    rs = conj_times(r, q)
    ps = conj_times(p, q)
    s01 = (c * p[1] - rs[0], -c * p[0] - rs[1])
    s02 = (b * q[1] + pr[0], pr[1] - b * q[0])
    s12 = (a * r[1] - ps[0], -a * r[0] - ps[1])
    adj = [
        [(1.0 + rr - bc, a), add(s01, p), add(s02, q)],
        [(s01[0] - p[0], p[1] - s01[1]), (1.0 + qq - ac, b), add(s12, r)],
        [(s02[0] - q[0], q[1] - s02[1]), (s12[0] - r[0], r[1] - s12[1]), (1.0 + pp - ab, c)],
    ]
    rotation = [[times(entry, inv) for entry in row] for row in adj]
    for i in range(3):
        rotation[i][i] = (rotation[i][i][0] - 1.0, rotation[i][i][1])
    stacked = tuple(
        jnp.stack([jnp.stack([entry[part] for entry in row]) for row in rotation])
        for part in range(2)
    )
    return mm(stacked, link)


def kernel(
    links_hbm, kicks_hbm, separations_hbm, out,
    links, kicks, separations, fetch_sem, first_set, second_set, late_set, turn_set, turn2_set,
    win, kwin, held, lines, send_sem, recv_sem,
):
    slabs, sxs, syzs = (lax.axis_size(axis) for axis in ("slab", "sx", "syz"))
    slab, sx, syz = (lax.axis_index(axis) for axis in ("slab", "sx", "syz"))

    def peer(ds, dx, dy):
        return (
            lax.rem(slab + ds + slabs, slabs),
            lax.rem(sx + dx + sxs, sxs),
            lax.rem(syz + dy + syzs, syzs),
        )

    peers = [(ds, *face) for ds in (-1, 1) for face in FACES]
    peers += [(2, dx, 0) for dx in (-1, 0, 1)] + [(0, *face) for face in RING]
    peers.sort(key=lambda one: -sum(map(abs, one)))
    barrier = pltpu.get_barrier_semaphore()
    for one in peers:
        pl.semaphore_signal(barrier, inc=1, device_id=peer(*one), device_id_type=MESH)

    fetches = [
        pltpu.make_async_copy(links_hbm, links, fetch_sem.at[0]),
        pltpu.make_async_copy(kicks_hbm, kicks, fetch_sem.at[1]),
        pltpu.make_async_copy(separations_hbm, separations, fetch_sem.at[2]),
    ]
    for fetch in fetches:
        fetch.start()
    started = []

    def send(src, dst, target):
        index = len(started)
        copy = pltpu.make_async_remote_copy(
            src_ref=src,
            dst_ref=dst,
            send_sem=send_sem.at[index],
            recv_sem=recv_sem.at[index],
            device_id=peer(*target),
            device_id_type=MESH,
        )
        copy.start()
        started.append(copy)
        return copy

    shape = (8, 128)
    lane = lax.broadcasted_iota(jnp.int32, shape, 1)
    row = lax.broadcasted_iota(jnp.int32, shape, 0)
    half = lane % 16
    quarter = lane // 32
    low_half = lane < 64
    middle = jnp.logical_and(lane >= 32, lane < 96)
    first_of_half = (lane % 64) < 32
    odd_site = (sx * 3 + row + lane // 16) % 2
    is_odd = [odd_site == 1, odd_site == 0]
    last_half, first_half = half == 15, half == 0

    def own_index(time):
        lane3 = lax.broadcasted_iota(jnp.int32, (3, 128), 1)
        row3 = lax.broadcasted_iota(jnp.int32, (3, 128), 0)
        y = (lane3 % 64) // 16
        bit = (time + sx * 3 + row3 + y + lane3 // 64) % 2
        return y * 32 + (lane3 % 16) * 2 + bit

    own_gather = [own_index(0), own_index(1)]

    first3 = first_of_half[0:3]

    def put(bufs, pair, first, second):
        x_buf, p_buf, m_buf = bufs[:3]
        count = first.shape[0]
        rolled = pltpu.roll(first, 96, 2)
        x_buf[2 * pair : 2 * pair + count, OWN] = first
        x_buf[2 * pair + count : 2 * pair + 2 * count, OWN] = second
        p_buf[pair : pair + count, OWN] = jnp.where(first3, rolled, second)
        m_buf[pair : pair + count, OWN] = jnp.where(first3, second, rolled)

    def spread(bufs, places, rows, ds=0, goal=None, shift=0):
        goal = bufs if goal is None else goal
        copies = []
        for face in RING if ds == 0 else FACES:
            for low, high, count in runs(places, rows, face):
                dx, dy = face
                out_rows, in_rows = rows_sent(dx, count)
                to = low + shift
                if dy == 0:
                    src, dst = bufs[0], goal[0]
                    low, high, to = 2 * low, 2 * high, 2 * to
                else:
                    src, dst = (bufs[1], goal[3]) if dy == 1 else (bufs[2], goal[4])
                copies.append(
                    send(
                        src.at[pl.ds(low, high - low), out_rows],
                        dst.at[pl.ds(to, high - low), in_rows],
                        (ds, dx, dy),
                    )
                )
        return copies

    def assemble(bufs, pair, count):
        x_buf, _, _, lo_buf, hi_buf = bufs
        lo, hi = lo_buf[pair : pair + count], hi_buf[pair : pair + count]
        found = [[None, None], [None, None]]
        for member in range(2):
            start = 2 * pair + member * count
            own = x_buf[start : start + count]
            for parity in range(2):
                q = 2 * parity + member
                edge = jnp.where(quarter == q, lo, hi)
                if q:
                    edge = pltpu.roll(edge, 128 - 32 * q, 2)
                centre = pltpu.roll(own, 32 if parity == 0 else 96, 2)
                found[parity][member] = jnp.where(middle, centre, edge)
        return found

    def take_in(bufs, places, entries):
        for entry in entries:
            if len(entry) == 2:
                found = assemble(bufs, places[entry], LINK)
                for parity in range(2):
                    for part, value in enumerate(restore(*found[parity])):
                        win[FIELD_OF[entry], parity, part] = value
            else:
                found = assemble(bufs, places[entry], KICK)
                for parity in range(2):
                    for member in range(2):
                        kwin[KICK_OF[entry], parity, 4 * member : 4 * member + 4] = found[parity][member]

    def packed(parts, time):
        return jnp.stack([jnp.take_along_axis(part, own_gather[time], axis=1) for part in parts])

    def pack(bufs, places, entries):
        for entry in entries:
            if len(entry) == 2:
                direction, time = entry
                whole = [
                    packed(
                        [links[direction, part, i, j, :, time] for i in range(3) for j in range(3)], time
                    )
                    for part in range(2)
                ]
                put(bufs, places[entry], *compress(*whole))
            else:
                sweep, direction, time = entry
                parts = [kicks[sweep, direction, a, :, time].astype(jnp.float32) for a in range(8)]
                put(bufs, places[entry], packed(parts[:4], time), packed(parts[4:], time))

    def wait(copies):
        for copy in copies:
            copy.wait_recv()

    for fetch in fetches:
        fetch.wait()
    pack(first_set, FIRST, FIRST)
    pl.semaphore_wait(barrier, len(peers))

    first_copies = spread(first_set, FIRST, FIRST_ROWS)
    second_copies = spread(first_set, FIRST, FROZEN_ROWS, -1, second_set, SECOND[3, 2] - FIRST[3, 0])
    pack(second_set, SECOND, SECOND_ROWS)
    second_copies += spread(second_set, SECOND, SECOND_ROWS)
    pack(late_set, LATE, LATE)
    late_copies = spread(late_set, LATE, LATE_ROWS)

    def shifted(pair, axis, sign, time, parity):
        def one(value):
            if axis == 0:
                return value
            flat = value.reshape(9, 8, 128)
            if axis == 1:
                flat = pltpu.roll(flat, 7 if sign == 1 else 1, 1)
            elif axis == 2:
                flat = pltpu.roll(flat, 112 if sign == 1 else 16, 2)
            else:
                odd = is_odd[(time + parity) % 2]
                if sign == 1:
                    inner = jnp.where(last_half, pltpu.roll(flat, 15, 2), pltpu.roll(flat, 127, 2))
                    flat = jnp.where(odd, inner, flat)
                else:
                    inner = jnp.where(first_half, pltpu.roll(flat, 113, 2), pltpu.roll(flat, 1, 2))
                    flat = jnp.where(odd, flat, inner)
            return flat.reshape(3, 3, 8, 128)

        return one(pair[0]), one(pair[1])

    def link(direction, time, parity):
        field = FIELD_OF[direction, time]
        return tuple(win[field, parity, part].reshape(3, 3, 8, 128) for part in range(2))

    def staples(mu, time, parity, planes):
        total = None
        other = 1 - parity
        for nu in planes:
            if mu == 0:
                ahead = link(nu, time + 1, other)
                ahead_low = link(nu, time + 1, parity)
            else:
                ahead = shifted(link(nu, time, other), mu, 1, time, parity)
            if nu == 0:
                above, below = link(mu, time + 1, other), link(mu, time - 1, other)
                low_time = time - 1
            else:
                above = shifted(link(mu, time, other), nu, 1, time, parity)
                below = link(mu, time, other)
                low_time = time
            if mu != 0:
                ahead_low = shifted(
                    link(nu, low_time, parity), mu, 1, low_time, other
                )
            upper = mm_nh(mm_nh(ahead, above), link(nu, time, parity))
            lower = mm_hn(mm(below, ahead_low), link(nu, low_time, other))
            lower = shifted(lower, nu, -1, time, parity)
            both = add(upper, lower)
            total = both if total is None else add(total, both)
        return total

    def ahead_of(slot, mu, time, parity, planes):
        for part, value in enumerate(staples(mu, time, parity, planes)):
            held[slot, part] = value

    def substep(sweep, mu, parity, time=1, slot=None, done=()):
        current = link(mu, time, parity)
        noise = kwin[KICK_OF[sweep, mu, time], parity]
        planes = [nu for nu in range(4) if nu != mu and nu not in done]
        total = staples(mu, time, parity, planes)
        if done:
            total = add(total, (held[slot, 0], held[slot, 1]))
        new = cayley(mm(current, total), noise, current)
        field = FIELD_OF[mu, time]
        for part in range(2):
            win[field, parity, part] = new[part].reshape(9, 8, 128)

    def own_part(two):
        return jnp.where(low_half, pltpu.roll(two[0], 96, 2), pltpu.roll(two[1], 32, 2))

    def pass_on(bufs, places, rows, entry):
        whole = [
            own_part([win[FIELD_OF[entry], parity, part] for parity in range(2)])[:, OWN]
            for part in range(2)
        ]
        put(bufs, places[entry], *compress(*whole))
        return spread(bufs, places, {entry: rows[entry]})

    def measure(sweep):
        products = [mm(link(0, 0, parity), link(0, 1, 1 - parity)) for parity in range(2)]
        whole = [
            own_part([product[part].reshape(9, 8, 128) for product in products])[:, OWN]
            for part in range(2)
        ]
        for part, value in enumerate(compress(*whole)):
            lines[sweep, 0, LINK * part : LINK * part + LINK, 0:3] = value
        copies = []
        src = lines.at[sweep, 0, :, pl.ds(0, 3)]
        for ds in (2, 1, 3, 0):
            copies.append(send(src, lines.at[sweep, ds, :, pl.ds(3, 3)], (-ds, -1, 0)))
        for ds in (2, 1, 3):
            copies.append(send(src, lines.at[sweep, ds, :, pl.ds(0, 3)], (-ds, 0, 0)))
        return copies

    wait(first_copies)
    take_in(first_set, FIRST, FIRST)
    substep(0, 0, 0, 0)
    substep(0, 0, 1, 0)
    turn_first = pass_on(turn_set, TURN, TURN_ROWS, (0, 0))
    wait(second_copies)
    take_in(second_set, SECOND, SECOND)
    substep(0, 0, 0, 1)
    substep(0, 0, 1, 1)
    turn_first += pass_on(turn_set, TURN, TURN_ROWS, (0, 1))
    substep(0, 1, 0)
    turn_last = pass_on(turn_set, TURN, TURN_ROWS, (1, 1))
    line_copies = measure(0)
    ahead_of(0, 2, 1, 0, (3,))
    wait(late_copies)
    take_in(late_set, LATE, LATE)
    wait(turn_first)
    take_in(turn_set, TURN, ((0, 0), (0, 1)))
    ahead_of(1, 1, 1, 1, (0,))
    ahead_of(2, 2, 1, 1, (0,))
    ahead_of(3, 3, 1, 0, (0,))
    wait(turn_last)
    take_in(turn_set, TURN, ((1, 1),))
    substep(0, 1, 1, 1, 1, (0,))
    turn_first = pass_on(turn2_set, TURN2, TURN2_ROWS, (1, 1))
    substep(0, 2, 0, 1, 0, (3,))
    substep(0, 2, 1, 1, 2, (0,))
    turn_first += pass_on(turn2_set, TURN2, TURN2_ROWS, (2, 1))
    substep(0, 3, 0, 1, 3, (0,))
    turn_last = pass_on(turn2_set, TURN2, TURN2_ROWS, (3, 1))
    ahead_of(0, 3, 1, 1, (0,))
    wait(turn_first)
    take_in(turn2_set, TURN2, ((1, 1), (2, 1)))
    ahead_of(1, 0, 0, 0, (1, 2))
    ahead_of(2, 0, 1, 0, (1, 2))
    wait(turn_last)
    take_in(turn2_set, TURN2, ((3, 1),))
    substep(0, 3, 1, 1, 0, (0,))
    for time in range(2):
        substep(1, 0, 0, time, 1 + time, (1, 2))
        substep(1, 0, 1, time)
    line_copies += measure(1)
    wait(line_copies)

    def line(sweep, ds):
        whole = restore(lines[sweep, ds, 0:LINK], lines[sweep, ds, LINK : 2 * LINK])
        return tuple(part.reshape(3, 3, 8, 128) for part in whole)

    line_of = [[line(m, ds) for ds in range(4)] for m in range(SWEEPS)]
    low = [mm(line_of[m][0], line_of[n][1]) for m in range(SWEEPS) for n in range(SWEEPS)]
    high = [mm(line_of[m][2], line_of[n][3]) for m in range(SWEEPS) for n in range(SWEEPS)]
    loops = []
    for left in low:
        for right in high:
            rr, ri = (jnp.swapaxes(part, 0, 1) for part in right)
            loops.append(jnp.sum((left[0] * rr - left[1] * ri).reshape(9, 8, 128), axis=0))
            loops.append(jnp.sum((left[0] * ri + left[1] * rr).reshape(9, 8, 128), axis=0))
    loops = jnp.stack(loops)
    distance = separations[slab]
    result = None
    for r in (3, 2, 1):
        far = pltpu.roll(loops, 8 - r, 1)
        if r % 2:
            far = pltpu.roll(far, 64, 2)
        value = jnp.sum(loops * far, axis=0)
        result = value if result is None else jnp.where(distance == r, value, result)
    lane3 = lax.broadcasted_iota(jnp.int32, (3, 128), 1)
    row3 = lax.broadcasted_iota(jnp.int32, (3, 128), 0)
    y, z = lane3 // 32, lane3 % 32
    index = ((z + y + row3 + sx * 3) % 2) * 64 + y * 16 + z // 2
    out[:, 0] = jnp.take_along_axis(result[0:3], index, axis=1)

    for copy in started:
        copy.wait_send()


def local(gauge_links, langevin_noise, separations):
    def buffers(pairs):
        halves = tuple(pltpu.VMEM((pairs, 8, 128), jnp.float32) for _ in range(4))
        return (pltpu.VMEM((2 * pairs, 8, 128), jnp.float32), *halves)

    sets = (FIRST_PAIRS, SECOND_PAIRS, LATE_PAIRS, TURN_PAIRS, TURN2_PAIRS)
    vmem = pl.BlockSpec(memory_space=pltpu.VMEM)
    links = jnp.swapaxes(gauge_links, 4, 5)
    kicks = jnp.swapaxes(langevin_noise, 3, 4)
    correlator = pl.pallas_call(
        kernel,
        out_shape=jax.ShapeDtypeStruct((3, 1, 128), jnp.float32),
        in_specs=[
            pl.BlockSpec(memory_space=pltpu.HBM),
            pl.BlockSpec(memory_space=pltpu.HBM),
            pl.BlockSpec(memory_space=pltpu.HBM),
        ],
        out_specs=vmem,
        scratch_shapes=[
            pltpu.VMEM(links.shape, jnp.float32),
            pltpu.VMEM(kicks.shape, kicks.dtype),
            pltpu.SMEM(separations.shape, jnp.int32),
            pltpu.SemaphoreType.DMA((3,)),
        ]
        + [buffers(pairs) for pairs in sets] + [
            pltpu.VMEM((len(FIELDS), 2, 2, 9, 8, 128), jnp.float32),
            pltpu.VMEM((len(KICKS), 2, 8, 8, 128), jnp.float32),
            pltpu.VMEM((4, 2, 3, 3, 8, 128), jnp.float32),
            pltpu.VMEM((SWEEPS, 4, 2 * LINK, 8, 128), jnp.float32),
            pltpu.SemaphoreType.DMA((COPIES,)),
            pltpu.SemaphoreType.DMA((COPIES,)),
        ],
        compiler_params=pltpu.CompilerParams(
            collective_id=0, has_side_effects=True, vmem_limit_bytes=VMEM_LIMIT
        ),
    )(links, kicks, separations)
    return jnp.swapaxes(correlator, 0, 1) * (1.0 / SWEEPS**4)


def solution(mesh):
    return jax.shard_map(
        local,
        mesh=mesh,
        in_specs=(
            P(None, None, None, None, "slab", "sx", "syz"),
            P(None, None, None, "slab", "sx", "syz"),
            P(),
        ),
        out_specs=P("slab", "sx", "syz"),
        check_vma=False,
    )
```

```python
import jax
import jax.numpy as jnp
from jax import lax
from jax.experimental import pallas as pl
from jax.experimental.pallas import tpu as pltpu
from jax.sharding import PartitionSpec as P

SITES_ALONG_Z = 32
SWEEPS = 2

step_drift = 0.2
step_noise = 0.4
root_third = 0.5773502691896258

MESH = pl.DeviceIdType.MESH
VMEM_LIMIT = 60 * 1024 * 1024

OWN = slice(2, 5)
FIELDS = ((0, 0), (0, 1), (1, 1), (2, 1), (3, 1), (1, 0), (2, 0), (3, 0), (1, 2), (2, 2), (3, 2))
FIELD_OF = {field: index for index, field in enumerate(FIELDS)}
KICKS = ((0, 0, 0), (0, 0, 1), (0, 1, 1), (0, 2, 1), (0, 3, 1), (1, 0, 0), (1, 0, 1))
KICK_OF = {kick: index for index, kick in enumerate(KICKS)}
LINK, KICK = 7, 4


def size(entry):
    return LINK if len(entry) == 2 else KICK


def placed(*groups):
    places, x_end, y_end = {}, 0, 0
    for group in groups:
        members = group if isinstance(group[0], tuple) else (group,)
        for half, entry in enumerate(members):
            places[entry] = (x_end, y_end, half)
            x_end += size(entry)
        y_end += size(members[0])
    return places, (x_end, y_end)


FIRST_GROUPS = ((0, 0), (0, 0, 0), (2, 0), ((3, 0), (1, 0)), ((1, 1), (3, 1)), (2, 1))
FROZEN_GROUPS = ((2, 2), ((3, 2), (1, 2)))
SECOND_GROUPS = ((0, 1), ((0, 0, 1), (0, 1, 1)))
LATE_GROUPS = (((0, 2, 1), (0, 3, 1)), ((1, 0, 0), (1, 0, 1)))
FIRST, FIRST_PAIRS = placed(*FIRST_GROUPS)
SECOND, SECOND_PAIRS = placed(*FROZEN_GROUPS, *SECOND_GROUPS)
LATE, LATE_PAIRS = placed(*LATE_GROUPS)
TURN, TURN_PAIRS = placed((0, 0), (0, 1), (1, 1))
TURN2, TURN2_PAIRS = placed((1, 1), (2, 1), (3, 1))
FIRST_ROWS = {
    (0, 0): (2, 2, 1, 1, 1, 1),
    (0, 0, 0): (1, 1, 0, 0, 1, 1),
    (2, 0): (1, 1, 1, 0, 1, 1),
    (3, 0): (1, 1, 0, 0, 1, 1),
    (1, 0): (2, 1, 2, 2, 1, 1),
    (1, 1): (2, 2, 1, 1, 1, 1),
    (3, 1): (2, 2, 2, 2, 2, 2),
    (2, 1): (2, 2, 2, 2, 2, 2),
}
FROZEN_ROWS = {
    (2, 0): (1, 2, 1, 0, 2, 1),
    (3, 0): (1, 2, 0, 0, 1, 1),
    (1, 0): (2, 2, 2, 2, 1, 1),
}
SECOND_ROWS = {
    (0, 1): (2, 3, 1, 1, 2, 2),
    (0, 0, 1): (1, 2, 0, 0, 1, 1),
    (0, 1, 1): (2, 1, 2, 2, 1, 1),
}
LATE_ROWS = {
    (0, 2, 1): (1, 1, 1, 0, 1, 0),
    (0, 3, 1): (1, 1, 0, 0, 0, 0),
    (1, 0, 0): (1, 1, 0, 0, 0, 0),
    (1, 0, 1): (1, 1, 0, 0, 0, 0),
}
TURN_ROWS = {
    (0, 0): (2, 2, 2, 2, 2, 2),
    (0, 1): (2, 2, 2, 2, 2, 2),
    (1, 1): (2, 1, 2, 2, 1, 1),
}
TURN2_ROWS = {
    (1, 1): (2, 1, 1, 1, 0, 0),
    (2, 1): (1, 1, 1, 0, 1, 0),
    (3, 1): (2, 2, 1, 1, 1, 1),
}
FACES = tuple((dx, dy) for dx in (-1, 0, 1) for dy in (-1, 0, 1))
FACES = tuple(sorted(FACES, key=lambda face: -abs(face[0]) - abs(face[1])))
RING = tuple(face for face in FACES if face != (0, 0))


def runs(places, rows, face):
    dx, dy = face
    found = {}
    for entry, needed in rows.items():
        if dx == 0:
            count = 3
        elif dy == 0:
            count = needed[0 if dx == 1 else 1]
        else:
            count = needed[(2 if dx == 1 else 4) + (0 if dy == 1 else 1)]
        low = places[entry][0 if dy == 0 else 1]
        high = low + size(entry)
        found[low] = (high, max(count, found.get(low, (0, 0))[1]))
    merged = []
    for low, (high, count) in sorted(found.items()):
        if not count:
            continue
        if merged and merged[-1][1:] == (low, count):
            merged[-1] = (merged[-1][0], high, count)
        else:
            merged.append((low, high, count))
    return merged


def count_of(places, rows, faces):
    return sum(len(runs(places, rows, face)) for face in faces)


COPIES = (
    count_of(FIRST, FIRST_ROWS, RING)
    + count_of(FIRST, FROZEN_ROWS, FACES)
    + count_of(SECOND, SECOND_ROWS, RING)
    + count_of(LATE, LATE_ROWS, RING)
    + sum(count_of(TURN, {entry: TURN_ROWS[entry]}, RING) for entry in TURN)
    + sum(count_of(TURN2, {entry: TURN2_ROWS[entry]}, RING) for entry in TURN2)
    + 7 * SWEEPS
)


def rows_sent(dx, count):
    if dx == 1:
        return pl.ds(5 - count, count), pl.ds(2 - count, count)
    if dx == -1:
        return pl.ds(2, count), pl.ds(5, count)
    return pl.ds(2, 3), pl.ds(2, 3)


def mm(a, b):
    real = imag = None
    for k in range(3):
        ar, ai = a[0][:, k][:, None], a[1][:, k][:, None]
        br, bi = b[0][k][None], b[1][k][None]
        re, im = ar * br - ai * bi, ar * bi + ai * br
        real, imag = (re, im) if real is None else (real + re, imag + im)
    return real, imag


def mm_nh(a, b):
    real = imag = None
    for k in range(3):
        ar, ai = a[0][:, k][:, None], a[1][:, k][:, None]
        br, bi = b[0][:, k][None], b[1][:, k][None]
        re, im = ar * br + ai * bi, ai * br - ar * bi
        real, imag = (re, im) if real is None else (real + re, imag + im)
    return real, imag


def mm_hn(a, b):
    real = imag = None
    for k in range(3):
        ar, ai = a[0][k][:, None], a[1][k][:, None]
        br, bi = b[0][k][None], b[1][k][None]
        re, im = ar * br + ai * bi, ar * bi - ai * br
        real, imag = (re, im) if real is None else (real + re, imag + im)
    return real, imag


def times(a, b):
    return a[0] * b[0] - a[1] * b[1], a[0] * b[1] + a[1] * b[0]


def conj_times(a, b):
    return a[0] * b[0] + a[1] * b[1], a[0] * b[1] - a[1] * b[0]


def add(a, b):
    return a[0] + b[0], a[1] + b[1]


def cross(re, im):
    entry = [(re[k], im[k]) for k in range(6)]
    found = []
    for j in range(3):
        k, m = (j + 1) % 3, (j + 2) % 3
        one, two = times(entry[k], entry[3 + m]), times(entry[m], entry[3 + k])
        found.append((one[0] - two[0], one[1] - two[1]))
    return found


def compress(re, im):
    terms = [times((re[6 + j], im[6 + j]), value) for j, value in enumerate(cross(re, im))]
    phase = add(add(terms[0], terms[1]), terms[2])
    return (
        jnp.concatenate([re[0:6], phase[0][None]], axis=0),
        jnp.concatenate([im[0:6], phase[1][None]], axis=0),
    )


def restore(re, im):
    third = [conj_times(value, (re[6], im[6])) for value in cross(re, im)]
    return (
        jnp.concatenate([re[0:6], jnp.stack([value[0] for value in third])], axis=0),
        jnp.concatenate([im[0:6], jnp.stack([value[1] for value in third])], axis=0),
    )


def cayley(product, noise, link):
    mr, mi = product
    n = noise
    drift = 0.25 * step_drift
    kick = 0.25 * step_noise

    def off(i, j, nr, ni):
        return (
            kick * nr - drift * (mr[i, j] - mr[j, i]),
            kick * ni - drift * (mi[i, j] + mi[j, i]),
        )

    p = off(0, 1, n[1], n[0])
    q = off(0, 2, n[4], n[3])
    r = off(1, 2, n[6], n[5])
    third = (mi[0, 0] + mi[1, 1] + mi[2, 2]) / 3.0
    eighth = root_third * n[7]
    a = kick * (eighth + n[2]) - 2.0 * drift * (mi[0, 0] - third)
    b = kick * (eighth - n[2]) - 2.0 * drift * (mi[1, 1] - third)
    c = -(a + b)
    pp = p[0] * p[0] + p[1] * p[1]
    qq = q[0] * q[0] + q[1] * q[1]
    rr = r[0] * r[0] + r[1] * r[1]
    bc, ac, ab = b * c, a * c, a * b
    pr = times(p, r)
    real = 1.0 + (pp + qq + rr) - (ab + ac + bc)
    odd = a * rr + b * qq + c * pp - a * bc - 2.0 * (pr[1] * q[0] - pr[0] * q[1])
    weight = 2.0 / (real * real + odd * odd)
    inv = (real * weight, odd * weight)
    rs = conj_times(r, q)
    ps = conj_times(p, q)
    s01 = (c * p[1] - rs[0], -c * p[0] - rs[1])
    s02 = (b * q[1] + pr[0], pr[1] - b * q[0])
    s12 = (a * r[1] - ps[0], -a * r[0] - ps[1])
    adj = [
        [(1.0 + rr - bc, a), add(s01, p), add(s02, q)],
        [(s01[0] - p[0], p[1] - s01[1]), (1.0 + qq - ac, b), add(s12, r)],
        [(s02[0] - q[0], q[1] - s02[1]), (s12[0] - r[0], r[1] - s12[1]), (1.0 + pp - ab, c)],
    ]
    rotation = [[times(entry, inv) for entry in row] for row in adj]
    for i in range(3):
        rotation[i][i] = (rotation[i][i][0] - 1.0, rotation[i][i][1])
    stacked = tuple(
        jnp.stack([jnp.stack([entry[part] for entry in row]) for row in rotation])
        for part in range(2)
    )
    return mm(stacked, link)


def kernel(
    links_hbm, kicks_hbm, separations_hbm, out,
    links, kicks, separations, fetch_sem, first_set, second_set, late_set, turn_set, turn2_set,
    win, kwin, held, lines, send_sem, recv_sem,
):
    slabs, sxs, syzs = (lax.axis_size(axis) for axis in ("slab", "sx", "syz"))
    slab, sx, syz = (lax.axis_index(axis) for axis in ("slab", "sx", "syz"))

    def peer(ds, dx, dy):
        return (
            lax.rem(slab + ds + slabs, slabs),
            lax.rem(sx + dx + sxs, sxs),
            lax.rem(syz + dy + syzs, syzs),
        )

    peers = [(ds, *face) for ds in (-1, 1) for face in FACES]
    peers += [(2, dx, 0) for dx in (-1, 0, 1)] + [(0, *face) for face in RING]
    peers.sort(key=lambda one: -sum(map(abs, one)))
    barrier = pltpu.get_barrier_semaphore()
    for one in peers:
        pl.semaphore_signal(barrier, inc=1, device_id=peer(*one), device_id_type=MESH)

    fetches = [
        pltpu.make_async_copy(links_hbm, links, fetch_sem.at[0]),
        pltpu.make_async_copy(kicks_hbm, kicks, fetch_sem.at[1]),
        pltpu.make_async_copy(separations_hbm, separations, fetch_sem.at[2]),
    ]
    for fetch in fetches:
        fetch.start()
    started = []

    def send(src, dst, target):
        index = len(started)
        copy = pltpu.make_async_remote_copy(
            src_ref=src,
            dst_ref=dst,
            send_sem=send_sem.at[index],
            recv_sem=recv_sem.at[index],
            device_id=peer(*target),
            device_id_type=MESH,
        )
        copy.start()
        started.append(copy)
        return copy

    shape = (8, 128)
    lane = lax.broadcasted_iota(jnp.int32, shape, 1)
    row = lax.broadcasted_iota(jnp.int32, shape, 0)
    half = lane % 16
    quarter = lane // 32
    low_half = lane < 64
    middle = jnp.logical_and(lane >= 32, lane < 96)
    first_of_half = (lane % 64) < 32
    odd_site = (sx * 3 + row + lane // 16) % 2
    is_odd = [odd_site == 1, odd_site == 0]
    last_half, first_half = half == 15, half == 0

    def own_index(time):
        lane3 = lax.broadcasted_iota(jnp.int32, (3, 128), 1)
        row3 = lax.broadcasted_iota(jnp.int32, (3, 128), 0)
        y = (lane3 % 64) // 16
        bit = (time + sx * 3 + row3 + y + lane3 // 64) % 2
        return y * 32 + (lane3 % 16) * 2 + bit

    own_gather = [own_index(0), own_index(1)]

    first3 = first_of_half[0:3]
    second3 = (lane[0:3] % 32) >= 16

    def put(bufs, places, *entries):
        x_buf, p_buf, m_buf = bufs[:3]
        upper, lower = [], []
        for entry, first, second in entries:
            x, y, _ = places[entry]
            count = size(entry)
            rolled = pltpu.roll(first, 96, 2)
            x_buf[2 * x : 2 * x + count, OWN] = first
            x_buf[2 * x + count : 2 * x + 2 * count, OWN] = second
            upper.append(jnp.where(first3, rolled, second))
            lower.append(jnp.where(first3, second, rolled))
        if len(entries) == 2:
            upper = [jnp.where(second3, upper[0], pltpu.roll(upper[1], 112, 2))]
            lower = [jnp.where(second3, pltpu.roll(lower[1], 16, 2), lower[0])]
        p_buf[y : y + count, OWN] = upper[0]
        m_buf[y : y + count, OWN] = lower[0]

    def spread(bufs, places, rows, ds=0, goal=None, shift=(0, 0)):
        goal = bufs if goal is None else goal
        copies = []
        for face in RING if ds == 0 else FACES:
            for low, high, count in runs(places, rows, face):
                dx, dy = face
                out_rows, in_rows = rows_sent(dx, count)
                to = low + shift[0 if dy == 0 else 1]
                if dy == 0:
                    src, dst = bufs[0], goal[0]
                    low, high, to = 2 * low, 2 * high, 2 * to
                else:
                    src, dst = (bufs[1], goal[3]) if dy == 1 else (bufs[2], goal[4])
                copies.append(
                    send(
                        src.at[pl.ds(low, high - low), out_rows],
                        dst.at[pl.ds(to, high - low), in_rows],
                        (ds, dx, dy),
                    )
                )
        return copies

    def assemble(bufs, place, count):
        x_buf, _, _, lo_buf, hi_buf = bufs
        x, y, second = place
        lo, hi = lo_buf[y : y + count], hi_buf[y : y + count]
        if second:
            lo, hi = pltpu.roll(lo, 16, 2), pltpu.roll(hi, 112, 2)
        found = [[None, None], [None, None]]
        for member in range(2):
            start = 2 * x + member * count
            own = x_buf[start : start + count]
            for parity in range(2):
                q = 2 * parity + member
                edge = jnp.where(quarter == q, lo, hi)
                if q:
                    edge = pltpu.roll(edge, 128 - 32 * q, 2)
                centre = pltpu.roll(own, 32 if parity == 0 else 96, 2)
                found[parity][member] = jnp.where(middle, centre, edge)
        return found

    def take_in(bufs, places, entries):
        for entry in entries:
            if len(entry) == 2:
                found = assemble(bufs, places[entry], LINK)
                for parity in range(2):
                    for part, value in enumerate(restore(*found[parity])):
                        win[FIELD_OF[entry], parity, part] = value
            else:
                found = assemble(bufs, places[entry], KICK)
                for parity in range(2):
                    for member in range(2):
                        kwin[KICK_OF[entry], parity, 4 * member : 4 * member + 4] = found[parity][member]

    def packed(parts, time):
        return jnp.stack([jnp.take_along_axis(part, own_gather[time], axis=1) for part in parts])

    def pack(bufs, places, groups):
        for group in groups:
            members = []
            for entry in group if isinstance(group[0], tuple) else (group,):
                if len(entry) == 2:
                    direction, time = entry
                    whole = [
                        packed(
                            [
                                links[direction, part, i, j, :, time]
                                for i in range(3)
                                for j in range(3)
                            ],
                            time,
                        )
                        for part in range(2)
                    ]
                    members.append((entry, *compress(*whole)))
                else:
                    sweep, direction, time = entry
                    parts = [
                        kicks[sweep, direction, a, :, time].astype(jnp.float32) for a in range(8)
                    ]
                    members.append((entry, packed(parts[:4], time), packed(parts[4:], time)))
            put(bufs, places, *members)

    def wait(copies):
        for copy in copies:
            copy.wait_recv()

    for fetch in fetches:
        fetch.wait()
    pack(first_set, FIRST, FIRST_GROUPS)
    pl.semaphore_wait(barrier, len(peers))

    first_copies = spread(first_set, FIRST, FIRST_ROWS)
    shift = tuple(SECOND[2, 2][k] - FIRST[2, 0][k] for k in range(2))
    second_copies = spread(first_set, FIRST, FROZEN_ROWS, -1, second_set, shift)
    pack(second_set, SECOND, SECOND_GROUPS)
    second_copies += spread(second_set, SECOND, SECOND_ROWS)
    pack(late_set, LATE, LATE_GROUPS)
    late_copies = spread(late_set, LATE, LATE_ROWS)

    def shifted(pair, axis, sign, time, parity):
        def one(value):
            if axis == 0:
                return value
            flat = value.reshape(9, 8, 128)
            if axis == 1:
                flat = pltpu.roll(flat, 7 if sign == 1 else 1, 1)
            elif axis == 2:
                flat = pltpu.roll(flat, 112 if sign == 1 else 16, 2)
            else:
                odd = is_odd[(time + parity) % 2]
                if sign == 1:
                    inner = jnp.where(last_half, pltpu.roll(flat, 15, 2), pltpu.roll(flat, 127, 2))
                    flat = jnp.where(odd, inner, flat)
                else:
                    inner = jnp.where(first_half, pltpu.roll(flat, 113, 2), pltpu.roll(flat, 1, 2))
                    flat = jnp.where(odd, flat, inner)
            return flat.reshape(3, 3, 8, 128)

        return one(pair[0]), one(pair[1])

    def link(direction, time, parity):
        field = FIELD_OF[direction, time]
        return tuple(win[field, parity, part].reshape(3, 3, 8, 128) for part in range(2))

    def staples(mu, time, parity, planes):
        total = None
        other = 1 - parity
        for nu in planes:
            if mu == 0:
                ahead = link(nu, time + 1, other)
                ahead_low = link(nu, time + 1, parity)
            else:
                ahead = shifted(link(nu, time, other), mu, 1, time, parity)
            if nu == 0:
                above, below = link(mu, time + 1, other), link(mu, time - 1, other)
                low_time = time - 1
            else:
                above = shifted(link(mu, time, other), nu, 1, time, parity)
                below = link(mu, time, other)
                low_time = time
            if mu != 0:
                ahead_low = shifted(
                    link(nu, low_time, parity), mu, 1, low_time, other
                )
            upper = mm_nh(mm_nh(ahead, above), link(nu, time, parity))
            lower = mm_hn(mm(below, ahead_low), link(nu, low_time, other))
            lower = shifted(lower, nu, -1, time, parity)
            both = add(upper, lower)
            total = both if total is None else add(total, both)
        return total

    def ahead_of(slot, mu, time, parity, planes):
        for part, value in enumerate(staples(mu, time, parity, planes)):
            held[slot, part] = value

    def substep(sweep, mu, parity, time=1, slot=None, done=()):
        current = link(mu, time, parity)
        noise = kwin[KICK_OF[sweep, mu, time], parity]
        planes = [nu for nu in range(4) if nu != mu and nu not in done]
        total = staples(mu, time, parity, planes)
        if done:
            total = add(total, (held[slot, 0], held[slot, 1]))
        new = cayley(mm(current, total), noise, current)
        field = FIELD_OF[mu, time]
        for part in range(2):
            win[field, parity, part] = new[part].reshape(9, 8, 128)

    def own_part(two):
        return jnp.where(low_half, pltpu.roll(two[0], 96, 2), pltpu.roll(two[1], 32, 2))

    def pass_on(bufs, places, rows, entry):
        whole = [
            own_part([win[FIELD_OF[entry], parity, part] for parity in range(2)])[:, OWN]
            for part in range(2)
        ]
        put(bufs, places, (entry, *compress(*whole)))
        return spread(bufs, places, {entry: rows[entry]})

    def measure(sweep):
        products = [mm(link(0, 0, parity), link(0, 1, 1 - parity)) for parity in range(2)]
        whole = [
            own_part([product[part].reshape(9, 8, 128) for product in products])[:, OWN]
            for part in range(2)
        ]
        for part, value in enumerate(compress(*whole)):
            lines[sweep, 0, LINK * part : LINK * part + LINK, 0:3] = value
        copies = []
        src = lines.at[sweep, 0, :, pl.ds(0, 3)]
        for ds in (2, 1, 3, 0):
            copies.append(send(src, lines.at[sweep, ds, :, pl.ds(3, 3)], (-ds, -1, 0)))
        for ds in (2, 1, 3):
            copies.append(send(src, lines.at[sweep, ds, :, pl.ds(0, 3)], (-ds, 0, 0)))
        return copies

    wait(first_copies)
    take_in(first_set, FIRST, FIRST)
    substep(0, 0, 0, 0)
    substep(0, 0, 1, 0)
    turn_first = pass_on(turn_set, TURN, TURN_ROWS, (0, 0))
    wait(second_copies)
    take_in(second_set, SECOND, SECOND)
    substep(0, 0, 0, 1)
    substep(0, 0, 1, 1)
    turn_first += pass_on(turn_set, TURN, TURN_ROWS, (0, 1))
    substep(0, 1, 0)
    turn_last = pass_on(turn_set, TURN, TURN_ROWS, (1, 1))
    line_copies = measure(0)
    ahead_of(0, 2, 1, 0, (3,))
    wait(late_copies)
    take_in(late_set, LATE, LATE)
    wait(turn_first)
    take_in(turn_set, TURN, ((0, 0), (0, 1)))
    ahead_of(1, 1, 1, 1, (0,))
    ahead_of(2, 2, 1, 1, (0,))
    ahead_of(3, 3, 1, 0, (0,))
    wait(turn_last)
    take_in(turn_set, TURN, ((1, 1),))
    substep(0, 1, 1, 1, 1, (0,))
    turn_first = pass_on(turn2_set, TURN2, TURN2_ROWS, (1, 1))
    substep(0, 2, 0, 1, 0, (3,))
    substep(0, 2, 1, 1, 2, (0,))
    turn_first += pass_on(turn2_set, TURN2, TURN2_ROWS, (2, 1))
    substep(0, 3, 0, 1, 3, (0,))
    turn_last = pass_on(turn2_set, TURN2, TURN2_ROWS, (3, 1))
    ahead_of(0, 3, 1, 1, (0,))
    wait(turn_first)
    take_in(turn2_set, TURN2, ((1, 1), (2, 1)))
    ahead_of(1, 0, 0, 0, (1, 2))
    ahead_of(2, 0, 1, 0, (1, 2))
    wait(turn_last)
    take_in(turn2_set, TURN2, ((3, 1),))
    substep(0, 3, 1, 1, 0, (0,))
    for time in range(2):
        substep(1, 0, 0, time, 1 + time, (1, 2))
        substep(1, 0, 1, time)
    line_copies += measure(1)
    wait(line_copies)

    def line(sweep, ds):
        whole = restore(lines[sweep, ds, 0:LINK], lines[sweep, ds, LINK : 2 * LINK])
        return tuple(part.reshape(3, 3, 8, 128) for part in whole)

    line_of = [[line(m, ds) for ds in range(4)] for m in range(SWEEPS)]
    low = [mm(line_of[m][0], line_of[n][1]) for m in range(SWEEPS) for n in range(SWEEPS)]
    high = [mm(line_of[m][2], line_of[n][3]) for m in range(SWEEPS) for n in range(SWEEPS)]
    loops = []
    for left in low:
        for right in high:
            rr, ri = (jnp.swapaxes(part, 0, 1) for part in right)
            loops.append(jnp.sum((left[0] * rr - left[1] * ri).reshape(9, 8, 128), axis=0))
            loops.append(jnp.sum((left[0] * ri + left[1] * rr).reshape(9, 8, 128), axis=0))
    loops = jnp.stack(loops)
    distance = separations[slab]
    result = None
    for r in (3, 2, 1):
        far = pltpu.roll(loops, 8 - r, 1)
        if r % 2:
            far = pltpu.roll(far, 64, 2)
        value = jnp.sum(loops * far, axis=0)
        result = value if result is None else jnp.where(distance == r, value, result)
    lane3 = lax.broadcasted_iota(jnp.int32, (3, 128), 1)
    row3 = lax.broadcasted_iota(jnp.int32, (3, 128), 0)
    y, z = lane3 // 32, lane3 % 32
    index = ((z + y + row3 + sx * 3) % 2) * 64 + y * 16 + z // 2
    out[:, 0] = jnp.take_along_axis(result[0:3], index, axis=1)

    for copy in started:
        copy.wait_send()


def local(gauge_links, langevin_noise, separations):
    def buffers(ends):
        halves = tuple(pltpu.VMEM((ends[1], 8, 128), jnp.float32) for _ in range(4))
        return (pltpu.VMEM((2 * ends[0], 8, 128), jnp.float32), *halves)

    sets = (FIRST_PAIRS, SECOND_PAIRS, LATE_PAIRS, TURN_PAIRS, TURN2_PAIRS)
    vmem = pl.BlockSpec(memory_space=pltpu.VMEM)
    links = jnp.swapaxes(gauge_links, 4, 5)
    kicks = jnp.swapaxes(langevin_noise, 3, 4)
    correlator = pl.pallas_call(
        kernel,
        out_shape=jax.ShapeDtypeStruct((3, 1, 128), jnp.float32),
        in_specs=[
            pl.BlockSpec(memory_space=pltpu.HBM),
            pl.BlockSpec(memory_space=pltpu.HBM),
            pl.BlockSpec(memory_space=pltpu.HBM),
        ],
        out_specs=vmem,
        scratch_shapes=[
            pltpu.VMEM(links.shape, jnp.float32),
            pltpu.VMEM(kicks.shape, kicks.dtype),
            pltpu.SMEM(separations.shape, jnp.int32),
            pltpu.SemaphoreType.DMA((3,)),
        ]
        + [buffers(pairs) for pairs in sets] + [
            pltpu.VMEM((len(FIELDS), 2, 2, 9, 8, 128), jnp.float32),
            pltpu.VMEM((len(KICKS), 2, 8, 8, 128), jnp.float32),
            pltpu.VMEM((4, 2, 3, 3, 8, 128), jnp.float32),
            pltpu.VMEM((SWEEPS, 4, 2 * LINK, 8, 128), jnp.float32),
            pltpu.SemaphoreType.DMA((COPIES,)),
            pltpu.SemaphoreType.DMA((COPIES,)),
        ],
        compiler_params=pltpu.CompilerParams(
            collective_id=0, has_side_effects=True, vmem_limit_bytes=VMEM_LIMIT
        ),
    )(links, kicks, separations)
    return jnp.swapaxes(correlator, 0, 1) * (1.0 / SWEEPS**4)


def solution(mesh):
    return jax.shard_map(
        local,
        mesh=mesh,
        in_specs=(
            P(None, None, None, None, "slab", "sx", "syz"),
            P(None, None, None, "slab", "sx", "syz"),
            P(),
        ),
        out_specs=P("slab", "sx", "syz"),
        check_vma=False,
    )
```

```python
from functools import partial

import jax
import jax.numpy as jnp
from jax import lax
from jax.experimental import pallas as pl
from jax.experimental.pallas import tpu as pltpu
from jax.sharding import PartitionSpec as P

SITES_ALONG_Z = 32
SWEEPS = 2

step_drift = 0.2
step_noise = 0.4
root_third = 0.5773502691896258

MESH = pl.DeviceIdType.MESH
VMEM_LIMIT = 60 * 1024 * 1024

OWN = slice(2, 5)
FIELDS = ((0, 0), (0, 1), (1, 1), (2, 1), (3, 1), (1, 0), (2, 0), (3, 0), (1, 2), (2, 2), (3, 2))
FIELD_OF = {field: index for index, field in enumerate(FIELDS)}
KICKS = ((0, 0, 0), (0, 0, 1), (0, 1, 1), (0, 2, 1), (0, 3, 1), (1, 0, 0), (1, 0, 1))
KICK_OF = {kick: index for index, kick in enumerate(KICKS)}
LINK, KICK = 7, 4


def size(entry):
    return LINK if len(entry) == 2 else KICK


def placed(*groups):
    places, x_end, y_end = {}, 0, 0
    for group in groups:
        members = group if isinstance(group[0], tuple) else (group,)
        for half, entry in enumerate(members):
            places[entry] = (x_end, y_end, half)
            x_end += size(entry)
        y_end += size(members[0])
    return places, (x_end, y_end)


FIRST_GROUPS = ((0, 0), (0, 0, 0), (2, 0), ((3, 0), (1, 0)), ((1, 1), (3, 1)), (2, 1))
FROZEN_GROUPS = ((2, 2), ((3, 2), (1, 2)))
SECOND_GROUPS = ((0, 1), ((0, 0, 1), (0, 1, 1)))
LATE_GROUPS = (((0, 2, 1), (0, 3, 1)), ((1, 0, 0), (1, 0, 1)))
FIRST, FIRST_PAIRS = placed(*FIRST_GROUPS)
SECOND, SECOND_PAIRS = placed(*FROZEN_GROUPS, *SECOND_GROUPS)
LATE, LATE_PAIRS = placed(*LATE_GROUPS)
TURN, TURN_PAIRS = placed((0, 0), (0, 1), (1, 1))
TURN2, TURN2_PAIRS = placed((1, 1), (2, 1), (3, 1))
FIRST_ROWS = {
    (0, 0): (2, 2, 1, 1, 1, 1),
    (0, 0, 0): (1, 1, 0, 0, 1, 1),
    (2, 0): (1, 1, 1, 0, 1, 1),
    (3, 0): (1, 1, 0, 0, 1, 1),
    (1, 0): (2, 1, 2, 2, 1, 1),
    (1, 1): (2, 2, 1, 1, 1, 1),
    (3, 1): (2, 2, 2, 2, 2, 2),
    (2, 1): (2, 2, 2, 2, 2, 2),
}
FROZEN_ROWS = {
    (2, 2): (1, 2, 1, 0, 2, 1),
    (3, 2): (1, 2, 0, 0, 1, 1),
    (1, 2): (2, 2, 2, 2, 1, 1),
}
SECOND_ROWS = {
    (0, 1): (2, 3, 1, 1, 2, 2),
    (0, 0, 1): (1, 2, 0, 0, 1, 1),
    (0, 1, 1): (2, 1, 2, 2, 1, 1),
}
LATE_ROWS = {
    (0, 2, 1): (1, 1, 1, 0, 1, 0),
    (0, 3, 1): (1, 1, 0, 0, 0, 0),
    (1, 0, 0): (1, 1, 0, 0, 0, 0),
    (1, 0, 1): (1, 1, 0, 0, 0, 0),
}
TURN_ROWS = {
    (0, 0): (2, 2, 2, 2, 2, 2),
    (0, 1): (2, 2, 2, 2, 2, 2),
    (1, 1): (2, 1, 2, 2, 1, 1),
}
TURN2_ROWS = {
    (1, 1): (2, 1, 1, 1, 0, 0),
    (2, 1): (1, 1, 1, 0, 1, 0),
    (3, 1): (2, 2, 1, 1, 1, 1),
}
FACES = tuple((dx, dy) for dx in (-1, 0, 1) for dy in (-1, 0, 1))
FACES = tuple(sorted(FACES, key=lambda face: -abs(face[0]) - abs(face[1])))
RING = tuple(face for face in FACES if face != (0, 0))


def runs(places, rows, face):
    dx, dy = face
    found = {}
    for entry, needed in rows.items():
        if dx == 0:
            count = 3
        elif dy == 0:
            count = needed[0 if dx == 1 else 1]
        else:
            count = needed[(2 if dx == 1 else 4) + (0 if dy == 1 else 1)]
        low = places[entry][0 if dy == 0 else 1]
        high = low + size(entry)
        found[low] = (high, max(count, found.get(low, (0, 0))[1]))
    merged = []
    for low, (high, count) in sorted(found.items()):
        if not count:
            continue
        if merged and merged[-1][1:] == (low, count):
            merged[-1] = (merged[-1][0], high, count)
        else:
            merged.append((low, high, count))
    return merged


def count_of(places, rows, faces):
    return sum(len(runs(places, rows, face)) for face in faces)


COPIES = (
    count_of(FIRST, FIRST_ROWS, RING)
    + 3
    + count_of(SECOND, FROZEN_ROWS, RING)
    + count_of(SECOND, SECOND_ROWS, RING)
    + count_of(LATE, LATE_ROWS, RING)
    + sum(count_of(TURN, {entry: TURN_ROWS[entry]}, RING) for entry in TURN)
    + sum(count_of(TURN2, {entry: TURN2_ROWS[entry]}, RING) for entry in TURN2)
    + 7 * SWEEPS
)


def rows_sent(dx, count):
    if dx == 1:
        return pl.ds(5 - count, count), pl.ds(2 - count, count)
    if dx == -1:
        return pl.ds(2, count), pl.ds(5, count)
    return pl.ds(2, 3), pl.ds(2, 3)


def mm(a, b):
    real = imag = None
    for k in range(3):
        ar, ai = a[0][:, k][:, None], a[1][:, k][:, None]
        br, bi = b[0][k][None], b[1][k][None]
        re, im = ar * br - ai * bi, ar * bi + ai * br
        real, imag = (re, im) if real is None else (real + re, imag + im)
    return real, imag


def mm_nh(a, b):
    real = imag = None
    for k in range(3):
        ar, ai = a[0][:, k][:, None], a[1][:, k][:, None]
        br, bi = b[0][:, k][None], b[1][:, k][None]
        re, im = ar * br + ai * bi, ai * br - ar * bi
        real, imag = (re, im) if real is None else (real + re, imag + im)
    return real, imag


def mm_hn(a, b):
    real = imag = None
    for k in range(3):
        ar, ai = a[0][k][:, None], a[1][k][:, None]
        br, bi = b[0][k][None], b[1][k][None]
        re, im = ar * br + ai * bi, ar * bi - ai * br
        real, imag = (re, im) if real is None else (real + re, imag + im)
    return real, imag


def times(a, b):
    return a[0] * b[0] - a[1] * b[1], a[0] * b[1] + a[1] * b[0]


def conj_times(a, b):
    return a[0] * b[0] + a[1] * b[1], a[0] * b[1] - a[1] * b[0]


def add(a, b):
    return a[0] + b[0], a[1] + b[1]


def cross(re, im):
    entry = [(re[k], im[k]) for k in range(6)]
    found = []
    for j in range(3):
        k, m = (j + 1) % 3, (j + 2) % 3
        one, two = times(entry[k], entry[3 + m]), times(entry[m], entry[3 + k])
        found.append((one[0] - two[0], one[1] - two[1]))
    return found


def compress(re, im):
    terms = [times((re[6 + j], im[6 + j]), value) for j, value in enumerate(cross(re, im))]
    phase = add(add(terms[0], terms[1]), terms[2])
    return (
        jnp.concatenate([re[0:6], phase[0][None]], axis=0),
        jnp.concatenate([im[0:6], phase[1][None]], axis=0),
    )


def restore(re, im):
    third = [conj_times(value, (re[6], im[6])) for value in cross(re, im)]
    return (
        jnp.concatenate([re[0:6], jnp.stack([value[0] for value in third])], axis=0),
        jnp.concatenate([im[0:6], jnp.stack([value[1] for value in third])], axis=0),
    )


def rotated(product, noise, link):
    mr, mi = product
    n = noise
    drift = 0.25 * step_drift
    kick = 0.25 * step_noise

    def off(i, j, nr, ni):
        return (
            kick * nr - drift * (mr[i, j] - mr[j, i]),
            kick * ni - drift * (mi[i, j] + mi[j, i]),
        )

    p = off(0, 1, n[1], n[0])
    q = off(0, 2, n[4], n[3])
    r = off(1, 2, n[6], n[5])
    third = (mi[0, 0] + mi[1, 1] + mi[2, 2]) / 3.0
    eighth = root_third * n[7]
    a = kick * (eighth + n[2]) - 2.0 * drift * (mi[0, 0] - third)
    b = kick * (eighth - n[2]) - 2.0 * drift * (mi[1, 1] - third)
    c = -(a + b)
    pp = p[0] * p[0] + p[1] * p[1]
    qq = q[0] * q[0] + q[1] * q[1]
    rr = r[0] * r[0] + r[1] * r[1]
    bc, ac, ab = b * c, a * c, a * b
    pr = times(p, r)
    real = 1.0 + (pp + qq + rr) - (ab + ac + bc)
    odd = a * rr + b * qq + c * pp - a * bc - 2.0 * (pr[1] * q[0] - pr[0] * q[1])
    weight = 2.0 / (real * real + odd * odd)
    inv = (real * weight, odd * weight)
    rs = conj_times(r, q)
    ps = conj_times(p, q)
    s01 = (c * p[1] - rs[0], -c * p[0] - rs[1])
    s02 = (b * q[1] + pr[0], pr[1] - b * q[0])
    s12 = (a * r[1] - ps[0], -a * r[0] - ps[1])
    adj = [
        [(1.0 + rr - bc, a), add(s01, p), add(s02, q)],
        [(s01[0] - p[0], p[1] - s01[1]), (1.0 + qq - ac, b), add(s12, r)],
        [(s02[0] - q[0], q[1] - s02[1]), (s12[0] - r[0], r[1] - s12[1]), (1.0 + pp - ab, c)],
    ]
    rotation = [[times(entry, inv) for entry in row] for row in adj]
    for i in range(3):
        rotation[i][i] = (rotation[i][i][0] - 1.0, rotation[i][i][1])
    stacked = tuple(
        jnp.stack([jnp.stack([entry[part] for entry in row]) for row in rotation])
        for part in range(2)
    )
    return mm(stacked, link)


def kernel(
    links_hbm, kicks_hbm, separations_hbm, out, windows,
    links, kicks, separations, fetch_sem, first_set, second_set, late_set, turn_set, turn2_set,
    win, kwin, held, lines, send_sem, recv_sem,
):
    slabs, sxs, syzs = (lax.axis_size(axis) for axis in ("slab", "sx", "syz"))
    slab, sx, syz = (lax.axis_index(axis) for axis in ("slab", "sx", "syz"))

    def peer(ds, dx, dy):
        return (
            lax.rem(slab + ds + slabs, slabs),
            lax.rem(sx + dx + sxs, sxs),
            lax.rem(syz + dy + syzs, syzs),
        )

    peers = [(ds, dx, 0) for ds in (-1, 1, 2) for dx in (-1, 0, 1)] + [(0, *face) for face in RING]
    peers.sort(key=lambda one: -sum(map(abs, one)))
    barrier = pltpu.get_barrier_semaphore()
    for one in peers:
        pl.semaphore_signal(barrier, inc=1, device_id=peer(*one), device_id_type=MESH)

    fetches = [
        pltpu.make_async_copy(links_hbm, links, fetch_sem.at[0]),
        pltpu.make_async_copy(kicks_hbm, kicks, fetch_sem.at[1]),
        pltpu.make_async_copy(separations_hbm, separations, fetch_sem.at[2]),
    ]
    for fetch in fetches:
        fetch.start()
    started = []

    def send(src, dst, target):
        index = len(started)
        copy = pltpu.make_async_remote_copy(
            src_ref=src,
            dst_ref=dst,
            send_sem=send_sem.at[index],
            recv_sem=recv_sem.at[index],
            device_id=peer(*target),
            device_id_type=MESH,
        )
        copy.start()
        started.append(copy)
        return copy

    shape = (8, 128)
    lane = lax.broadcasted_iota(jnp.int32, shape, 1)
    row = lax.broadcasted_iota(jnp.int32, shape, 0)
    half = lane % 16
    quarter = lane // 32
    low_half = lane < 64
    middle = jnp.logical_and(lane >= 32, lane < 96)
    first_of_half = (lane % 64) < 32
    odd_site = (sx * 3 + row + lane // 16) % 2
    is_odd = [odd_site == 1, odd_site == 0]
    last_half, first_half = half == 15, half == 0

    def own_index(time):
        lane3 = lax.broadcasted_iota(jnp.int32, (3, 128), 1)
        row3 = lax.broadcasted_iota(jnp.int32, (3, 128), 0)
        y = (lane3 % 64) // 16
        bit = (time + sx * 3 + row3 + y + lane3 // 64) % 2
        return y * 32 + (lane3 % 16) * 2 + bit

    own_gather = [own_index(0), own_index(1)]

    first3 = first_of_half[0:3]
    second3 = (lane[0:3] % 32) >= 16

    def put(bufs, places, *entries):
        x_buf, p_buf, m_buf = bufs[:3]
        upper, lower = [], []
        for entry, first, second in entries:
            x, y, _ = places[entry]
            count = size(entry)
            rolled = pltpu.roll(first, 96, 2)
            x_buf[2 * x : 2 * x + count, OWN] = first
            x_buf[2 * x + count : 2 * x + 2 * count, OWN] = second
            upper.append(jnp.where(first3, rolled, second))
            lower.append(jnp.where(first3, second, rolled))
        if len(entries) == 2:
            upper = [jnp.where(second3, upper[0], pltpu.roll(upper[1], 112, 2))]
            lower = [jnp.where(second3, pltpu.roll(lower[1], 16, 2), lower[0])]
        p_buf[y : y + count, OWN] = upper[0]
        m_buf[y : y + count, OWN] = lower[0]

    def spread(bufs, places, rows):
        copies = []
        for face in RING:
            for low, high, count in runs(places, rows, face):
                dx, dy = face
                out_rows, in_rows = rows_sent(dx, count)
                if dy == 0:
                    src = dst = bufs[0]
                    low, high = 2 * low, 2 * high
                else:
                    src, dst = (bufs[1], bufs[3]) if dy == 1 else (bufs[2], bufs[4])
                copies.append(
                    send(
                        src.at[pl.ds(low, high - low), out_rows],
                        dst.at[pl.ds(low, high - low), in_rows],
                        (0, dx, dy),
                    )
                )
        return copies

    def assemble(bufs, place, count):
        x_buf, _, _, lo_buf, hi_buf = bufs
        x, y, second = place
        lo, hi = lo_buf[y : y + count], hi_buf[y : y + count]
        if second:
            lo, hi = pltpu.roll(lo, 16, 2), pltpu.roll(hi, 112, 2)
        found = [[None, None], [None, None]]
        for member in range(2):
            start = 2 * x + member * count
            own = x_buf[start : start + count]
            for parity in range(2):
                q = 2 * parity + member
                edge = jnp.where(quarter == q, lo, hi)
                if q:
                    edge = pltpu.roll(edge, 128 - 32 * q, 2)
                centre = pltpu.roll(own, 32 if parity == 0 else 96, 2)
                found[parity][member] = jnp.where(middle, centre, edge)
        return found

    def take_in(bufs, places, entries):
        for entry in entries:
            if len(entry) == 2:
                found = assemble(bufs, places[entry], LINK)
                for parity in range(2):
                    for part, value in enumerate(restore(*found[parity])):
                        win[FIELD_OF[entry], parity, part] = value
            else:
                found = assemble(bufs, places[entry], KICK)
                for parity in range(2):
                    for member in range(2):
                        kwin[KICK_OF[entry], parity, 4 * member : 4 * member + 4] = found[parity][member]

    def packed(parts, time):
        return jnp.stack([jnp.take_along_axis(part, own_gather[time], axis=1) for part in parts])

    def pack(bufs, places, groups):
        for group in groups:
            members = []
            for entry in group if isinstance(group[0], tuple) else (group,):
                if len(entry) == 2:
                    direction, time = entry
                    whole = [
                        packed(
                            [
                                links[direction, part, i, j, :, time]
                                for i in range(3)
                                for j in range(3)
                            ],
                            time,
                        )
                        for part in range(2)
                    ]
                    members.append((entry, *compress(*whole)))
                else:
                    sweep, direction, time = entry
                    parts = [
                        kicks[sweep, direction, a, :, time].astype(jnp.float32) for a in range(8)
                    ]
                    members.append((entry, packed(parts[:4], time), packed(parts[4:], time)))
            put(bufs, places, *members)

    def wait(copies):
        for copy in copies:
            copy.wait_recv()

    for fetch in fetches:
        fetch.wait()
    pack(first_set, FIRST, FIRST_GROUPS)
    pl.semaphore_wait(barrier, len(peers))

    frozen_copies = []
    for k in range(3):
        low, high = FIRST[2, 0][min(k, 1)], FIRST[1, 0][min(k, 1)] + LINK
        goal = SECOND[2, 2][min(k, 1)]
        if k == 0:
            low, high, goal = 2 * low, 2 * high, 2 * goal
        frozen_copies.append(
            send(
                first_set[k].at[pl.ds(low, high - low), pl.ds(2, 3)],
                second_set[k].at[pl.ds(goal, high - low), pl.ds(2, 3)],
                (-1, 0, 0),
            )
        )
    first_copies = spread(first_set, FIRST, FIRST_ROWS)
    pack(second_set, SECOND, SECOND_GROUPS)
    second_copies = spread(second_set, SECOND, SECOND_ROWS)
    pack(late_set, LATE, LATE_GROUPS)
    wait(frozen_copies)
    second_copies += spread(second_set, SECOND, FROZEN_ROWS)
    late_copies = spread(late_set, LATE, LATE_ROWS)

    def shifted(pair, axis, sign, time, parity):
        def one(value):
            if axis == 0:
                return value
            flat = value.reshape(9, 8, 128)
            if axis == 1:
                flat = pltpu.roll(flat, 7 if sign == 1 else 1, 1)
            elif axis == 2:
                flat = pltpu.roll(flat, 112 if sign == 1 else 16, 2)
            else:
                odd = is_odd[(time + parity) % 2]
                if sign == 1:
                    inner = jnp.where(last_half, pltpu.roll(flat, 15, 2), pltpu.roll(flat, 127, 2))
                    flat = jnp.where(odd, inner, flat)
                else:
                    inner = jnp.where(first_half, pltpu.roll(flat, 113, 2), pltpu.roll(flat, 1, 2))
                    flat = jnp.where(odd, flat, inner)
            return flat.reshape(3, 3, 8, 128)

        return one(pair[0]), one(pair[1])

    def link(direction, time, parity):
        field = FIELD_OF[direction, time]
        return tuple(win[field, parity, part].reshape(3, 3, 8, 128) for part in range(2))

    def staples(mu, time, parity, planes):
        total = None
        other = 1 - parity
        for nu in planes:
            if mu == 0:
                ahead = link(nu, time + 1, other)
                ahead_low = link(nu, time + 1, parity)
            else:
                ahead = shifted(link(nu, time, other), mu, 1, time, parity)
            if nu == 0:
                above, below = link(mu, time + 1, other), link(mu, time - 1, other)
                low_time = time - 1
            else:
                above = shifted(link(mu, time, other), nu, 1, time, parity)
                below = link(mu, time, other)
                low_time = time
            if mu != 0:
                ahead_low = shifted(
                    link(nu, low_time, parity), mu, 1, low_time, other
                )
            upper = mm_nh(mm_nh(ahead, above), link(nu, time, parity))
            lower = mm_hn(mm(below, ahead_low), link(nu, low_time, other))
            lower = shifted(lower, nu, -1, time, parity)
            both = add(upper, lower)
            total = both if total is None else add(total, both)
        return total

    def ahead_of(slot, mu, time, parity, planes):
        for part, value in enumerate(staples(mu, time, parity, planes)):
            held[slot, part] = value

    def substep(sweep, mu, parity, time=1, slot=None, done=()):
        current = link(mu, time, parity)
        noise = kwin[KICK_OF[sweep, mu, time], parity]
        planes = [nu for nu in range(4) if nu != mu and nu not in done]
        total = staples(mu, time, parity, planes)
        if done:
            total = add(total, (held[slot, 0], held[slot, 1]))
        new = rotated(mm(current, total), noise, current)
        field = FIELD_OF[mu, time]
        for part in range(2):
            win[field, parity, part] = new[part].reshape(9, 8, 128)

    def own_part(two):
        return jnp.where(low_half, pltpu.roll(two[0], 96, 2), pltpu.roll(two[1], 32, 2))

    def pass_on(bufs, places, rows, entry):
        whole = [
            own_part([win[FIELD_OF[entry], parity, part] for parity in range(2)])[:, OWN]
            for part in range(2)
        ]
        put(bufs, places, (entry, *compress(*whole)))
        return spread(bufs, places, {entry: rows[entry]})

    def measure(sweep):
        products = [mm(link(0, 0, parity), link(0, 1, 1 - parity)) for parity in range(2)]
        whole = [
            own_part([product[part].reshape(9, 8, 128) for product in products])[:, OWN]
            for part in range(2)
        ]
        for part, value in enumerate(compress(*whole)):
            lines[sweep, 0, LINK * part : LINK * part + LINK, 0:3] = value
        copies = []
        src = lines.at[sweep, 0, :, pl.ds(0, 3)]
        for ds in (2, 1, 3, 0):
            copies.append(send(src, lines.at[sweep, ds, :, pl.ds(3, 3)], (-ds, -1, 0)))
        for ds in (2, 1, 3):
            copies.append(send(src, lines.at[sweep, ds, :, pl.ds(0, 3)], (-ds, 0, 0)))
        return copies

    wait(first_copies)
    take_in(first_set, FIRST, FIRST)
    substep(0, 0, 0, 0)
    substep(0, 0, 1, 0)
    turn_first = pass_on(turn_set, TURN, TURN_ROWS, (0, 0))
    ahead_of(1, 1, 1, 0, (2, 3))
    wait(second_copies)
    take_in(second_set, SECOND, SECOND)
    substep(0, 0, 0, 1)
    substep(0, 0, 1, 1)
    turn_first += pass_on(turn_set, TURN, TURN_ROWS, (0, 1))
    substep(0, 1, 0, 1, 1, (2, 3))
    turn_last = pass_on(turn_set, TURN, TURN_ROWS, (1, 1))
    line_copies = measure(0)
    ahead_of(0, 2, 1, 0, (3,))
    wait(late_copies)
    take_in(late_set, LATE, LATE)
    wait(turn_first)
    take_in(turn_set, TURN, ((0, 0), (0, 1)))
    ahead_of(1, 1, 1, 1, (0,))
    ahead_of(2, 2, 1, 1, (0,))
    ahead_of(3, 3, 1, 0, (0,))
    wait(turn_last)
    take_in(turn_set, TURN, ((1, 1),))
    substep(0, 1, 1, 1, 1, (0,))
    turn_first = pass_on(turn2_set, TURN2, TURN2_ROWS, (1, 1))
    substep(0, 2, 0, 1, 0, (3,))
    substep(0, 2, 1, 1, 2, (0,))
    turn_first += pass_on(turn2_set, TURN2, TURN2_ROWS, (2, 1))
    substep(0, 3, 0, 1, 3, (0,))
    turn_last = pass_on(turn2_set, TURN2, TURN2_ROWS, (3, 1))
    ahead_of(0, 3, 1, 1, (0,))
    wait(turn_first)
    take_in(turn2_set, TURN2, ((1, 1), (2, 1)))
    ahead_of(1, 0, 0, 0, (1, 2))
    ahead_of(2, 0, 1, 0, (1, 2))
    wait(turn_last)
    take_in(turn2_set, TURN2, ((3, 1),))
    substep(0, 3, 1, 1, 0, (0,))
    for time in range(2):
        substep(1, 0, 0, time, 1 + time, (1, 2))
        substep(1, 0, 1, time)
    last_copies = measure(1)
    keep = pltpu.make_async_copy(win, windows, fetch_sem.at[3])
    keep.start()

    def line(sweep, ds):
        whole = restore(lines[sweep, ds, 0:LINK], lines[sweep, ds, LINK : 2 * LINK])
        return tuple(part.reshape(3, 3, 8, 128) for part in whole)

    wait(line_copies)
    line_of = [[line(0, ds) for ds in range(4)]]
    low, high = {(0, 0): mm(line_of[0][0], line_of[0][1])}, {(0, 0): mm(line_of[0][2], line_of[0][3])}
    wait(last_copies)
    line_of.append([line(1, ds) for ds in range(4)])
    for pick in ((0, 1), (1, 0), (1, 1)):
        low[pick] = mm(line_of[pick[0]][0], line_of[pick[1]][1])
        high[pick] = mm(line_of[pick[0]][2], line_of[pick[1]][3])
    loops = []
    for left in low.values():
        for right in high.values():
            rr, ri = (jnp.swapaxes(part, 0, 1) for part in right)
            loops.append(jnp.sum((left[0] * rr - left[1] * ri).reshape(9, 8, 128), axis=0))
            loops.append(jnp.sum((left[0] * ri + left[1] * rr).reshape(9, 8, 128), axis=0))
    loops = jnp.stack(loops)
    distance = separations[slab]
    result = None
    for r in (3, 2, 1):
        far = pltpu.roll(loops, 8 - r, 1)
        if r % 2:
            far = pltpu.roll(far, 64, 2)
        value = jnp.sum(loops * far, axis=0)
        result = value if result is None else jnp.where(distance == r, value, result)
    lane3 = lax.broadcasted_iota(jnp.int32, (3, 128), 1)
    row3 = lax.broadcasted_iota(jnp.int32, (3, 128), 0)
    y, z = lane3 // 32, lane3 % 32
    index = ((z + y + row3 + sx * 3) % 2) * 64 + y * 16 + z // 2
    out[:, 0] = jnp.take_along_axis(result[0:3], index, axis=1)

    keep.wait()
    for copy in started:
        copy.wait_send()


def extended_2(block, sides, width):
    for axis, dim in sides:
        count = lax.axis_size(axis)
        forward = [(i, i + 1) for i in range(count - 1)]
        forward.append((count - 1, 0))
        backward = [(target, source) for source, target in forward]
        low = lax.ppermute(
            lax.slice_in_dim(block, block.shape[dim] - width, None, axis=dim), axis, forward
        )
        high = lax.ppermute(lax.slice_in_dim(block, 0, width, axis=dim), axis, backward)
        block = jnp.concatenate([low, block, high], axis=dim)
    return block


def shifted(block, axis, distance):
    devices = range(lax.axis_size(axis))
    route = [((i - distance) % len(devices), i) for i in devices]
    return lax.ppermute(block, axis, route)


def swapped(matrix_part):
    return jnp.swapaxes(matrix_part, 0, 1)


def dagger(matrix):
    return jnp.stack([swapped(matrix[0]), -swapped(matrix[1])])


def matrix_product(first, second):
    summed = None
    for middle in range(first.shape[1]):
        first_real = first[0][:, middle][:, None]
        first_imag = first[1][:, middle][:, None]
        second_real = second[0][middle][None]
        second_imag = second[1][middle][None]
        term_value = jnp.stack(
            [
                first_real * second_real - first_imag * second_imag,
                first_real * second_imag + first_imag * second_real,
            ]
        )
        summed = term_value if summed is None else summed + term_value
    return summed


def identity_like(matrix_part):
    return jnp.eye(3, dtype=matrix_part.dtype).reshape((3, 3) + (1,) * (matrix_part.ndim - 2))


def traceless_anti(matrix):
    anti_real = 0.5 * (matrix[0] - swapped(matrix[0]))
    anti_imag = 0.5 * (matrix[1] + swapped(matrix[1]))
    trace_third = (anti_imag[0, 0] + anti_imag[1, 1] + anti_imag[2, 2]) / 3.0
    anti_imag = anti_imag - identity_like(anti_imag) * trace_third[None, None]
    return jnp.stack([anti_real, anti_imag])


def algebra(coeffs):
    zero_part = jnp.zeros_like(coeffs[0])
    diag_first = coeffs[2] + root_third * coeffs[7]
    diag_second = -coeffs[2] + root_third * coeffs[7]
    diag_third = -2.0 * root_third * coeffs[7]
    herm_real = jnp.stack(
        [
            jnp.stack([diag_first, coeffs[0], coeffs[3]]),
            jnp.stack([coeffs[0], diag_second, coeffs[5]]),
            jnp.stack([coeffs[3], coeffs[5], diag_third]),
        ]
    )
    herm_imag = jnp.stack(
        [
            jnp.stack([zero_part, -coeffs[1], -coeffs[4]]),
            jnp.stack([coeffs[1], zero_part, -coeffs[6]]),
            jnp.stack([coeffs[4], coeffs[6], zero_part]),
        ]
    )
    return 0.5 * jnp.stack([-herm_imag, herm_real])


def complex_times(first, second):
    return (
        first[0] * second[0] - first[1] * second[1],
        first[0] * second[1] + first[1] * second[0],
    )


def cayley(generator, matrix):
    shift_real = identity_like(generator[0]) - 0.5 * generator[0]
    shift_imag = -0.5 * generator[1]

    def element(row_index, col_index):
        return (shift_real[row_index % 3, col_index % 3], shift_imag[row_index % 3, col_index % 3])

    cofactor = []
    for row_index in range(3):
        cof_row = []
        for col_index in range(3):
            forward = complex_times(
                element(row_index + 1, col_index + 1), element(row_index + 2, col_index + 2)
            )
            backward = complex_times(
                element(row_index + 1, col_index + 2), element(row_index + 2, col_index + 1)
            )
            cof_row.append((forward[0] - backward[0], forward[1] - backward[1]))
        cofactor.append(cof_row)
    det_real = 0.0
    det_imag = 0.0
    for col_index in range(3):
        det_term = complex_times(element(0, col_index), cofactor[0][col_index])
        det_real = det_real + det_term[0]
        det_imag = det_imag + det_term[1]
    weight = 1.0 / (det_real * det_real + det_imag * det_imag)
    inverse_det = (det_real * weight, -det_imag * weight)
    rotation_real = []
    rotation_imag = []
    for row_index in range(3):
        real_row = []
        imag_row = []
        for col_index in range(3):
            inverse_entry = complex_times(cofactor[col_index][row_index], inverse_det)
            delta_value = 1.0 if row_index == col_index else 0.0
            real_row.append(2.0 * inverse_entry[0] - delta_value)
            imag_row.append(2.0 * inverse_entry[1])
        rotation_real.append(jnp.stack(real_row))
        rotation_imag.append(jnp.stack(imag_row))
    rotation = jnp.stack([jnp.stack(rotation_real), jnp.stack(rotation_imag)])
    return matrix_product(rotation, matrix)


def unit_step(direction):
    return tuple((1 if axis_number == direction else 0 for axis_number in range(4)))


def add_steps(first, second):
    return tuple((first_part + second_part for first_part, second_part in zip(first, second)))


def negate(offsets):
    return tuple((-part_value for part_value in offsets))


def staple_sum(fetcher, direction):
    summed = None
    resting = (0, 0, 0, 0)
    onward = unit_step(direction)
    for transverse in range(4):
        if transverse == direction:
            continue
        across = unit_step(transverse)
        upper_loop = matrix_product(
            matrix_product(fetcher(transverse, onward), dagger(fetcher(direction, across))),
            dagger(fetcher(transverse, resting)),
        )
        lower_loop = matrix_product(
            matrix_product(
                dagger(fetcher(transverse, add_steps(onward, negate(across)))),
                dagger(fetcher(direction, negate(across))),
            ),
            fetcher(transverse, negate(across)),
        )
        summed = upper_loop + lower_loop if summed is None else summed + upper_loop + lower_loop
    return summed


def updated_link(fetcher, direction, coeffs):
    current = fetcher(direction, (0, 0, 0, 0))
    force = traceless_anti(matrix_product(current, staple_sum(fetcher, direction)))
    generator = -step_drift * force + step_noise * algebra(coeffs)
    return cayley(generator, current)


def extend(lattice, top_slice):
    stacked = jnp.concatenate([lattice, top_slice], axis=4)
    widened = extended_2(stacked, (("sx", 5),), 1)
    return extended_2(widened, (("syz", 6),), SITES_ALONG_Z)


def pick_field(extended, z_coord, x_count, yz_count, link_dir, offsets):
    t_step, x_step, y_step, z_step = offsets
    portion = extended[link_dir]
    if t_step == 1:
        portion = portion[:, :, :, 1:]
    else:
        portion = portion[:, :, :, :-1]
        if t_step == -1:
            portion = jnp.roll(portion, 1, axis=3)
    portion = portion[:, :, :, :, 1 + x_step : 1 + x_step + x_count]
    offset = (1 + y_step) * SITES_ALONG_Z
    portion = portion[:, :, :, :, :, offset : offset + yz_count]
    if z_step == 1:
        portion = jnp.where(
            z_coord == SITES_ALONG_Z - 1,
            jnp.roll(portion, SITES_ALONG_Z - 1, axis=-1),
            jnp.roll(portion, -1, axis=-1),
        )
    if z_step == -1:
        portion = jnp.where(
            z_coord == 0,
            jnp.roll(portion, 1 - SITES_ALONG_Z, axis=-1),
            jnp.roll(portion, 1, axis=-1),
        )
    return portion


def last_links(windows, gauge_links, langevin_noise):
    time_count, x_count, yz_count = gauge_links.shape[4:]
    y_count = yz_count // SITES_ALONG_Z
    time_coord = lax.axis_index("slab") * time_count + jnp.arange(time_count)
    x_coord = lax.axis_index("sx") * x_count + jnp.arange(x_count)
    cell_index = jnp.arange(yz_count)
    z_coord = cell_index % SITES_ALONG_Z
    yz_coord = lax.axis_index("syz") * y_count + cell_index // SITES_ALONG_Z + z_coord
    parity = (time_coord[:, None, None] + x_coord[None, :, None] + yz_coord[None, None, :]) % 2
    interior = jnp.broadcast_to((jnp.arange(time_count) != 0)[:, None, None], parity.shape)
    own = jnp.repeat(windows[:, :, :, :, OWN, 32:96], 2, axis=-1)
    lattice = gauge_links
    for (direction, time), index in FIELD_OF.items():
        if time < time_count:
            value = jnp.where(parity[time] == 0, own[index, 0], own[index, 1])
            lattice = lattice.at[direction, :, :, :, time].set(
                value.reshape(2, 3, 3, x_count, yz_count)
            )
    above_face = shifted(gauge_links[1:, :, :, :, 0:1], "slab", -1)
    top_slice = jnp.concatenate(
        [jnp.zeros_like(gauge_links[0:1, :, :, :, 0:1]), above_face], axis=0
    )
    for direction in range(1, 4):
        kick_field = langevin_noise[SWEEPS - 1, direction].astype(jnp.float32)
        for colour in range(2):
            extended = extend(lattice, top_slice)
            fetcher = partial(pick_field, extended, z_coord, x_count, yz_count)
            candidate = updated_link(fetcher, direction, kick_field)
            chosen = jnp.logical_and(parity == colour, interior)
            lattice = lattice.at[direction].set(
                jnp.where(chosen, candidate, lattice[direction])
            )
    return lattice


def local(gauge_links, langevin_noise, separations):
    def buffers(ends):
        halves = tuple(pltpu.VMEM((ends[1], 8, 128), jnp.float32) for _ in range(4))
        return (pltpu.VMEM((2 * ends[0], 8, 128), jnp.float32), *halves)

    sets = (FIRST_PAIRS, SECOND_PAIRS, LATE_PAIRS, TURN_PAIRS, TURN2_PAIRS)
    vmem = pl.BlockSpec(memory_space=pltpu.VMEM)
    links = jnp.swapaxes(gauge_links, 4, 5)
    kicks = jnp.swapaxes(langevin_noise, 3, 4)
    win_shape = (len(FIELDS), 2, 2, 9, 8, 128)
    correlator, windows = pl.pallas_call(
        kernel,
        out_shape=(
            jax.ShapeDtypeStruct((3, 1, 128), jnp.float32),
            jax.ShapeDtypeStruct(win_shape, jnp.float32),
        ),
        in_specs=[
            pl.BlockSpec(memory_space=pltpu.HBM),
            pl.BlockSpec(memory_space=pltpu.HBM),
            pl.BlockSpec(memory_space=pltpu.HBM),
        ],
        out_specs=(vmem, pl.BlockSpec(memory_space=pltpu.HBM)),
        scratch_shapes=[
            pltpu.VMEM(links.shape, jnp.float32),
            pltpu.VMEM(kicks.shape, kicks.dtype),
            pltpu.SMEM(separations.shape, jnp.int32),
            pltpu.SemaphoreType.DMA((4,)),
        ]
        + [buffers(pairs) for pairs in sets] + [
            pltpu.VMEM(win_shape, jnp.float32),
            pltpu.VMEM((len(KICKS), 2, 8, 8, 128), jnp.float32),
            pltpu.VMEM((4, 2, 3, 3, 8, 128), jnp.float32),
            pltpu.VMEM((SWEEPS, 4, 2 * LINK, 8, 128), jnp.float32),
            pltpu.SemaphoreType.DMA((COPIES,)),
            pltpu.SemaphoreType.DMA((COPIES,)),
        ],
        compiler_params=pltpu.CompilerParams(
            collective_id=0, has_side_effects=True, vmem_limit_bytes=VMEM_LIMIT
        ),
    )(links, kicks, separations)
    last_links(windows, gauge_links, langevin_noise)
    return jnp.swapaxes(correlator, 0, 1) * (1.0 / SWEEPS**4)


def solution(mesh):
    return jax.shard_map(
        local,
        mesh=mesh,
        in_specs=(
            P(None, None, None, None, "slab", "sx", "syz"),
            P(None, None, None, "slab", "sx", "syz"),
            P(),
        ),
        out_specs=P("slab", "sx", "syz"),
        check_vma=False,
    )
```

```python
from functools import partial

import jax
import jax.numpy as jnp
from jax import lax
from jax.experimental import pallas as pl
from jax.experimental.pallas import tpu as pltpu
from jax.sharding import PartitionSpec as P

SITES_ALONG_Z = 32
SWEEPS = 2

step_drift = 0.2
step_noise = 0.4
root_third = 0.5773502691896258

MESH = pl.DeviceIdType.MESH
VMEM_LIMIT = 60 * 1024 * 1024

OWN = slice(2, 5)
FIELDS = ((0, 0), (0, 1), (1, 1), (2, 1), (3, 1), (1, 0), (2, 0), (3, 0), (1, 2), (2, 2), (3, 2))
FIELD_OF = {field: index for index, field in enumerate(FIELDS)}
KICKS = ((0, 0, 0), (0, 0, 1), (0, 1, 1), (0, 2, 1), (0, 3, 1), (1, 0, 0), (1, 0, 1))
KICK_OF = {kick: index for index, kick in enumerate(KICKS)}
LINK, KICK = 7, 4


def size(entry):
    return LINK if len(entry) == 2 else KICK


def placed(*groups):
    places, x_end, y_end = {}, 0, 0
    for group in groups:
        members = group if isinstance(group[0], tuple) else (group,)
        for half, entry in enumerate(members):
            places[entry] = (x_end, y_end, half)
            x_end += size(entry)
        y_end += size(members[0])
    return places, (x_end, y_end)


FIRST_GROUPS = ((0, 0), (0, 0, 0), (2, 0), ((3, 0), (1, 0)), ((1, 1), (3, 1)), (2, 1))
FROZEN_GROUPS = ((2, 2), ((3, 2), (1, 2)))
SECOND_GROUPS = ((0, 1), ((0, 0, 1), (0, 1, 1)))
LATE_GROUPS = (((0, 2, 1), (0, 3, 1)), ((1, 0, 0), (1, 0, 1)))
FIRST, FIRST_PAIRS = placed(*FIRST_GROUPS)
SECOND, SECOND_PAIRS = placed(*FROZEN_GROUPS, *SECOND_GROUPS)
LATE, LATE_PAIRS = placed(*LATE_GROUPS)
TURN, TURN_PAIRS = placed((0, 0), (0, 1), (1, 1))
TURN2, TURN2_PAIRS = placed((1, 1), (2, 1), (3, 1))
FIRST_ROWS = {
    (0, 0): (2, 2, 1, 1, 1, 1),
    (0, 0, 0): (1, 1, 0, 0, 1, 1),
    (2, 0): (1, 1, 1, 0, 1, 1),
    (3, 0): (1, 1, 0, 0, 1, 1),
    (1, 0): (2, 1, 2, 2, 1, 1),
    (1, 1): (2, 2, 1, 1, 1, 1),
    (3, 1): (2, 2, 2, 2, 2, 2),
    (2, 1): (2, 2, 2, 2, 2, 2),
}
FROZEN_ROWS = {
    (2, 2): (1, 2, 1, 0, 2, 1),
    (3, 2): (1, 2, 0, 0, 1, 1),
    (1, 2): (2, 2, 2, 2, 1, 1),
}
SECOND_ROWS = {
    (0, 1): (2, 3, 1, 1, 2, 2),
    (0, 0, 1): (1, 2, 0, 0, 1, 1),
    (0, 1, 1): (2, 1, 2, 2, 1, 1),
}
LATE_ROWS = {
    (0, 2, 1): (1, 1, 1, 0, 1, 0),
    (0, 3, 1): (1, 1, 0, 0, 0, 0),
    (1, 0, 0): (1, 1, 0, 0, 0, 0),
    (1, 0, 1): (1, 1, 0, 0, 0, 0),
}
TURN_ROWS = {
    (0, 0): (2, 2, 2, 2, 2, 2),
    (0, 1): (2, 2, 2, 2, 2, 2),
    (1, 1): (2, 1, 2, 2, 1, 1),
}
TURN2_ROWS = {
    (1, 1): (2, 1, 1, 1, 0, 0),
    (2, 1): (1, 1, 1, 0, 1, 0),
    (3, 1): (2, 2, 1, 1, 1, 1),
}
FACES = tuple((dx, dy) for dx in (-1, 0, 1) for dy in (-1, 0, 1))
FACES = tuple(sorted(FACES, key=lambda face: -abs(face[0]) - abs(face[1])))
RING = tuple(face for face in FACES if face != (0, 0))


def runs(places, rows, face):
    dx, dy = face
    found = {}
    for entry, needed in rows.items():
        if dx == 0:
            count = 3
        elif dy == 0:
            count = needed[0 if dx == 1 else 1]
        else:
            count = needed[(2 if dx == 1 else 4) + (0 if dy == 1 else 1)]
        low = places[entry][0 if dy == 0 else 1]
        high = low + size(entry)
        found[low] = (high, max(count, found.get(low, (0, 0))[1]))
    merged = []
    for low, (high, count) in sorted(found.items()):
        if not count:
            continue
        if merged and merged[-1][1:] == (low, count):
            merged[-1] = (merged[-1][0], high, count)
        else:
            merged.append((low, high, count))
    return merged


def count_of(places, rows, faces):
    return sum(len(runs(places, rows, face)) for face in faces)


COPIES = (
    count_of(FIRST, FIRST_ROWS, RING)
    + 3
    + count_of(SECOND, FROZEN_ROWS, RING)
    + count_of(SECOND, SECOND_ROWS, RING)
    + count_of(LATE, LATE_ROWS, RING)
    + sum(count_of(TURN, {entry: TURN_ROWS[entry]}, RING) for entry in TURN)
    + sum(count_of(TURN2, {entry: TURN2_ROWS[entry]}, RING) for entry in TURN2)
    + 7 * SWEEPS
)


def rows_sent(dx, count):
    if dx == 1:
        return pl.ds(5 - count, count), pl.ds(2 - count, count)
    if dx == -1:
        return pl.ds(2, count), pl.ds(5, count)
    return pl.ds(2, 3), pl.ds(2, 3)


def mm(a, b):
    real = imag = None
    for k in range(3):
        ar, ai = a[0][:, k][:, None], a[1][:, k][:, None]
        br, bi = b[0][k][None], b[1][k][None]
        re, im = ar * br - ai * bi, ar * bi + ai * br
        real, imag = (re, im) if real is None else (real + re, imag + im)
    return real, imag


def mm_nh(a, b):
    real = imag = None
    for k in range(3):
        ar, ai = a[0][:, k][:, None], a[1][:, k][:, None]
        br, bi = b[0][:, k][None], b[1][:, k][None]
        re, im = ar * br + ai * bi, ai * br - ar * bi
        real, imag = (re, im) if real is None else (real + re, imag + im)
    return real, imag


def mm_hn(a, b):
    real = imag = None
    for k in range(3):
        ar, ai = a[0][k][:, None], a[1][k][:, None]
        br, bi = b[0][k][None], b[1][k][None]
        re, im = ar * br + ai * bi, ar * bi - ai * br
        real, imag = (re, im) if real is None else (real + re, imag + im)
    return real, imag


def times(a, b):
    return a[0] * b[0] - a[1] * b[1], a[0] * b[1] + a[1] * b[0]


def conj_times(a, b):
    return a[0] * b[0] + a[1] * b[1], a[0] * b[1] - a[1] * b[0]


def add(a, b):
    return a[0] + b[0], a[1] + b[1]


def cross(re, im):
    entry = [(re[k], im[k]) for k in range(6)]
    found = []
    for j in range(3):
        k, m = (j + 1) % 3, (j + 2) % 3
        one, two = times(entry[k], entry[3 + m]), times(entry[m], entry[3 + k])
        found.append((one[0] - two[0], one[1] - two[1]))
    return found


def compress(re, im):
    terms = [times((re[6 + j], im[6 + j]), value) for j, value in enumerate(cross(re, im))]
    phase = add(add(terms[0], terms[1]), terms[2])
    return (
        jnp.concatenate([re[0:6], phase[0][None]], axis=0),
        jnp.concatenate([im[0:6], phase[1][None]], axis=0),
    )


def restore(re, im):
    third = [conj_times(value, (re[6], im[6])) for value in cross(re, im)]
    return (
        jnp.concatenate([re[0:6], jnp.stack([value[0] for value in third])], axis=0),
        jnp.concatenate([im[0:6], jnp.stack([value[1] for value in third])], axis=0),
    )


def rotated(product, noise, link):
    mr, mi = product
    n = noise
    drift = 0.25 * step_drift
    kick = 0.25 * step_noise

    def off(i, j, nr, ni):
        return (
            kick * nr - drift * (mr[i, j] - mr[j, i]),
            kick * ni - drift * (mi[i, j] + mi[j, i]),
        )

    p = off(0, 1, n[1], n[0])
    q = off(0, 2, n[4], n[3])
    r = off(1, 2, n[6], n[5])
    third = (mi[0, 0] + mi[1, 1] + mi[2, 2]) / 3.0
    eighth = root_third * n[7]
    a = kick * (eighth + n[2]) - 2.0 * drift * (mi[0, 0] - third)
    b = kick * (eighth - n[2]) - 2.0 * drift * (mi[1, 1] - third)
    c = -(a + b)
    pp = p[0] * p[0] + p[1] * p[1]
    qq = q[0] * q[0] + q[1] * q[1]
    rr = r[0] * r[0] + r[1] * r[1]
    bc, ac, ab = b * c, a * c, a * b
    pr = times(p, r)
    real = 1.0 + (pp + qq + rr) - (ab + ac + bc)
    odd = a * rr + b * qq + c * pp - a * bc - 2.0 * (pr[1] * q[0] - pr[0] * q[1])
    weight = 2.0 / (real * real + odd * odd)
    inv = (real * weight, odd * weight)
    rs = conj_times(r, q)
    ps = conj_times(p, q)
    s01 = (c * p[1] - rs[0], -c * p[0] - rs[1])
    s02 = (b * q[1] + pr[0], pr[1] - b * q[0])
    s12 = (a * r[1] - ps[0], -a * r[0] - ps[1])
    adj = [
        [(1.0 + rr - bc, a), add(s01, p), add(s02, q)],
        [(s01[0] - p[0], p[1] - s01[1]), (1.0 + qq - ac, b), add(s12, r)],
        [(s02[0] - q[0], q[1] - s02[1]), (s12[0] - r[0], r[1] - s12[1]), (1.0 + pp - ab, c)],
    ]
    rotation = [[times(entry, inv) for entry in row] for row in adj]
    for i in range(3):
        rotation[i][i] = (rotation[i][i][0] - 1.0, rotation[i][i][1])
    stacked = tuple(
        jnp.stack([jnp.stack([entry[part] for entry in row]) for row in rotation])
        for part in range(2)
    )
    return mm(stacked, link)


def kernel(
    links_hbm, kicks_hbm, separations_hbm, out, windows,
    links, kicks, separations, fetch_sem, first_set, second_set, late_set, turn_set, turn2_set,
    win, kwin, held, lines, send_sem, recv_sem,
):
    slabs, sxs, syzs = (lax.axis_size(axis) for axis in ("slab", "sx", "syz"))
    slab, sx, syz = (lax.axis_index(axis) for axis in ("slab", "sx", "syz"))

    def peer(ds, dx, dy):
        return (
            lax.rem(slab + ds + slabs, slabs),
            lax.rem(sx + dx + sxs, sxs),
            lax.rem(syz + dy + syzs, syzs),
        )

    peers = [(0, *face) for face in RING] + [(1, 0, 0)]
    barrier = pltpu.get_barrier_semaphore()
    for one in peers:
        pl.semaphore_signal(barrier, inc=1, device_id=peer(*one), device_id_type=MESH)

    fetches = [
        pltpu.make_async_copy(links_hbm, links, fetch_sem.at[0]),
        pltpu.make_async_copy(kicks_hbm, kicks, fetch_sem.at[1]),
        pltpu.make_async_copy(separations_hbm, separations, fetch_sem.at[2]),
    ]
    for fetch in fetches:
        fetch.start()
    started = []

    def send(src, dst, target):
        index = len(started)
        copy = pltpu.make_async_remote_copy(
            src_ref=src,
            dst_ref=dst,
            send_sem=send_sem.at[index],
            recv_sem=recv_sem.at[index],
            device_id=peer(*target),
            device_id_type=MESH,
        )
        copy.start()
        started.append(copy)
        return copy

    shape = (8, 128)
    lane = lax.broadcasted_iota(jnp.int32, shape, 1)
    row = lax.broadcasted_iota(jnp.int32, shape, 0)
    half = lane % 16
    quarter = lane // 32
    low_half = lane < 64
    middle = jnp.logical_and(lane >= 32, lane < 96)
    first_of_half = (lane % 64) < 32
    odd_site = (sx * 3 + row + lane // 16) % 2
    is_odd = [odd_site == 1, odd_site == 0]
    last_half, first_half = half == 15, half == 0

    def own_index(time):
        lane3 = lax.broadcasted_iota(jnp.int32, (3, 128), 1)
        row3 = lax.broadcasted_iota(jnp.int32, (3, 128), 0)
        y = (lane3 % 64) // 16
        bit = (time + sx * 3 + row3 + y + lane3 // 64) % 2
        return y * 32 + (lane3 % 16) * 2 + bit

    own_gather = [own_index(0), own_index(1)]

    first3 = first_of_half[0:3]
    second3 = (lane[0:3] % 32) >= 16

    def put(bufs, places, *entries):
        x_buf, p_buf, m_buf = bufs[:3]
        upper, lower = [], []
        for entry, first, second in entries:
            x, y, _ = places[entry]
            count = size(entry)
            rolled = pltpu.roll(first, 96, 2)
            x_buf[2 * x : 2 * x + count, OWN] = first
            x_buf[2 * x + count : 2 * x + 2 * count, OWN] = second
            upper.append(jnp.where(first3, rolled, second))
            lower.append(jnp.where(first3, second, rolled))
        if len(entries) == 2:
            upper = [jnp.where(second3, upper[0], pltpu.roll(upper[1], 112, 2))]
            lower = [jnp.where(second3, pltpu.roll(lower[1], 16, 2), lower[0])]
        p_buf[y : y + count, OWN] = upper[0]
        m_buf[y : y + count, OWN] = lower[0]

    def spread(bufs, places, rows):
        copies = []
        for face in RING:
            for low, high, count in runs(places, rows, face):
                dx, dy = face
                out_rows, in_rows = rows_sent(dx, count)
                if dy == 0:
                    src = dst = bufs[0]
                    low, high = 2 * low, 2 * high
                else:
                    src, dst = (bufs[1], bufs[3]) if dy == 1 else (bufs[2], bufs[4])
                copies.append(
                    send(
                        src.at[pl.ds(low, high - low), out_rows],
                        dst.at[pl.ds(low, high - low), in_rows],
                        (0, dx, dy),
                    )
                )
        return copies

    def assemble(bufs, place, count):
        x_buf, _, _, lo_buf, hi_buf = bufs
        x, y, second = place
        lo, hi = lo_buf[y : y + count], hi_buf[y : y + count]
        if second:
            lo, hi = pltpu.roll(lo, 16, 2), pltpu.roll(hi, 112, 2)
        found = [[None, None], [None, None]]
        for member in range(2):
            start = 2 * x + member * count
            own = x_buf[start : start + count]
            for parity in range(2):
                q = 2 * parity + member
                edge = jnp.where(quarter == q, lo, hi)
                if q:
                    edge = pltpu.roll(edge, 128 - 32 * q, 2)
                centre = pltpu.roll(own, 32 if parity == 0 else 96, 2)
                found[parity][member] = jnp.where(middle, centre, edge)
        return found

    def take_in(bufs, places, entries):
        for entry in entries:
            if len(entry) == 2:
                found = assemble(bufs, places[entry], LINK)
                for parity in range(2):
                    for part, value in enumerate(restore(*found[parity])):
                        win[FIELD_OF[entry], parity, part] = value
            else:
                found = assemble(bufs, places[entry], KICK)
                for parity in range(2):
                    for member in range(2):
                        kwin[KICK_OF[entry], parity, 4 * member : 4 * member + 4] = found[parity][member]

    def packed(parts, time):
        return jnp.stack([jnp.take_along_axis(part, own_gather[time], axis=1) for part in parts])

    def pack(bufs, places, groups):
        for group in groups:
            members = []
            for entry in group if isinstance(group[0], tuple) else (group,):
                if len(entry) == 2:
                    direction, time = entry
                    whole = [
                        packed(
                            [
                                links[direction, part, i, j, :, time]
                                for i in range(3)
                                for j in range(3)
                            ],
                            time,
                        )
                        for part in range(2)
                    ]
                    members.append((entry, *compress(*whole)))
                else:
                    sweep, direction, time = entry
                    parts = [
                        kicks[sweep, direction, a, :, time].astype(jnp.float32) for a in range(8)
                    ]
                    members.append((entry, packed(parts[:4], time), packed(parts[4:], time)))
            put(bufs, places, *members)

    def wait(copies):
        for copy in copies:
            copy.wait_recv()

    for fetch in fetches:
        fetch.wait()
    pack(first_set, FIRST, FIRST_GROUPS)
    pl.semaphore_wait(barrier, len(peers))

    frozen_copies = []
    for k in range(3):
        low, high = FIRST[2, 0][min(k, 1)], FIRST[1, 0][min(k, 1)] + LINK
        goal = SECOND[2, 2][min(k, 1)]
        if k == 0:
            low, high, goal = 2 * low, 2 * high, 2 * goal
        frozen_copies.append(
            send(
                first_set[k].at[pl.ds(low, high - low), pl.ds(2, 3)],
                second_set[k].at[pl.ds(goal, high - low), pl.ds(2, 3)],
                (-1, 0, 0),
            )
        )
    first_copies = spread(first_set, FIRST, FIRST_ROWS)
    pack(second_set, SECOND, SECOND_GROUPS)
    second_copies = spread(second_set, SECOND, SECOND_ROWS)
    pack(late_set, LATE, LATE_GROUPS)
    wait(frozen_copies)
    second_copies += spread(second_set, SECOND, FROZEN_ROWS)
    late_copies = spread(late_set, LATE, LATE_ROWS)

    def shifted(pair, axis, sign, time, parity):
        def one(value):
            if axis == 0:
                return value
            flat = value.reshape(9, 8, 128)
            if axis == 1:
                flat = pltpu.roll(flat, 7 if sign == 1 else 1, 1)
            elif axis == 2:
                flat = pltpu.roll(flat, 112 if sign == 1 else 16, 2)
            else:
                odd = is_odd[(time + parity) % 2]
                if sign == 1:
                    inner = jnp.where(last_half, pltpu.roll(flat, 15, 2), pltpu.roll(flat, 127, 2))
                    flat = jnp.where(odd, inner, flat)
                else:
                    inner = jnp.where(first_half, pltpu.roll(flat, 113, 2), pltpu.roll(flat, 1, 2))
                    flat = jnp.where(odd, flat, inner)
            return flat.reshape(3, 3, 8, 128)

        return one(pair[0]), one(pair[1])

    def link(direction, time, parity):
        field = FIELD_OF[direction, time]
        return tuple(win[field, parity, part].reshape(3, 3, 8, 128) for part in range(2))

    def staples(mu, time, parity, planes):
        total = None
        other = 1 - parity
        for nu in planes:
            if mu == 0:
                ahead = link(nu, time + 1, other)
                ahead_low = link(nu, time + 1, parity)
            else:
                ahead = shifted(link(nu, time, other), mu, 1, time, parity)
            if nu == 0:
                above, below = link(mu, time + 1, other), link(mu, time - 1, other)
                low_time = time - 1
            else:
                above = shifted(link(mu, time, other), nu, 1, time, parity)
                below = link(mu, time, other)
                low_time = time
            if mu != 0:
                ahead_low = shifted(
                    link(nu, low_time, parity), mu, 1, low_time, other
                )
            upper = mm_nh(mm_nh(ahead, above), link(nu, time, parity))
            lower = mm_hn(mm(below, ahead_low), link(nu, low_time, other))
            lower = shifted(lower, nu, -1, time, parity)
            both = add(upper, lower)
            total = both if total is None else add(total, both)
        return total

    def ahead_of(slot, mu, time, parity, planes):
        for part, value in enumerate(staples(mu, time, parity, planes)):
            held[slot, part] = value

    def substep(sweep, mu, parity, time=1, slot=None, done=()):
        current = link(mu, time, parity)
        noise = kwin[KICK_OF[sweep, mu, time], parity]
        planes = [nu for nu in range(4) if nu != mu and nu not in done]
        total = staples(mu, time, parity, planes)
        if done:
            total = add(total, (held[slot, 0], held[slot, 1]))
        new = rotated(mm(current, total), noise, current)
        field = FIELD_OF[mu, time]
        for part in range(2):
            win[field, parity, part] = new[part].reshape(9, 8, 128)

    def own_part(two):
        return jnp.where(low_half, pltpu.roll(two[0], 96, 2), pltpu.roll(two[1], 32, 2))

    def pass_on(bufs, places, rows, entry):
        whole = [
            own_part([win[FIELD_OF[entry], parity, part] for parity in range(2)])[:, OWN]
            for part in range(2)
        ]
        put(bufs, places, (entry, *compress(*whole)))
        return spread(bufs, places, {entry: rows[entry]})

    def measure(sweep):
        products = [mm(link(0, 0, parity), link(0, 1, 1 - parity)) for parity in range(2)]
        whole = [
            own_part([product[part].reshape(9, 8, 128) for product in products])[:, OWN]
            for part in range(2)
        ]
        for part, value in enumerate(compress(*whole)):
            lines[sweep, 0, LINK * part : LINK * part + LINK, 0:3] = value
    def hand_lines(sweep, slabs_below):
        copies = {}
        src = lines.at[sweep, 0, :, pl.ds(0, 3)]
        for ds in slabs_below:
            copies[ds, 1] = send(src, lines.at[sweep, ds, :, pl.ds(3, 3)], (-ds, -1, 0))
        for ds in slabs_below:
            if ds:
                copies[ds, 0] = send(src, lines.at[sweep, ds, :, pl.ds(0, 3)], (-ds, 0, 0))
        return copies

    wait(first_copies)
    take_in(first_set, FIRST, FIRST)
    substep(0, 0, 0, 0)
    substep(0, 0, 1, 0)
    turn_first = pass_on(turn_set, TURN, TURN_ROWS, (0, 0))
    ahead_of(1, 1, 1, 0, (2, 3))
    wait(second_copies)
    take_in(second_set, SECOND, SECOND)
    substep(0, 0, 0, 1)
    substep(0, 0, 1, 1)
    turn_first += pass_on(turn_set, TURN, TURN_ROWS, (0, 1))
    substep(0, 1, 0, 1, 1, (2, 3))
    turn_last = pass_on(turn_set, TURN, TURN_ROWS, (1, 1))
    measure(0)
    line_copies = hand_lines(0, (1, 3, 0))
    ahead_of(0, 2, 1, 0, (3,))
    wait(late_copies)
    take_in(late_set, LATE, LATE)
    wait(turn_first)
    take_in(turn_set, TURN, ((0, 0), (0, 1)))
    ahead_of(1, 1, 1, 1, (0,))
    ahead_of(2, 2, 1, 1, (0,))
    ahead_of(3, 3, 1, 0, (0,))
    wait(turn_last)
    take_in(turn_set, TURN, ((1, 1),))
    substep(0, 1, 1, 1, 1, (0,))
    turn_first = pass_on(turn2_set, TURN2, TURN2_ROWS, (1, 1))
    substep(0, 2, 0, 1, 0, (3,))
    substep(0, 2, 1, 1, 2, (0,))
    turn_first += pass_on(turn2_set, TURN2, TURN2_ROWS, (2, 1))
    substep(0, 3, 0, 1, 3, (0,))
    turn_last = pass_on(turn2_set, TURN2, TURN2_ROWS, (3, 1))
    ahead_of(0, 3, 1, 1, (0,))
    wait([line_copies.pop((3, 0))])
    line_copies.update(hand_lines(0, (2,)))
    wait(turn_first)
    take_in(turn2_set, TURN2, ((1, 1), (2, 1)))
    ahead_of(1, 0, 0, 0, (1, 2))
    ahead_of(2, 0, 1, 0, (1, 2))
    wait(turn_last)
    take_in(turn2_set, TURN2, ((3, 1),))
    substep(0, 3, 1, 1, 0, (0,))
    for time in range(2):
        substep(1, 0, 0, time, 1 + time, (1, 2))
        substep(1, 0, 1, time)
    measure(1)
    last_copies = hand_lines(1, (2, 1, 3, 0))
    keep = pltpu.make_async_copy(win, windows, fetch_sem.at[3])
    keep.start()

    def line(sweep, ds):
        whole = restore(lines[sweep, ds, 0:LINK], lines[sweep, ds, LINK : 2 * LINK])
        return tuple(part.reshape(3, 3, 8, 128) for part in whole)

    wait(line_copies.values())
    line_of = [[line(0, ds) for ds in range(4)]]
    low, high = {(0, 0): mm(line_of[0][0], line_of[0][1])}, {(0, 0): mm(line_of[0][2], line_of[0][3])}
    wait(last_copies.values())
    line_of.append([line(1, ds) for ds in range(4)])
    for pick in ((0, 1), (1, 0), (1, 1)):
        low[pick] = mm(line_of[pick[0]][0], line_of[pick[1]][1])
        high[pick] = mm(line_of[pick[0]][2], line_of[pick[1]][3])
    loops = []
    for left in low.values():
        for right in high.values():
            rr, ri = (jnp.swapaxes(part, 0, 1) for part in right)
            loops.append(jnp.sum((left[0] * rr - left[1] * ri).reshape(9, 8, 128), axis=0))
            loops.append(jnp.sum((left[0] * ri + left[1] * rr).reshape(9, 8, 128), axis=0))
    loops = jnp.stack(loops)
    distance = separations[slab]
    result = None
    for r in (3, 2, 1):
        far = pltpu.roll(loops, 8 - r, 1)
        if r % 2:
            far = pltpu.roll(far, 64, 2)
        value = jnp.sum(loops * far, axis=0)
        result = value if result is None else jnp.where(distance == r, value, result)
    lane3 = lax.broadcasted_iota(jnp.int32, (3, 128), 1)
    row3 = lax.broadcasted_iota(jnp.int32, (3, 128), 0)
    y, z = lane3 // 32, lane3 % 32
    index = ((z + y + row3 + sx * 3) % 2) * 64 + y * 16 + z // 2
    out[:, 0] = jnp.take_along_axis(result[0:3], index, axis=1)

    keep.wait()
    for copy in started:
        copy.wait_send()


def extended_2(block, sides, width):
    for axis, dim in sides:
        count = lax.axis_size(axis)
        forward = [(i, i + 1) for i in range(count - 1)]
        forward.append((count - 1, 0))
        backward = [(target, source) for source, target in forward]
        low = lax.ppermute(
            lax.slice_in_dim(block, block.shape[dim] - width, None, axis=dim), axis, forward
        )
        high = lax.ppermute(lax.slice_in_dim(block, 0, width, axis=dim), axis, backward)
        block = jnp.concatenate([low, block, high], axis=dim)
    return block


def shifted(block, axis, distance):
    devices = range(lax.axis_size(axis))
    route = [((i - distance) % len(devices), i) for i in devices]
    return lax.ppermute(block, axis, route)


def swapped(matrix_part):
    return jnp.swapaxes(matrix_part, 0, 1)


def dagger(matrix):
    return jnp.stack([swapped(matrix[0]), -swapped(matrix[1])])


def matrix_product(first, second):
    summed = None
    for middle in range(first.shape[1]):
        first_real = first[0][:, middle][:, None]
        first_imag = first[1][:, middle][:, None]
        second_real = second[0][middle][None]
        second_imag = second[1][middle][None]
        term_value = jnp.stack(
            [
                first_real * second_real - first_imag * second_imag,
                first_real * second_imag + first_imag * second_real,
            ]
        )
        summed = term_value if summed is None else summed + term_value
    return summed


def identity_like(matrix_part):
    return jnp.eye(3, dtype=matrix_part.dtype).reshape((3, 3) + (1,) * (matrix_part.ndim - 2))


def traceless_anti(matrix):
    anti_real = 0.5 * (matrix[0] - swapped(matrix[0]))
    anti_imag = 0.5 * (matrix[1] + swapped(matrix[1]))
    trace_third = (anti_imag[0, 0] + anti_imag[1, 1] + anti_imag[2, 2]) / 3.0
    anti_imag = anti_imag - identity_like(anti_imag) * trace_third[None, None]
    return jnp.stack([anti_real, anti_imag])


def algebra(coeffs):
    zero_part = jnp.zeros_like(coeffs[0])
    diag_first = coeffs[2] + root_third * coeffs[7]
    diag_second = -coeffs[2] + root_third * coeffs[7]
    diag_third = -2.0 * root_third * coeffs[7]
    herm_real = jnp.stack(
        [
            jnp.stack([diag_first, coeffs[0], coeffs[3]]),
            jnp.stack([coeffs[0], diag_second, coeffs[5]]),
            jnp.stack([coeffs[3], coeffs[5], diag_third]),
        ]
    )
    herm_imag = jnp.stack(
        [
            jnp.stack([zero_part, -coeffs[1], -coeffs[4]]),
            jnp.stack([coeffs[1], zero_part, -coeffs[6]]),
            jnp.stack([coeffs[4], coeffs[6], zero_part]),
        ]
    )
    return 0.5 * jnp.stack([-herm_imag, herm_real])


def complex_times(first, second):
    return (
        first[0] * second[0] - first[1] * second[1],
        first[0] * second[1] + first[1] * second[0],
    )


def cayley(generator, matrix):
    shift_real = identity_like(generator[0]) - 0.5 * generator[0]
    shift_imag = -0.5 * generator[1]

    def element(row_index, col_index):
        return (shift_real[row_index % 3, col_index % 3], shift_imag[row_index % 3, col_index % 3])

    cofactor = []
    for row_index in range(3):
        cof_row = []
        for col_index in range(3):
            forward = complex_times(
                element(row_index + 1, col_index + 1), element(row_index + 2, col_index + 2)
            )
            backward = complex_times(
                element(row_index + 1, col_index + 2), element(row_index + 2, col_index + 1)
            )
            cof_row.append((forward[0] - backward[0], forward[1] - backward[1]))
        cofactor.append(cof_row)
    det_real = 0.0
    det_imag = 0.0
    for col_index in range(3):
        det_term = complex_times(element(0, col_index), cofactor[0][col_index])
        det_real = det_real + det_term[0]
        det_imag = det_imag + det_term[1]
    weight = 1.0 / (det_real * det_real + det_imag * det_imag)
    inverse_det = (det_real * weight, -det_imag * weight)
    rotation_real = []
    rotation_imag = []
    for row_index in range(3):
        real_row = []
        imag_row = []
        for col_index in range(3):
            inverse_entry = complex_times(cofactor[col_index][row_index], inverse_det)
            delta_value = 1.0 if row_index == col_index else 0.0
            real_row.append(2.0 * inverse_entry[0] - delta_value)
            imag_row.append(2.0 * inverse_entry[1])
        rotation_real.append(jnp.stack(real_row))
        rotation_imag.append(jnp.stack(imag_row))
    rotation = jnp.stack([jnp.stack(rotation_real), jnp.stack(rotation_imag)])
    return matrix_product(rotation, matrix)


def unit_step(direction):
    return tuple((1 if axis_number == direction else 0 for axis_number in range(4)))


def add_steps(first, second):
    return tuple((first_part + second_part for first_part, second_part in zip(first, second)))


def negate(offsets):
    return tuple((-part_value for part_value in offsets))


def staple_sum(fetcher, direction):
    summed = None
    resting = (0, 0, 0, 0)
    onward = unit_step(direction)
    for transverse in range(4):
        if transverse == direction:
            continue
        across = unit_step(transverse)
        upper_loop = matrix_product(
            matrix_product(fetcher(transverse, onward), dagger(fetcher(direction, across))),
            dagger(fetcher(transverse, resting)),
        )
        lower_loop = matrix_product(
            matrix_product(
                dagger(fetcher(transverse, add_steps(onward, negate(across)))),
                dagger(fetcher(direction, negate(across))),
            ),
            fetcher(transverse, negate(across)),
        )
        summed = upper_loop + lower_loop if summed is None else summed + upper_loop + lower_loop
    return summed


def updated_link(fetcher, direction, coeffs):
    current = fetcher(direction, (0, 0, 0, 0))
    force = traceless_anti(matrix_product(current, staple_sum(fetcher, direction)))
    generator = -step_drift * force + step_noise * algebra(coeffs)
    return cayley(generator, current)


def extend(lattice, top_slice):
    stacked = jnp.concatenate([lattice, top_slice], axis=4)
    widened = extended_2(stacked, (("sx", 5),), 1)
    return extended_2(widened, (("syz", 6),), SITES_ALONG_Z)


def pick_field(extended, z_coord, x_count, yz_count, link_dir, offsets):
    t_step, x_step, y_step, z_step = offsets
    portion = extended[link_dir]
    if t_step == 1:
        portion = portion[:, :, :, 1:]
    else:
        portion = portion[:, :, :, :-1]
        if t_step == -1:
            portion = jnp.roll(portion, 1, axis=3)
    portion = portion[:, :, :, :, 1 + x_step : 1 + x_step + x_count]
    offset = (1 + y_step) * SITES_ALONG_Z
    portion = portion[:, :, :, :, :, offset : offset + yz_count]
    if z_step == 1:
        portion = jnp.where(
            z_coord == SITES_ALONG_Z - 1,
            jnp.roll(portion, SITES_ALONG_Z - 1, axis=-1),
            jnp.roll(portion, -1, axis=-1),
        )
    if z_step == -1:
        portion = jnp.where(
            z_coord == 0,
            jnp.roll(portion, 1 - SITES_ALONG_Z, axis=-1),
            jnp.roll(portion, 1, axis=-1),
        )
    return portion


def last_links(windows, gauge_links, langevin_noise):
    time_count, x_count, yz_count = gauge_links.shape[4:]
    y_count = yz_count // SITES_ALONG_Z
    time_coord = lax.axis_index("slab") * time_count + jnp.arange(time_count)
    x_coord = lax.axis_index("sx") * x_count + jnp.arange(x_count)
    cell_index = jnp.arange(yz_count)
    z_coord = cell_index % SITES_ALONG_Z
    yz_coord = lax.axis_index("syz") * y_count + cell_index // SITES_ALONG_Z + z_coord
    parity = (time_coord[:, None, None] + x_coord[None, :, None] + yz_coord[None, None, :]) % 2
    interior = jnp.broadcast_to((jnp.arange(time_count) != 0)[:, None, None], parity.shape)
    own = jnp.repeat(windows[:, :, :, :, OWN, 32:96], 2, axis=-1)
    lattice = gauge_links
    for (direction, time), index in FIELD_OF.items():
        if time < time_count:
            value = jnp.where(parity[time] == 0, own[index, 0], own[index, 1])
            lattice = lattice.at[direction, :, :, :, time].set(
                value.reshape(2, 3, 3, x_count, yz_count)
            )
    above_face = shifted(gauge_links[1:, :, :, :, 0:1], "slab", -1)
    top_slice = jnp.concatenate(
        [jnp.zeros_like(gauge_links[0:1, :, :, :, 0:1]), above_face], axis=0
    )
    for direction in range(1, 4):
        kick_field = langevin_noise[SWEEPS - 1, direction].astype(jnp.float32)
        for colour in range(2):
            extended = extend(lattice, top_slice)
            fetcher = partial(pick_field, extended, z_coord, x_count, yz_count)
            candidate = updated_link(fetcher, direction, kick_field)
            chosen = jnp.logical_and(parity == colour, interior)
            lattice = lattice.at[direction].set(
                jnp.where(chosen, candidate, lattice[direction])
            )
    return lattice


def local(gauge_links, langevin_noise, separations):
    def buffers(ends):
        halves = tuple(pltpu.VMEM((ends[1], 8, 128), jnp.float32) for _ in range(4))
        return (pltpu.VMEM((2 * ends[0], 8, 128), jnp.float32), *halves)

    sets = (FIRST_PAIRS, SECOND_PAIRS, LATE_PAIRS, TURN_PAIRS, TURN2_PAIRS)
    vmem = pl.BlockSpec(memory_space=pltpu.VMEM)
    links = jnp.swapaxes(gauge_links, 4, 5)
    kicks = jnp.swapaxes(langevin_noise, 3, 4)
    win_shape = (len(FIELDS), 2, 2, 9, 8, 128)
    correlator, windows = pl.pallas_call(
        kernel,
        out_shape=(
            jax.ShapeDtypeStruct((3, 1, 128), jnp.float32),
            jax.ShapeDtypeStruct(win_shape, jnp.float32),
        ),
        in_specs=[
            pl.BlockSpec(memory_space=pltpu.HBM),
            pl.BlockSpec(memory_space=pltpu.HBM),
            pl.BlockSpec(memory_space=pltpu.HBM),
        ],
        out_specs=(vmem, pl.BlockSpec(memory_space=pltpu.HBM)),
        scratch_shapes=[
            pltpu.VMEM(links.shape, jnp.float32),
            pltpu.VMEM(kicks.shape, kicks.dtype),
            pltpu.SMEM(separations.shape, jnp.int32),
            pltpu.SemaphoreType.DMA((4,)),
        ]
        + [buffers(pairs) for pairs in sets] + [
            pltpu.VMEM(win_shape, jnp.float32),
            pltpu.VMEM((len(KICKS), 2, 8, 8, 128), jnp.float32),
            pltpu.VMEM((4, 2, 3, 3, 8, 128), jnp.float32),
            pltpu.VMEM((SWEEPS, 4, 2 * LINK, 8, 128), jnp.float32),
            pltpu.SemaphoreType.DMA((COPIES,)),
            pltpu.SemaphoreType.DMA((COPIES,)),
        ],
        compiler_params=pltpu.CompilerParams(
            collective_id=0, has_side_effects=True, vmem_limit_bytes=VMEM_LIMIT
        ),
    )(links, kicks, separations)
    last_links(windows, gauge_links, langevin_noise)
    return jnp.swapaxes(correlator, 0, 1) * (1.0 / SWEEPS**4)


def solution(mesh):
    return jax.shard_map(
        local,
        mesh=mesh,
        in_specs=(
            P(None, None, None, None, "slab", "sx", "syz"),
            P(None, None, None, "slab", "sx", "syz"),
            P(),
        ),
        out_specs=P("slab", "sx", "syz"),
        check_vma=False,
    )
```

```python
from functools import partial

import jax
import jax.numpy as jnp
from jax import lax
from jax.experimental import pallas as pl
from jax.experimental.pallas import tpu as pltpu
from jax.sharding import PartitionSpec as P

SITES_ALONG_Z = 32
SWEEPS = 2

step_drift = 0.2
step_noise = 0.4
root_third = 0.5773502691896258

MESH = pl.DeviceIdType.MESH
VMEM_LIMIT = 55168 * 1024

OWN = slice(2, 5)
FIELDS = ((0, 0), (0, 1), (1, 1), (2, 1), (3, 1), (1, 0), (2, 0), (3, 0), (1, 2), (2, 2), (3, 2))
FIELD_OF = {field: index for index, field in enumerate(FIELDS)}
KICKS = ((0, 0, 0), (0, 0, 1), (0, 1, 1), (0, 2, 1), (0, 3, 1), (1, 0, 0), (1, 0, 1))
KICK_OF = {kick: index for index, kick in enumerate(KICKS)}
LINK, KICK = 7, 4


def size(entry):
    return LINK if len(entry) == 2 else KICK


def placed(*groups):
    places, x_end, y_end = {}, 0, 0
    for group in groups:
        members = group if isinstance(group[0], tuple) else (group,)
        for half, entry in enumerate(members):
            places[entry] = (x_end, y_end, half)
            x_end += size(entry)
        y_end += size(members[0])
    return places, (x_end, y_end)


FIRST_GROUPS = ((0, 0), (0, 0, 0), (2, 0), ((3, 0), (1, 0)), ((1, 1), (3, 1)), (2, 1))
FROZEN_GROUPS = ((2, 2), ((3, 2), (1, 2)))
SECOND_GROUPS = ((0, 1), ((0, 0, 1), (0, 1, 1)))
LATE_GROUPS = (((0, 2, 1), (0, 3, 1)), ((1, 0, 0), (1, 0, 1)))
FIRST, FIRST_PAIRS = placed(*FIRST_GROUPS)
SECOND, SECOND_PAIRS = placed(*FROZEN_GROUPS, *SECOND_GROUPS)
LATE, LATE_PAIRS = placed(*LATE_GROUPS)
TURN, TURN_PAIRS = placed((0, 0), (0, 1), (1, 1))
TURN2, TURN2_PAIRS = placed((1, 1), (2, 1), (3, 1))
FIRST_ROWS = {
    (0, 0): (2, 2, 1, 1, 1, 1),
    (0, 0, 0): (1, 1, 0, 0, 1, 1),
    (2, 0): (1, 1, 1, 0, 1, 1),
    (3, 0): (1, 1, 0, 0, 1, 1),
    (1, 0): (2, 1, 2, 2, 1, 1),
    (1, 1): (2, 2, 1, 1, 1, 1),
    (3, 1): (2, 2, 2, 2, 2, 2),
    (2, 1): (2, 2, 2, 2, 2, 2),
}
FROZEN_ROWS = {
    (2, 2): (1, 2, 1, 0, 2, 1),
    (3, 2): (1, 2, 0, 0, 1, 1),
    (1, 2): (2, 2, 2, 2, 1, 1),
}
SECOND_ROWS = {
    (0, 1): (2, 3, 1, 1, 2, 2),
    (0, 0, 1): (1, 2, 0, 0, 1, 1),
    (0, 1, 1): (2, 1, 2, 2, 1, 1),
}
LATE_ROWS = {
    (0, 2, 1): (1, 1, 1, 0, 1, 0),
    (0, 3, 1): (1, 1, 0, 0, 0, 0),
    (1, 0, 0): (1, 1, 0, 0, 0, 0),
    (1, 0, 1): (1, 1, 0, 0, 0, 0),
}
TURN_ROWS = {
    (0, 0): (2, 2, 2, 2, 2, 2),
    (0, 1): (2, 2, 2, 2, 2, 2),
    (1, 1): (2, 1, 2, 2, 1, 1),
}
TURN2_ROWS = {
    (1, 1): (2, 1, 1, 1, 0, 0),
    (2, 1): (1, 1, 1, 0, 1, 0),
    (3, 1): (2, 2, 1, 1, 1, 1),
}
FACES = tuple((dx, dy) for dx in (-1, 0, 1) for dy in (-1, 0, 1))
FACES = tuple(sorted(FACES, key=lambda face: -abs(face[0]) - abs(face[1])))
RING = tuple(face for face in FACES if face != (0, 0))


def runs(places, rows, face):
    dx, dy = face
    found = {}
    for entry, needed in rows.items():
        if dx == 0:
            count = 3
        elif dy == 0:
            count = needed[0 if dx == 1 else 1]
        else:
            count = needed[(2 if dx == 1 else 4) + (0 if dy == 1 else 1)]
        low = places[entry][0 if dy == 0 else 1]
        high = low + size(entry)
        found[low] = (high, max(count, found.get(low, (0, 0))[1]))
    merged = []
    for low, (high, count) in sorted(found.items()):
        if not count:
            continue
        if merged and merged[-1][1:] == (low, count):
            merged[-1] = (merged[-1][0], high, count)
        else:
            merged.append((low, high, count))
    return merged


def count_of(places, rows, faces):
    return sum(len(runs(places, rows, face)) for face in faces)


COPIES = (
    count_of(FIRST, FIRST_ROWS, RING)
    + 3
    + count_of(SECOND, FROZEN_ROWS, RING)
    + count_of(SECOND, SECOND_ROWS, RING)
    + count_of(LATE, LATE_ROWS, RING)
    + sum(count_of(TURN, {entry: TURN_ROWS[entry]}, RING) for entry in TURN)
    + sum(count_of(TURN2, {entry: TURN2_ROWS[entry]}, RING) for entry in TURN2)
    + 7 * SWEEPS
)


def rows_sent(dx, count):
    if dx == 1:
        return pl.ds(5 - count, count), pl.ds(2 - count, count)
    if dx == -1:
        return pl.ds(2, count), pl.ds(5, count)
    return pl.ds(2, 3), pl.ds(2, 3)


def mm(a, b):
    real = imag = None
    for k in range(3):
        ar, ai = a[0][:, k][:, None], a[1][:, k][:, None]
        br, bi = b[0][k][None], b[1][k][None]
        re, im = ar * br - ai * bi, ar * bi + ai * br
        real, imag = (re, im) if real is None else (real + re, imag + im)
    return real, imag


def mm_nh(a, b):
    real = imag = None
    for k in range(3):
        ar, ai = a[0][:, k][:, None], a[1][:, k][:, None]
        br, bi = b[0][:, k][None], b[1][:, k][None]
        re, im = ar * br + ai * bi, ai * br - ar * bi
        real, imag = (re, im) if real is None else (real + re, imag + im)
    return real, imag


def mm_hn(a, b):
    real = imag = None
    for k in range(3):
        ar, ai = a[0][k][:, None], a[1][k][:, None]
        br, bi = b[0][k][None], b[1][k][None]
        re, im = ar * br + ai * bi, ar * bi - ai * br
        real, imag = (re, im) if real is None else (real + re, imag + im)
    return real, imag


def times(a, b):
    return a[0] * b[0] - a[1] * b[1], a[0] * b[1] + a[1] * b[0]


def conj_times(a, b):
    return a[0] * b[0] + a[1] * b[1], a[0] * b[1] - a[1] * b[0]


def add(a, b):
    return a[0] + b[0], a[1] + b[1]


def cross(re, im):
    entry = [(re[k], im[k]) for k in range(6)]
    found = []
    for j in range(3):
        k, m = (j + 1) % 3, (j + 2) % 3
        one, two = times(entry[k], entry[3 + m]), times(entry[m], entry[3 + k])
        found.append((one[0] - two[0], one[1] - two[1]))
    return found


def compress(re, im):
    terms = [times((re[6 + j], im[6 + j]), value) for j, value in enumerate(cross(re, im))]
    phase = add(add(terms[0], terms[1]), terms[2])
    return (
        jnp.concatenate([re[0:6], phase[0][None]], axis=0),
        jnp.concatenate([im[0:6], phase[1][None]], axis=0),
    )


def restore(re, im):
    third = [conj_times(value, (re[6], im[6])) for value in cross(re, im)]
    return (
        jnp.concatenate([re[0:6], jnp.stack([value[0] for value in third])], axis=0),
        jnp.concatenate([im[0:6], jnp.stack([value[1] for value in third])], axis=0),
    )


def rotated(product, noise, link):
    mr, mi = product
    n = noise
    drift = 0.25 * step_drift
    kick = 0.25 * step_noise

    def off(i, j, nr, ni):
        return (
            kick * nr - drift * (mr[i, j] - mr[j, i]),
            kick * ni - drift * (mi[i, j] + mi[j, i]),
        )

    p = off(0, 1, n[1], n[0])
    q = off(0, 2, n[4], n[3])
    r = off(1, 2, n[6], n[5])
    third = (mi[0, 0] + mi[1, 1] + mi[2, 2]) / 3.0
    eighth = root_third * n[7]
    a = kick * (eighth + n[2]) - 2.0 * drift * (mi[0, 0] - third)
    b = kick * (eighth - n[2]) - 2.0 * drift * (mi[1, 1] - third)
    c = -(a + b)
    pp = p[0] * p[0] + p[1] * p[1]
    qq = q[0] * q[0] + q[1] * q[1]
    rr = r[0] * r[0] + r[1] * r[1]
    bc, ac, ab = b * c, a * c, a * b
    pr = times(p, r)
    real = 1.0 + (pp + qq + rr) - (ab + ac + bc)
    odd = a * rr + b * qq + c * pp - a * bc - 2.0 * (pr[1] * q[0] - pr[0] * q[1])
    weight = 2.0 / (real * real + odd * odd)
    inv = (real * weight, odd * weight)
    rs = conj_times(r, q)
    ps = conj_times(p, q)
    s01 = (c * p[1] - rs[0], -c * p[0] - rs[1])
    s02 = (b * q[1] + pr[0], pr[1] - b * q[0])
    s12 = (a * r[1] - ps[0], -a * r[0] - ps[1])
    adj = [
        [(1.0 + rr - bc, a), add(s01, p), add(s02, q)],
        [(s01[0] - p[0], p[1] - s01[1]), (1.0 + qq - ac, b), add(s12, r)],
        [(s02[0] - q[0], q[1] - s02[1]), (s12[0] - r[0], r[1] - s12[1]), (1.0 + pp - ab, c)],
    ]
    rotation = [[times(entry, inv) for entry in row] for row in adj]
    for i in range(3):
        rotation[i][i] = (rotation[i][i][0] - 1.0, rotation[i][i][1])
    stacked = tuple(
        jnp.stack([jnp.stack([entry[part] for entry in row]) for row in rotation])
        for part in range(2)
    )
    return mm(stacked, link)


def kernel(
    links_hbm, kicks_hbm, separations_hbm, out, windows,
    links, kicks, separations, fetch_sem, first_set, second_set, late_set, turn_set, turn2_set,
    win, kwin, held, lines, send_sem, recv_sem,
):
    slabs, sxs, syzs = (lax.axis_size(axis) for axis in ("slab", "sx", "syz"))
    slab, sx, syz = (lax.axis_index(axis) for axis in ("slab", "sx", "syz"))

    def peer(ds, dx, dy):
        return (
            lax.rem(slab + ds + slabs, slabs),
            lax.rem(sx + dx + sxs, sxs),
            lax.rem(syz + dy + syzs, syzs),
        )

    peers = [(0, *face) for face in RING] + [(1, 0, 0)]
    barrier = pltpu.get_barrier_semaphore()
    for one in peers:
        pl.semaphore_signal(barrier, inc=1, device_id=peer(*one), device_id_type=MESH)

    fetches = [
        pltpu.make_async_copy(links_hbm, links, fetch_sem.at[0]),
        pltpu.make_async_copy(kicks_hbm, kicks, fetch_sem.at[1]),
        pltpu.make_async_copy(separations_hbm, separations, fetch_sem.at[2]),
    ]
    for fetch in fetches:
        fetch.start()
    started = []

    def send(src, dst, target):
        index = len(started)
        copy = pltpu.make_async_remote_copy(
            src_ref=src,
            dst_ref=dst,
            send_sem=send_sem.at[index],
            recv_sem=recv_sem.at[index],
            device_id=peer(*target),
            device_id_type=MESH,
        )
        copy.start()
        started.append(copy)
        return copy

    shape = (8, 128)
    lane = lax.broadcasted_iota(jnp.int32, shape, 1)
    row = lax.broadcasted_iota(jnp.int32, shape, 0)
    half = lane % 16
    quarter = lane // 32
    low_half = lane < 64
    middle = jnp.logical_and(lane >= 32, lane < 96)
    first_of_half = (lane % 64) < 32
    odd_site = (sx * 3 + row + lane // 16) % 2
    is_odd = [odd_site == 1, odd_site == 0]
    last_half, first_half = half == 15, half == 0

    def own_index(time):
        lane3 = lax.broadcasted_iota(jnp.int32, (3, 128), 1)
        row3 = lax.broadcasted_iota(jnp.int32, (3, 128), 0)
        y = (lane3 % 64) // 16
        bit = (time + sx * 3 + row3 + y + lane3 // 64) % 2
        return y * 32 + (lane3 % 16) * 2 + bit

    own_gather = [own_index(0), own_index(1)]

    first3 = first_of_half[0:3]
    second3 = (lane[0:3] % 32) >= 16

    def put(bufs, places, *entries):
        x_buf, p_buf, m_buf = bufs[:3]
        upper, lower = [], []
        for entry, first, second in entries:
            x, y, _ = places[entry]
            count = size(entry)
            rolled = pltpu.roll(first, 96, 2)
            x_buf[2 * x : 2 * x + count, OWN] = first
            x_buf[2 * x + count : 2 * x + 2 * count, OWN] = second
            upper.append(jnp.where(first3, rolled, second))
            lower.append(jnp.where(first3, second, rolled))
        if len(entries) == 2:
            upper = [jnp.where(second3, upper[0], pltpu.roll(upper[1], 112, 2))]
            lower = [jnp.where(second3, pltpu.roll(lower[1], 16, 2), lower[0])]
        p_buf[y : y + count, OWN] = upper[0]
        m_buf[y : y + count, OWN] = lower[0]

    def spread(bufs, places, rows):
        copies = []
        for face in RING:
            for low, high, count in runs(places, rows, face):
                dx, dy = face
                out_rows, in_rows = rows_sent(dx, count)
                if dy == 0:
                    src = dst = bufs[0]
                    low, high = 2 * low, 2 * high
                else:
                    src, dst = (bufs[1], bufs[3]) if dy == 1 else (bufs[2], bufs[4])
                copies.append(
                    send(
                        src.at[pl.ds(low, high - low), out_rows],
                        dst.at[pl.ds(low, high - low), in_rows],
                        (0, dx, dy),
                    )
                )
        return copies

    def assemble(bufs, place, count):
        x_buf, _, _, lo_buf, hi_buf = bufs
        x, y, second = place
        lo, hi = lo_buf[y : y + count], hi_buf[y : y + count]
        if second:
            lo, hi = pltpu.roll(lo, 16, 2), pltpu.roll(hi, 112, 2)
        found = [[None, None], [None, None]]
        for member in range(2):
            start = 2 * x + member * count
            own = x_buf[start : start + count]
            for parity in range(2):
                q = 2 * parity + member
                edge = jnp.where(quarter == q, lo, hi)
                if q:
                    edge = pltpu.roll(edge, 128 - 32 * q, 2)
                centre = pltpu.roll(own, 32 if parity == 0 else 96, 2)
                found[parity][member] = jnp.where(middle, centre, edge)
        return found

    def take_in(bufs, places, entries):
        for entry in entries:
            if len(entry) == 2:
                found = assemble(bufs, places[entry], LINK)
                for parity in range(2):
                    for part, value in enumerate(restore(*found[parity])):
                        win[FIELD_OF[entry], parity, part] = value
            else:
                found = assemble(bufs, places[entry], KICK)
                for parity in range(2):
                    for member in range(2):
                        kwin[KICK_OF[entry], parity, 4 * member : 4 * member + 4] = found[parity][member]

    def packed(parts, time):
        return jnp.stack([jnp.take_along_axis(part, own_gather[time], axis=1) for part in parts])

    def pack(bufs, places, groups):
        for group in groups:
            members = []
            for entry in group if isinstance(group[0], tuple) else (group,):
                if len(entry) == 2:
                    direction, time = entry
                    whole = [
                        packed(
                            [
                                links[direction, part, i, j, :, time]
                                for i in range(3)
                                for j in range(3)
                            ],
                            time,
                        )
                        for part in range(2)
                    ]
                    members.append((entry, *compress(*whole)))
                else:
                    sweep, direction, time = entry
                    parts = [
                        kicks[sweep, direction, a, :, time].astype(jnp.float32) for a in range(8)
                    ]
                    members.append((entry, packed(parts[:4], time), packed(parts[4:], time)))
            put(bufs, places, *members)

    def wait(copies):
        for copy in copies:
            copy.wait_recv()

    for fetch in fetches:
        fetch.wait()
    pack(first_set, FIRST, FIRST_GROUPS)
    pl.semaphore_wait(barrier, len(peers))

    frozen_copies = []
    for k in range(3):
        low, high = FIRST[2, 0][min(k, 1)], FIRST[1, 0][min(k, 1)] + LINK
        goal = SECOND[2, 2][min(k, 1)]
        if k == 0:
            low, high, goal = 2 * low, 2 * high, 2 * goal
        frozen_copies.append(
            send(
                first_set[k].at[pl.ds(low, high - low), pl.ds(2, 3)],
                second_set[k].at[pl.ds(goal, high - low), pl.ds(2, 3)],
                (-1, 0, 0),
            )
        )
    first_copies = spread(first_set, FIRST, FIRST_ROWS)
    pack(second_set, SECOND, SECOND_GROUPS)
    second_copies = spread(second_set, SECOND, SECOND_ROWS)
    pack(late_set, LATE, LATE_GROUPS)
    wait(frozen_copies)
    second_copies += spread(second_set, SECOND, FROZEN_ROWS)
    late_copies = spread(late_set, LATE, LATE_ROWS)

    def shifted(pair, axis, sign, time, parity):
        def one(value):
            if axis == 0:
                return value
            flat = value.reshape(9, 8, 128)
            if axis == 1:
                flat = pltpu.roll(flat, 7 if sign == 1 else 1, 1)
            elif axis == 2:
                flat = pltpu.roll(flat, 112 if sign == 1 else 16, 2)
            else:
                odd = is_odd[(time + parity) % 2]
                if sign == 1:
                    inner = jnp.where(last_half, pltpu.roll(flat, 15, 2), pltpu.roll(flat, 127, 2))
                    flat = jnp.where(odd, inner, flat)
                else:
                    inner = jnp.where(first_half, pltpu.roll(flat, 113, 2), pltpu.roll(flat, 1, 2))
                    flat = jnp.where(odd, flat, inner)
            return flat.reshape(3, 3, 8, 128)

        return one(pair[0]), one(pair[1])

    def link(direction, time, parity):
        field = FIELD_OF[direction, time]
        return tuple(win[field, parity, part].reshape(3, 3, 8, 128) for part in range(2))

    def staples(mu, time, parity, planes):
        total = None
        other = 1 - parity
        for nu in planes:
            if mu == 0:
                ahead = link(nu, time + 1, other)
                ahead_low = link(nu, time + 1, parity)
            else:
                ahead = shifted(link(nu, time, other), mu, 1, time, parity)
            if nu == 0:
                above, below = link(mu, time + 1, other), link(mu, time - 1, other)
                low_time = time - 1
            else:
                above = shifted(link(mu, time, other), nu, 1, time, parity)
                below = link(mu, time, other)
                low_time = time
            if mu != 0:
                ahead_low = shifted(
                    link(nu, low_time, parity), mu, 1, low_time, other
                )
            upper = mm_nh(mm_nh(ahead, above), link(nu, time, parity))
            lower = mm_hn(mm(below, ahead_low), link(nu, low_time, other))
            lower = shifted(lower, nu, -1, time, parity)
            both = add(upper, lower)
            total = both if total is None else add(total, both)
        return total

    def ahead_of(slot, mu, time, parity, planes):
        for part, value in enumerate(staples(mu, time, parity, planes)):
            held[slot, part] = value

    def substep(sweep, mu, parity, time=1, slot=None, done=()):
        current = link(mu, time, parity)
        noise = kwin[KICK_OF[sweep, mu, time], parity]
        planes = [nu for nu in range(4) if nu != mu and nu not in done]
        total = staples(mu, time, parity, planes)
        if done:
            total = add(total, (held[slot, 0], held[slot, 1]))
        new = rotated(mm(current, total), noise, current)
        field = FIELD_OF[mu, time]
        for part in range(2):
            win[field, parity, part] = new[part].reshape(9, 8, 128)

    def own_part(two):
        return jnp.where(low_half, pltpu.roll(two[0], 96, 2), pltpu.roll(two[1], 32, 2))

    def pass_on(bufs, places, rows, entry):
        whole = [
            own_part([win[FIELD_OF[entry], parity, part] for parity in range(2)])[:, OWN]
            for part in range(2)
        ]
        put(bufs, places, (entry, *compress(*whole)))
        return spread(bufs, places, {entry: rows[entry]})

    def measure(sweep):
        products = [mm(link(0, 0, parity), link(0, 1, 1 - parity)) for parity in range(2)]
        whole = [
            own_part([product[part].reshape(9, 8, 128) for product in products])[:, OWN]
            for part in range(2)
        ]
        for part, value in enumerate(compress(*whole)):
            lines[sweep, 0, LINK * part : LINK * part + LINK, 0:3] = value
    def hand_lines(sweep, slabs_below):
        copies = {}
        src = lines.at[sweep, 0, :, pl.ds(0, 3)]
        for ds in slabs_below:
            copies[ds, 1] = send(src, lines.at[sweep, ds, :, pl.ds(3, 3)], (-ds, -1, 0))
        for ds in slabs_below:
            if ds:
                copies[ds, 0] = send(src, lines.at[sweep, ds, :, pl.ds(0, 3)], (-ds, 0, 0))
        return copies

    wait(first_copies)
    take_in(first_set, FIRST, FIRST)
    substep(0, 0, 0, 0)
    substep(0, 0, 1, 0)
    turn_first = pass_on(turn_set, TURN, TURN_ROWS, (0, 0))
    ahead_of(1, 1, 1, 0, (2, 3))
    wait(second_copies)
    take_in(second_set, SECOND, SECOND)
    substep(0, 0, 0, 1)
    substep(0, 0, 1, 1)
    turn_first += pass_on(turn_set, TURN, TURN_ROWS, (0, 1))
    substep(0, 1, 0, 1, 1, (2, 3))
    turn_last = pass_on(turn_set, TURN, TURN_ROWS, (1, 1))
    measure(0)
    line_copies = hand_lines(0, (1, 3, 0))
    ahead_of(0, 2, 1, 0, (3,))
    wait(late_copies)
    take_in(late_set, LATE, LATE)
    wait(turn_first)
    take_in(turn_set, TURN, ((0, 0), (0, 1)))
    ahead_of(1, 1, 1, 1, (0,))
    ahead_of(2, 2, 1, 1, (0,))
    ahead_of(3, 3, 1, 0, (0,))
    wait(turn_last)
    take_in(turn_set, TURN, ((1, 1),))
    substep(0, 1, 1, 1, 1, (0,))
    turn_first = pass_on(turn2_set, TURN2, TURN2_ROWS, (1, 1))
    substep(0, 2, 0, 1, 0, (3,))
    substep(0, 2, 1, 1, 2, (0,))
    turn_first += pass_on(turn2_set, TURN2, TURN2_ROWS, (2, 1))
    substep(0, 3, 0, 1, 3, (0,))
    turn_last = pass_on(turn2_set, TURN2, TURN2_ROWS, (3, 1))
    ahead_of(0, 3, 1, 1, (0,))
    wait([line_copies.pop((3, 0))])
    line_copies.update(hand_lines(0, (2,)))
    wait(turn_first)
    take_in(turn2_set, TURN2, ((1, 1), (2, 1)))
    ahead_of(1, 0, 0, 0, (1, 2))
    ahead_of(2, 0, 1, 0, (1, 2))
    wait(turn_last)
    take_in(turn2_set, TURN2, ((3, 1),))
    substep(0, 3, 1, 1, 0, (0,))
    for time in range(2):
        substep(1, 0, 0, time, 1 + time, (1, 2))
        substep(1, 0, 1, time)
    measure(1)
    last_copies = hand_lines(1, (2, 1, 3, 0))
    keep = pltpu.make_async_copy(win, windows, fetch_sem.at[3])
    keep.start()

    def line(sweep, ds):
        whole = restore(lines[sweep, ds, 0:LINK], lines[sweep, ds, LINK : 2 * LINK])
        return tuple(part.reshape(3, 3, 8, 128) for part in whole)

    wait(line_copies.values())
    line_of = [[line(0, ds) for ds in range(4)]]
    low, high = {(0, 0): mm(line_of[0][0], line_of[0][1])}, {(0, 0): mm(line_of[0][2], line_of[0][3])}
    wait(last_copies.values())
    line_of.append([line(1, ds) for ds in range(4)])
    for pick in ((0, 1), (1, 0), (1, 1)):
        low[pick] = mm(line_of[pick[0]][0], line_of[pick[1]][1])
        high[pick] = mm(line_of[pick[0]][2], line_of[pick[1]][3])
    loops = []
    for left in low.values():
        for right in high.values():
            rr, ri = (jnp.swapaxes(part, 0, 1) for part in right)
            loops.append(jnp.sum((left[0] * rr - left[1] * ri).reshape(9, 8, 128), axis=0))
            loops.append(jnp.sum((left[0] * ri + left[1] * rr).reshape(9, 8, 128), axis=0))
    loops = jnp.stack(loops)
    distance = separations[slab]
    result = None
    for r in (3, 2, 1):
        far = pltpu.roll(loops, 8 - r, 1)
        if r % 2:
            far = pltpu.roll(far, 64, 2)
        value = jnp.sum(loops * far, axis=0)
        result = value if result is None else jnp.where(distance == r, value, result)
    lane3 = lax.broadcasted_iota(jnp.int32, (3, 128), 1)
    row3 = lax.broadcasted_iota(jnp.int32, (3, 128), 0)
    y, z = lane3 // 32, lane3 % 32
    index = ((z + y + row3 + sx * 3) % 2) * 64 + y * 16 + z // 2
    out[:, 0] = jnp.take_along_axis(result[0:3], index, axis=1)

    keep.wait()
    for copy in started:
        copy.wait_send()


def extended_2(block, sides, width):
    for axis, dim in sides:
        count = lax.axis_size(axis)
        forward = [(i, i + 1) for i in range(count - 1)]
        forward.append((count - 1, 0))
        backward = [(target, source) for source, target in forward]
        low = lax.ppermute(
            lax.slice_in_dim(block, block.shape[dim] - width, None, axis=dim), axis, forward
        )
        high = lax.ppermute(lax.slice_in_dim(block, 0, width, axis=dim), axis, backward)
        block = jnp.concatenate([low, block, high], axis=dim)
    return block


def shifted(block, axis, distance):
    devices = range(lax.axis_size(axis))
    route = [((i - distance) % len(devices), i) for i in devices]
    return lax.ppermute(block, axis, route)


def swapped(matrix_part):
    return jnp.swapaxes(matrix_part, 0, 1)


def dagger(matrix):
    return jnp.stack([swapped(matrix[0]), -swapped(matrix[1])])


def matrix_product(first, second):
    summed = None
    for middle in range(first.shape[1]):
        first_real = first[0][:, middle][:, None]
        first_imag = first[1][:, middle][:, None]
        second_real = second[0][middle][None]
        second_imag = second[1][middle][None]
        term_value = jnp.stack(
            [
                first_real * second_real - first_imag * second_imag,
                first_real * second_imag + first_imag * second_real,
            ]
        )
        summed = term_value if summed is None else summed + term_value
    return summed


def identity_like(matrix_part):
    return jnp.eye(3, dtype=matrix_part.dtype).reshape((3, 3) + (1,) * (matrix_part.ndim - 2))


def traceless_anti(matrix):
    anti_real = 0.5 * (matrix[0] - swapped(matrix[0]))
    anti_imag = 0.5 * (matrix[1] + swapped(matrix[1]))
    trace_third = (anti_imag[0, 0] + anti_imag[1, 1] + anti_imag[2, 2]) / 3.0
    anti_imag = anti_imag - identity_like(anti_imag) * trace_third[None, None]
    return jnp.stack([anti_real, anti_imag])


def algebra(coeffs):
    zero_part = jnp.zeros_like(coeffs[0])
    diag_first = coeffs[2] + root_third * coeffs[7]
    diag_second = -coeffs[2] + root_third * coeffs[7]
    diag_third = -2.0 * root_third * coeffs[7]
    herm_real = jnp.stack(
        [
            jnp.stack([diag_first, coeffs[0], coeffs[3]]),
            jnp.stack([coeffs[0], diag_second, coeffs[5]]),
            jnp.stack([coeffs[3], coeffs[5], diag_third]),
        ]
    )
    herm_imag = jnp.stack(
        [
            jnp.stack([zero_part, -coeffs[1], -coeffs[4]]),
            jnp.stack([coeffs[1], zero_part, -coeffs[6]]),
            jnp.stack([coeffs[4], coeffs[6], zero_part]),
        ]
    )
    return 0.5 * jnp.stack([-herm_imag, herm_real])


def complex_times(first, second):
    return (
        first[0] * second[0] - first[1] * second[1],
        first[0] * second[1] + first[1] * second[0],
    )


def cayley(generator, matrix):
    shift_real = identity_like(generator[0]) - 0.5 * generator[0]
    shift_imag = -0.5 * generator[1]

    def element(row_index, col_index):
        return (shift_real[row_index % 3, col_index % 3], shift_imag[row_index % 3, col_index % 3])

    cofactor = []
    for row_index in range(3):
        cof_row = []
        for col_index in range(3):
            forward = complex_times(
                element(row_index + 1, col_index + 1), element(row_index + 2, col_index + 2)
            )
            backward = complex_times(
                element(row_index + 1, col_index + 2), element(row_index + 2, col_index + 1)
            )
            cof_row.append((forward[0] - backward[0], forward[1] - backward[1]))
        cofactor.append(cof_row)
    det_real = 0.0
    det_imag = 0.0
    for col_index in range(3):
        det_term = complex_times(element(0, col_index), cofactor[0][col_index])
        det_real = det_real + det_term[0]
        det_imag = det_imag + det_term[1]
    weight = 1.0 / (det_real * det_real + det_imag * det_imag)
    inverse_det = (det_real * weight, -det_imag * weight)
    rotation_real = []
    rotation_imag = []
    for row_index in range(3):
        real_row = []
        imag_row = []
        for col_index in range(3):
            inverse_entry = complex_times(cofactor[col_index][row_index], inverse_det)
            delta_value = 1.0 if row_index == col_index else 0.0
            real_row.append(2.0 * inverse_entry[0] - delta_value)
            imag_row.append(2.0 * inverse_entry[1])
        rotation_real.append(jnp.stack(real_row))
        rotation_imag.append(jnp.stack(imag_row))
    rotation = jnp.stack([jnp.stack(rotation_real), jnp.stack(rotation_imag)])
    return matrix_product(rotation, matrix)


def unit_step(direction):
    return tuple((1 if axis_number == direction else 0 for axis_number in range(4)))


def add_steps(first, second):
    return tuple((first_part + second_part for first_part, second_part in zip(first, second)))


def negate(offsets):
    return tuple((-part_value for part_value in offsets))


def staple_sum(fetcher, direction):
    summed = None
    resting = (0, 0, 0, 0)
    onward = unit_step(direction)
    for transverse in range(4):
        if transverse == direction:
            continue
        across = unit_step(transverse)
        upper_loop = matrix_product(
            matrix_product(fetcher(transverse, onward), dagger(fetcher(direction, across))),
            dagger(fetcher(transverse, resting)),
        )
        lower_loop = matrix_product(
            matrix_product(
                dagger(fetcher(transverse, add_steps(onward, negate(across)))),
                dagger(fetcher(direction, negate(across))),
            ),
            fetcher(transverse, negate(across)),
        )
        summed = upper_loop + lower_loop if summed is None else summed + upper_loop + lower_loop
    return summed


def updated_link(fetcher, direction, coeffs):
    current = fetcher(direction, (0, 0, 0, 0))
    force = traceless_anti(matrix_product(current, staple_sum(fetcher, direction)))
    generator = -step_drift * force + step_noise * algebra(coeffs)
    return cayley(generator, current)


def extend(lattice, top_slice):
    stacked = jnp.concatenate([lattice, top_slice], axis=4)
    widened = extended_2(stacked, (("sx", 5),), 1)
    return extended_2(widened, (("syz", 6),), SITES_ALONG_Z)


def pick_field(extended, z_coord, x_count, yz_count, link_dir, offsets):
    t_step, x_step, y_step, z_step = offsets
    portion = extended[link_dir]
    if t_step == 1:
        portion = portion[:, :, :, 1:]
    else:
        portion = portion[:, :, :, :-1]
        if t_step == -1:
            portion = jnp.roll(portion, 1, axis=3)
    portion = portion[:, :, :, :, 1 + x_step : 1 + x_step + x_count]
    offset = (1 + y_step) * SITES_ALONG_Z
    portion = portion[:, :, :, :, :, offset : offset + yz_count]
    if z_step == 1:
        portion = jnp.where(
            z_coord == SITES_ALONG_Z - 1,
            jnp.roll(portion, SITES_ALONG_Z - 1, axis=-1),
            jnp.roll(portion, -1, axis=-1),
        )
    if z_step == -1:
        portion = jnp.where(
            z_coord == 0,
            jnp.roll(portion, 1 - SITES_ALONG_Z, axis=-1),
            jnp.roll(portion, 1, axis=-1),
        )
    return portion


def last_links(windows, gauge_links, langevin_noise):
    time_count, x_count, yz_count = gauge_links.shape[4:]
    y_count = yz_count // SITES_ALONG_Z
    time_coord = lax.axis_index("slab") * time_count + jnp.arange(time_count)
    x_coord = lax.axis_index("sx") * x_count + jnp.arange(x_count)
    cell_index = jnp.arange(yz_count)
    z_coord = cell_index % SITES_ALONG_Z
    yz_coord = lax.axis_index("syz") * y_count + cell_index // SITES_ALONG_Z + z_coord
    parity = (time_coord[:, None, None] + x_coord[None, :, None] + yz_coord[None, None, :]) % 2
    interior = jnp.broadcast_to((jnp.arange(time_count) != 0)[:, None, None], parity.shape)
    own = jnp.repeat(windows[:, :, :, :, OWN, 32:96], 2, axis=-1)
    lattice = gauge_links
    for (direction, time), index in FIELD_OF.items():
        if time < time_count:
            value = jnp.where(parity[time] == 0, own[index, 0], own[index, 1])
            lattice = lattice.at[direction, :, :, :, time].set(
                value.reshape(2, 3, 3, x_count, yz_count)
            )
    above_face = shifted(gauge_links[1:, :, :, :, 0:1], "slab", -1)
    top_slice = jnp.concatenate(
        [jnp.zeros_like(gauge_links[0:1, :, :, :, 0:1]), above_face], axis=0
    )
    for direction in range(1, 4):
        kick_field = langevin_noise[SWEEPS - 1, direction].astype(jnp.float32)
        for colour in range(2):
            extended = extend(lattice, top_slice)
            fetcher = partial(pick_field, extended, z_coord, x_count, yz_count)
            candidate = updated_link(fetcher, direction, kick_field)
            chosen = jnp.logical_and(parity == colour, interior)
            lattice = lattice.at[direction].set(
                jnp.where(chosen, candidate, lattice[direction])
            )
    return lattice


def local(gauge_links, langevin_noise, separations):
    def buffers(ends):
        halves = tuple(pltpu.VMEM((ends[1], 8, 128), jnp.float32) for _ in range(4))
        return (pltpu.VMEM((2 * ends[0], 8, 128), jnp.float32), *halves)

    sets = (FIRST_PAIRS, SECOND_PAIRS, LATE_PAIRS, TURN_PAIRS, TURN2_PAIRS)
    vmem = pl.BlockSpec(memory_space=pltpu.VMEM)
    links = jnp.swapaxes(gauge_links, 4, 5)
    kicks = jnp.swapaxes(langevin_noise, 3, 4)
    win_shape = (len(FIELDS), 2, 2, 9, 8, 128)
    correlator, windows = pl.pallas_call(
        kernel,
        out_shape=(
            jax.ShapeDtypeStruct((3, 1, 128), jnp.float32),
            jax.ShapeDtypeStruct(win_shape, jnp.float32),
        ),
        in_specs=[
            pl.BlockSpec(memory_space=pltpu.HBM),
            pl.BlockSpec(memory_space=pltpu.HBM),
            pl.BlockSpec(memory_space=pltpu.HBM),
        ],
        out_specs=(vmem, pl.BlockSpec(memory_space=pltpu.HBM)),
        scratch_shapes=[
            pltpu.VMEM(links.shape, jnp.float32),
            pltpu.VMEM(kicks.shape, kicks.dtype),
            pltpu.SMEM(separations.shape, jnp.int32),
            pltpu.SemaphoreType.DMA((4,)),
        ]
        + [buffers(pairs) for pairs in sets] + [
            pltpu.VMEM(win_shape, jnp.float32),
            pltpu.VMEM((len(KICKS), 2, 8, 8, 128), jnp.float32),
            pltpu.VMEM((4, 2, 3, 3, 8, 128), jnp.float32),
            pltpu.VMEM((SWEEPS, 4, 2 * LINK, 8, 128), jnp.float32),
            pltpu.SemaphoreType.DMA((COPIES,)),
            pltpu.SemaphoreType.DMA((COPIES,)),
        ],
        compiler_params=pltpu.CompilerParams(
            collective_id=0, has_side_effects=True, vmem_limit_bytes=VMEM_LIMIT
        ),
    )(links, kicks, separations)
    last_links(windows, gauge_links, langevin_noise)
    return jnp.swapaxes(correlator, 0, 1) * (1.0 / SWEEPS**4)


def solution(mesh):
    return jax.shard_map(
        local,
        mesh=mesh,
        in_specs=(
            P(None, None, None, None, "slab", "sx", "syz"),
            P(None, None, None, "slab", "sx", "syz"),
            P(),
        ),
        out_specs=P("slab", "sx", "syz"),
        check_vma=False,
    )
```
